32 devices in a mesh: dp: 8 (over y, x, core), seq: 4 (over z).
Axes of the slice: x: 2, y: 2, z: 4, core: 2. Of those that a mesh axis runs over, the one named last changes fastest.
Arguments:
- inputs: bfloat16 [32768, 1024], P(('dp', 'seq')), may hold values from -6 to 6
- timestep: bfloat16 [8, 1024], P('dp'), may hold values from -6 to 6
- context_len: int32 [8, 8], P('dp'), may hold values from 0 to 475, as said below
- out_grad: bfloat16 [32768, 1024], P(('dp', 'seq')), may hold values from -6 to 6
- qkv_weight: bfloat16 [1024, 3072], P(('dp', 'seq')), may hold values from -0.1875 to 0.1875
- out_weight: bfloat16 [1024, 1024], P(('dp', 'seq')), may hold values from -0.75 to 0.75
- in_weight: bfloat16 [1024, 4096], P(('dp', 'seq')), may hold values from -0.1875 to 0.1875
- back_weight: bfloat16 [4096, 1024], P(('dp', 'seq')), may hold values from -0.09375 to 0.09375
- vectors: bfloat16 [1024, 8], P(('dp', 'seq')), may hold values from -1.25 to 1.4
- bias_ff: bfloat16 [4096], P(('dp', 'seq')), may hold values from -3 to 3
Outputs:
- result: float32 [32768, 1024], P(('dp', 'seq'))
- grad_input: float32 [32768, 1024], P(('dp', 'seq'))
- grad_qkv: float32 [1024, 3072], P(('dp', 'seq'))
- grad_out: float32 [1024, 1024], P(('dp', 'seq'))
- grad_in: float32 [1024, 4096], P(('dp', 'seq'))
- grad_back: float32 [4096, 1024], P(('dp', 'seq'))
- grad_vectors: float32 [1024, 8], P(('dp', 'seq'))
- grad_bias_ff: float32 [4096], P(('dp', 'seq'))
The draws below stay inside these ranges and needn't reach their ends.
Inputs may be any that keep to these rules, and one draw needn't show every extreme that they name: `context_len`: some slot has exactly 475 context tokens.
All inputs are finite; a program needn't handle non-finite values.
Results may differ from the reference program's by a relative error of at most 0.012.
The reference program's roundings to bfloat16 on the way count: a program that leaves them out, or rounds other values in their place, can miss the bound.
Values may be sent and summed in bfloat16 or wider, within the bound.
A program may use at most 256 MiB of HBM per device.

```python
import jax
import jax.numpy as jnp
from jax import lax

D = 1024
HEADS = 16
FF = 4096
HEAD_DIM = 64
SLOT = 512
BLOCK = 25
CTX_MAX = 475
ROW_SLOTS = 8
ROW_TOK = 4096
ROWS = 8
TOKENS = 32768


def draw_context_len(key, part):
    key = jax.random.fold_in(key, 11)
    key_len, key_pick = jax.random.split(key)
    lengths = jax.random.randint(key_len, (ROWS, ROW_SLOTS), 0, CTX_MAX + 1)
    chosen = jax.random.randint(key_pick, (), 0, ROWS * ROW_SLOTS)
    flat_index = jnp.arange(ROWS * ROW_SLOTS, dtype=jnp.int32).reshape(ROWS, ROW_SLOTS)
    return jnp.where(flat_index == chosen, CTX_MAX, lengths).astype(jnp.int32)


def draw_vectors(key, part):
    key = jax.random.fold_in(key, 23)
    key_bias, key_gain = jax.random.split(key)
    biases = jnp.clip(0.4 * jax.random.normal(key_bias, (D, 8), jnp.float32), -1.2, 1.2)
    gain_draw = jax.random.uniform(key_gain, (D, 8), jnp.float32, 0.6, 1.4)
    column = jnp.arange(8, dtype=jnp.int32)[None, :]
    is_gain = (column == 4) | (column == 6)
    return jnp.where(is_gain, gain_draw, biases).astype(jnp.bfloat16)


def raised(array, stream_key, source, target, blocks, factor):
    owner, partner = [(jnp.arange(array.shape[axis_at]) // (array.shape[axis_at] // blocks)).reshape([-1 if axis == axis_at else 1 for axis in range(array.ndim)]) for axis_at in (source, target)]
    chosen = jax.random.permutation(stream_key, blocks)[partner]
    strong = (owner == chosen) | (owner == (partner + blocks // 2) % blocks)
    return jnp.where(strong, factor * array, array)


def steps_of(own_key, extent, cuts, least, high):
    loudness = 1.0
    for position, shards_of in cuts:
        draws = jax.random.uniform(jax.random.fold_in(jax.random.fold_in(own_key, 6), position), (shards_of,), jnp.float32, least / len(cuts), high / len(cuts))
        loudness = loudness * jnp.repeat(jnp.exp(draws), extent[position] // shards_of).reshape((-1,) + (1,) * (len(extent) - 1 - position))
    return loudness


def centred(stream_key, shape, spread, bound, shards=(), kind=jnp.bfloat16):
    gain = steps_of(stream_key, shape, shards, -0.22, 0.18) if shards else 1.0
    array = jax.random.normal(stream_key, shape, jnp.float32) * spread * gain
    return jnp.minimum(jnp.maximum(array, -bound), bound).astype(kind)


def gaussian_with(stream_key, dims, deviation, limit, shards, heavy, kind=jnp.bfloat16):
    result = deviation * jax.random.normal(stream_key, dims, jnp.float32)
    if shards:
        result = result * steps_of(stream_key, dims, shards, -0.22, 0.18)
    return jnp.clip(raised(result, jax.random.fold_in(stream_key, 3), *heavy), -limit, limit).astype(kind)


def setup_inputs(seed: int = 0) -> dict:
    seeds = jax.random.split(jax.random.key(seed), 11)
    return {
        "inputs": centred(seeds[0], (TOKENS, D), 1.0, 6.0, ((0, 32),)),
        "timestep": centred(seeds[1], (ROWS, D), 1.0, 6.0, ((0, 8),)),
        "context_len": draw_context_len(jax.random.fold_in(seeds[10], 71), 0),
        "out_grad": gaussian_with(seeds[3], (TOKENS, D), 1.0, 6.0, ((0, 32),), (0, 1, 32, 2.75)),
        "qkv_weight": centred(seeds[4], (D, 3 * D), D ** -0.5, 0.1875, ((0, 32),)),
        "out_weight": centred(seeds[5], (D, D), (D // 16) ** -0.5, 0.75, ((0, 32),)),
        "in_weight": centred(seeds[6], (D, FF), D ** -0.5, 0.1875, ((0, 32),)),
        "back_weight": centred(seeds[7], (FF, D), FF ** -0.5, 0.09375, ((0, 32),)),
        "vectors": draw_vectors(jax.random.fold_in(seeds[10], 71), 0),
        "bias_ff": centred(seeds[9], (FF,), 0.5, 3.0, ((0, 32),)),
    }


@jax.custom_vjp
def low(v):
    return lax.optimization_barrier(v.astype(jnp.bfloat16)).astype(jnp.float32)

@jax.custom_vjp
def low_back(v):
    return v

def low_keep(v):
    return (low(v), None)

def low_pass(kept, grad):
    return (grad,)

def back_keep(v):
    return (v, None)

def back_low(kept, grad):
    return (low(grad),)
low.defvjp(low_keep, low_pass)
low_back.defvjp(back_keep, back_low)
norm_eps = 1e-05
highest = lax.Precision.HIGHEST

def norm_layer(resid, gain_vec, shift_vec):
    row_mean = lax.optimization_barrier(jnp.mean(resid, axis=-1, keepdims=True))
    centered = resid - row_mean
    variance = lax.optimization_barrier(jnp.mean(centered * centered, axis=-1, keepdims=True))
    return centered * lax.rsqrt(variance + norm_eps) * gain_vec + shift_vec

def slot_attention(queries, key_vecs, values, live_len):
    inv_root = 1.0 / jnp.sqrt(jnp.float32(HEAD_DIM))
    raw_scores = jnp.einsum('qhd,khd->hqk', queries, key_vecs, precision=highest) * inv_root
    scores = low_back(raw_scores)
    key_valid = jnp.arange(SLOT, dtype=jnp.int32) < live_len
    masked = jnp.where(key_valid[None, None, :], scores, -1e+30)
    row_max = lax.optimization_barrier(jnp.max(masked, axis=-1, keepdims=True))
    exp_scores = jnp.exp(masked - row_max)
    attn_probs = low(exp_scores / lax.optimization_barrier(jnp.sum(exp_scores, axis=-1, keepdims=True)))
    return jnp.einsum('hqk,khd->qhd', attn_probs, values, precision=highest)

def row_forward(x_row, emb_row, live_row, params):
    qkv_full, out_full, in_full, back_full, vec_all, bias_all = params
    resid_in = x_row + emb_row[None, :]
    layer_in = low(resid_in)
    qkv_proj = jnp.dot(layer_in, qkv_full, precision=highest)
    queries = low_back(low(qkv_proj[:, :D] + vec_all[:, 0]))
    key_vecs = low_back(low(qkv_proj[:, D:2 * D]))
    values = low_back(low(qkv_proj[:, 2 * D:] + vec_all[:, 1]))
    slot_shape = (ROW_SLOTS, SLOT, HEADS, HEAD_DIM)
    checked = jax.checkpoint(slot_attention)
    context = lax.map(lambda parts: checked(parts[0], parts[1], parts[2], parts[3]), (queries.reshape(slot_shape), key_vecs.reshape(slot_shape), values.reshape(slot_shape), live_row))
    context = low_back(low(context.reshape(ROW_TOK, D)))
    attn_out = low_back(jnp.dot(context, out_full, precision=highest)) + vec_all[:, 2]
    normed_mid = norm_layer(resid_in + attn_out, vec_all[:, 4], vec_all[:, 5])
    pre_act = low_back(jnp.dot(low(normed_mid), in_full, precision=highest)) + bias_all
    hidden = low(jax.nn.gelu(pre_act, approximate=False))
    branch = low_back(jnp.dot(hidden, back_full, precision=highest)) + vec_all[:, 3]
    return norm_layer(normed_mid + branch, vec_all[:, 6], vec_all[:, 7])

def reference(inputs, timestep, context_len, out_grad, qkv_weight, out_weight, in_weight, back_weight, vectors, bias_ff):
    params = (qkv_weight.astype(jnp.float32), out_weight.astype(jnp.float32), in_weight.astype(jnp.float32), back_weight.astype(jnp.float32), vectors.astype(jnp.float32), bias_ff.astype(jnp.float32))
    rows_x = inputs.astype(jnp.float32).reshape(ROWS, ROW_TOK, D)
    embeds = timestep.astype(jnp.float32)
    live_all = (context_len + BLOCK).astype(jnp.int32)
    cotangent = out_grad.astype(jnp.float32).reshape(ROWS, ROW_TOK, D)

    def row_step(totals, row_data):
        x_row, emb_row, live_row, cot_row = row_data

        def forward(x_value, param_value):
            return row_forward(x_value, emb_row, live_row, param_value)
        out_row, pullback = jax.vjp(forward, x_row, params)
        in_grad, param_grads = pullback(cot_row)
        totals = jax.tree.map(lambda a, b: a + b, totals, param_grads)
        return (totals, (out_row, in_grad))
    zero_grads = jax.tree.map(jnp.zeros_like, params)
    totals, (out_rows, grad_rows) = lax.scan(row_step, zero_grads, (rows_x, embeds, live_all, cotangent))
    return (out_rows.reshape(TOKENS, D), grad_rows.reshape(TOKENS, D), totals[0], totals[1], totals[2], totals[3], totals[4], totals[5])
```

```python
import functools
import math

import jax
import jax.numpy as jnp
from jax import lax
from jax.experimental import pallas as pl
from jax.experimental.pallas import tpu as pltpu
from jax.sharding import PartitionSpec as P

HEAD_DIM = 64
SLOT = 512
BLOCK = 25


norm_eps = 1e-05


def norm_forward(resid, gain_vec, shift_vec):
    row_mean = jnp.mean(resid, axis=-1, keepdims=True)
    centered = resid - row_mean
    variance = jnp.mean(centered * centered, axis=-1, keepdims=True)
    inv_std = lax.rsqrt(variance + norm_eps)
    normed = centered * inv_std
    return (normed * gain_vec + shift_vec, normed, inv_std)


def norm_backward(grad_out, normed, inv_std, gain_vec):
    grad_norm = grad_out * gain_vec
    grad_resid = inv_std * (
        grad_norm
        - jnp.mean(grad_norm, axis=-1, keepdims=True)
        - normed * jnp.mean(grad_norm * normed, axis=-1, keepdims=True)
    )
    return (grad_resid, jnp.sum(grad_out * normed, axis=0), jnp.sum(grad_out, axis=0))


def gelu_slope(pre_act):
    return 0.5 * (1.0 + lax.erf(pre_act * math.sqrt(0.5))) + pre_act * jnp.exp(
        -0.5 * pre_act * pre_act
    ) / math.sqrt(2.0 * math.pi)


def slot_scores(queries, key_vecs, live_len):
    inv_root = 1.0 / math.sqrt(HEAD_DIM)
    raw_scores = (
        jnp.einsum("qhd,khd->hqk", queries, key_vecs, preferred_element_type=jnp.float32) * inv_root
    )
    key_valid = jnp.arange(SLOT, dtype=jnp.int32) < live_len
    return jnp.where(key_valid[None, None, :], raw_scores, -1e30)


def slot_forward(parts):
    queries, key_vecs, values, live_len = parts
    masked = slot_scores(queries, key_vecs, live_len)
    row_max = jnp.max(masked, axis=-1, keepdims=True)
    exp_scores = jnp.exp(masked - row_max)
    exp_total = jnp.sum(exp_scores, axis=-1, keepdims=True)
    attn_probs = (exp_scores / exp_total).astype(jnp.bfloat16)
    context = jnp.einsum("hqk,khd->qhd", attn_probs, values, preferred_element_type=jnp.float32)
    return (context.astype(jnp.bfloat16), (row_max + jnp.log(exp_total))[..., 0])


def slot_backward(parts):
    queries, key_vecs, values, live_len, log_total, grad_ctx = parts
    inv_root = 1.0 / math.sqrt(HEAD_DIM)
    masked = slot_scores(queries, key_vecs, live_len)
    attn_exact = jnp.exp(masked - log_total[..., None])
    attn_probs = attn_exact.astype(jnp.bfloat16)
    grad_probs = jnp.einsum("qhd,khd->hqk", grad_ctx, values, preferred_element_type=jnp.float32)
    row_dot = jnp.sum(attn_exact * grad_probs, axis=-1, keepdims=True)
    grad_scores = (attn_exact * (grad_probs - row_dot)).astype(jnp.bfloat16)
    grad_query = (
        jnp.einsum("hqk,khd->qhd", grad_scores, key_vecs, preferred_element_type=jnp.float32)
        * inv_root
    )
    grad_key = (
        jnp.einsum("hqk,qhd->khd", grad_scores, queries, preferred_element_type=jnp.float32)
        * inv_root
    )
    grad_value = jnp.einsum(
        "hqk,qhd->khd", attn_probs, grad_ctx, preferred_element_type=jnp.float32
    )
    return (
        grad_query.astype(jnp.bfloat16),
        grad_key.astype(jnp.bfloat16),
        grad_value.astype(jnp.bfloat16),
    )


MESH = pl.DeviceIdType.MESH
LANES = 128
F32 = jnp.float32
BF16 = jnp.bfloat16


class Grid:
    def __init__(self, mesh):
        dp, self.nz = mesh.shape["dp"], mesh.shape["seq"]
        self.nc = 2 if dp % 2 == 0 else 1
        rest = dp // self.nc
        self.nx = max(k for k in range(1, math.isqrt(rest) + 1) if rest % k == 0)
        self.ny = rest // self.nx
        self.count = dp * self.nz

    def here(self):
        dp = lax.axis_index("dp")
        self.z = lax.axis_index("seq")
        self.c = dp % self.nc
        self.x = (dp // self.nc) % self.nx
        self.y = dp // (self.nc * self.nx)

    def device(self, y, x, c, z):
        return ((y * self.nx + x) * self.nc + c, z)

    def off(self, axis, step):
        return (getattr(self, axis) + step) % getattr(self, "n" + axis)

    def peer(self, axis, step):
        at = {name: getattr(self, name) for name in "yxcz"}
        at[axis] = self.off(axis, step)
        return self.device(**at)

    def peers(self):
        return [self.peer(axis, step) for axis in "zxyc" for step in range(1, getattr(self, "n" + axis))]


def greet(grid):
    barrier = pltpu.get_barrier_semaphore()
    peers = grid.peers()
    for peer in peers:
        pl.semaphore_signal(barrier, inc=1, device_id=peer, device_id_type=MESH)
    pl.semaphore_wait(barrier, len(peers))


class Sems:
    def __init__(self, send, recv):
        self.send, self.recv, self.used = send, recv, 0

    def remote(self, src, dst, device):
        k = self.used
        self.used += 1
        return pltpu.make_async_remote_copy(
            src_ref=src,
            dst_ref=dst,
            send_sem=self.send.at[k],
            recv_sem=self.recv.at[k],
            device_id=device,
            device_id_type=MESH,
        )


def block_rows(start, size):
    return pl.ds(pl.multiple_of(start * size, size), size)


class Gather:
    def __init__(self, grid, sems, local_sem, shard, full, cols):
        self.grid, self.sems, self.local_sem = grid, sems, local_sem
        self.shard, self.full, self.cols = shard, full, cols
        self.rows = shard.shape[0]
        self.half = self.rows * grid.nz // 2
        self.sent = []

    def go(self, copies):
        for copy in copies:
            copy.start()
        self.sent += copies
        self.flying = copies

    def landed(self):
        for copy in self.flying:
            copy.wait_recv()

    def start(self):
        g = self.grid
        own = self.full.at[g.y, g.x, g.c, block_rows(g.z, self.rows), self.cols]
        src = self.shard.at[:, self.cols]
        self.own = pltpu.make_async_copy(src, own, self.local_sem)
        self.own.start()
        self.go([self.sems.remote(src, own, g.peer("z", k)) for k in range(1, g.nz)])

    def second(self):
        g = self.grid
        self.landed()
        self.own.wait()
        a = self.full.at[g.y, g.x, g.c, pl.ds(0, self.half), self.cols]
        b = self.full.at[g.y, g.x, g.c, pl.ds(self.half, self.half), self.cols]
        self.go(
            [self.sems.remote(a, a, g.peer("x", k)) for k in range(1, g.nx)]
            + [self.sems.remote(b, b, g.peer("y", k)) for k in range(1, g.ny)]
        )

    def third(self):
        g = self.grid
        self.landed()
        a = self.full.at[g.y, :, g.c, pl.ds(0, self.half), self.cols]
        b = self.full.at[:, g.x, g.c, pl.ds(self.half, self.half), self.cols]
        self.go(
            [self.sems.remote(a, a, g.peer("y", k)) for k in range(1, g.ny)]
            + [self.sems.remote(b, b, g.peer("x", k)) for k in range(1, g.nx)]
        )

    def fourth(self):
        g = self.grid
        self.landed()
        a = self.full.at[:, :, g.c, :, self.cols]
        self.go([self.sems.remote(a, a, g.peer("c", k)) for k in range(1, g.nc)])

    def finish(self):
        self.landed()

    def drain(self):
        for copy in self.sent:
            copy.wait_send()


def gather_sems(grid):
    return grid.nz - 1 + 2 * (grid.nx - 1) + 2 * (grid.ny - 1) + grid.nc - 1


def pipeline(jobs, stages):
    for tick in range(len(jobs) + len(stages) - 1):
        for s in reversed(range(len(stages))):
            if 0 <= tick - s < len(jobs):
                getattr(jobs[tick - s], stages[s])()


def gather_kernel(grid, blocks, *refs):
    n = len(blocks)
    shards, fulls, (send, recv, local) = refs[:n], refs[n : 2 * n], refs[2 * n :]
    grid.here()
    greet(grid)
    sems = Sems(send, recv)
    jobs = []
    for shard, full, width in zip(shards, fulls, blocks):
        for at in range(0, shard.shape[1], width):
            jobs.append(Gather(grid, sems, local.at[len(jobs)], shard, full, pl.ds(at, width)))
    pipeline(jobs, ["start", "second", "third", "fourth", "finish"])
    for job in jobs:
        job.drain()


def gather_all(grid, shards, widths):
    count = sum(s.shape[1] // w for s, w in zip(shards, widths))
    any_spec = pl.BlockSpec(memory_space=pl.ANY)
    return pl.pallas_call(
        functools.partial(gather_kernel, grid, widths),
        out_shape=[
            jax.ShapeDtypeStruct((grid.ny, grid.nx, grid.nc, grid.nz * s.shape[0], s.shape[1]), s.dtype)
            for s in shards
        ],
        in_specs=[any_spec] * len(shards),
        out_specs=[any_spec] * len(shards),
        scratch_shapes=[
            pltpu.SemaphoreType.DMA((count * gather_sems(grid),)),
            pltpu.SemaphoreType.DMA((count * gather_sems(grid),)),
            pltpu.SemaphoreType.DMA((count,)),
        ],
        compiler_params=pltpu.CompilerParams(collective_id=1, has_side_effects=True),
        name="gather_weights",
    )(*shards)


def add_into(dst, srcs, rows, step=32):
    @pl.loop(0, rows // step)
    def _(i):
        at = block_rows(i, step)
        total = dst[at, :].astype(F32)
        for src in srcs:
            total += src[at, :].astype(F32)
        dst[at, :] = total.astype(dst.dtype)


class Reduce:
    def __init__(self, grid, sems, bufs):
        self.grid, self.sems = grid, sems
        self.sum, self.in2a, self.in2b, self.in3a, self.in3b, self.in4 = bufs
        self.half = self.sum.shape[2] // 2
        self.rows = self.sum.shape[2] // grid.nz
        self.sent = []

    go, landed, drain = Gather.go, Gather.landed, Gather.drain

    def start(self, other):
        g = self.grid
        self.go([self.sems.remote(other, self.sum, g.peer("c", 1))])

    def second(self, own):
        g = self.grid
        self.landed()
        for y in range(g.ny):
            for x in range(g.nx):
                add_into(self.sum.at[y, x], [own.at[y, x]], 2 * self.half)
        lo, hi = pl.ds(0, self.half), pl.ds(self.half, self.half)
        self.go(
            [
                self.sems.remote(self.sum.at[g.off("y", k), :, lo], self.in2a.at[k - 1], g.peer("y", k))
                for k in range(1, g.ny)
            ]
            + [
                self.sems.remote(self.sum.at[:, g.off("x", k), hi], self.in2b.at[k - 1], g.peer("x", k))
                for k in range(1, g.nx)
            ]
        )

    def third(self):
        g = self.grid
        self.landed()
        lo, hi = pl.ds(0, self.half), pl.ds(self.half, self.half)
        for x in range(g.nx):
            add_into(self.sum.at[g.y, x, lo], [self.in2a.at[k, x] for k in range(g.ny - 1)], self.half)
        for y in range(g.ny):
            add_into(self.sum.at[y, g.x, hi], [self.in2b.at[k, y] for k in range(g.nx - 1)], self.half)
        self.go(
            [
                self.sems.remote(self.sum.at[g.y, g.off("x", k), lo], self.in3a.at[k - 1], g.peer("x", k))
                for k in range(1, g.nx)
            ]
            + [
                self.sems.remote(self.sum.at[g.off("y", k), g.x, hi], self.in3b.at[k - 1], g.peer("y", k))
                for k in range(1, g.ny)
            ]
        )

    def fourth(self):
        g = self.grid
        self.landed()
        lo, hi = pl.ds(0, self.half), pl.ds(self.half, self.half)
        add_into(self.sum.at[g.y, g.x, lo], [self.in3a.at[k] for k in range(g.nx - 1)], self.half)
        add_into(self.sum.at[g.y, g.x, hi], [self.in3b.at[k] for k in range(g.ny - 1)], self.half)
        self.go(
            [
                self.sems.remote(
                    self.sum.at[g.y, g.x, block_rows(g.off("z", k), self.rows)], self.in4.at[k - 1], g.peer("z", k)
                )
                for k in range(1, g.nz)
            ]
        )

    def finish(self, out, cols):
        g = self.grid
        self.landed()
        total = self.sum[g.y, g.x, block_rows(g.z, self.rows), :].astype(F32)
        for k in range(g.nz - 1):
            total += self.in4[k].astype(F32)
        out[:, cols] = total


def reduce_bufs(grid, rows, width, count):
    group, half = rows * grid.nz, rows * grid.nz // 2
    ny, nx = grid.ny, grid.nx
    return [
        pltpu.VMEM((count, *shape, width), BF16)
        for shape in (
            (ny, nx, group),
            (ny - 1, nx, half),
            (nx - 1, ny, half),
            (nx - 1, half),
            (ny - 1, half),
            (grid.nz - 1, rows),
        )
    ]


def reduce_sems(grid):
    return grid.nz - 1 + 2 * (grid.nx - 1) + 2 * (grid.ny - 1) + grid.nc - 1


class Feed:
    def __init__(self, job, grid, part, cols, own, own_sem, out):
        self.job, self.grid, self.part, self.cols, self.own, self.own_sem, self.out = job, grid, part, cols, own, own_sem, out

    def start(self):
        g = self.grid
        self.copy = pltpu.make_async_copy(self.part.at[:, :, g.c, :, self.cols], self.own, self.own_sem)
        self.copy.start()
        self.job.start(self.part.at[:, :, g.off("c", 1), :, self.cols])

    def second(self):
        self.copy.wait()
        self.job.second(self.own)

    def third(self):
        self.job.third()

    def fourth(self):
        self.job.fourth()

    def finish(self):
        self.job.finish(self.out, self.cols)


def reduce_kernel(grid, widths, *refs):
    n = len(widths)
    parts, outs, scratch = refs[:n], refs[n : 2 * n], refs[2 * n :]
    send, recv, local = scratch[:3]
    bufs = scratch[3:]
    grid.here()
    greet(grid)
    sems = Sems(send, recv)
    jobs = []
    for i, (part, out, width) in enumerate(zip(parts, outs, widths)):
        own, *mine = bufs[7 * i : 7 * i + 7]
        for k in range(part.shape[4] // width):
            job = Reduce(grid, sems, [b.at[k] for b in mine])
            jobs.append(Feed(job, grid, part, pl.ds(k * width, width), own.at[k % 2], local.at[len(jobs)], out))
    pipeline(jobs, ["start", "second", "third", "fourth", "finish"])
    for feed in jobs:
        feed.job.drain()


def reduce_all(grid, parts, widths):
    counts = [p.shape[4] // w for p, w in zip(parts, widths)]
    rows = [p.shape[3] // grid.nz for p in parts]
    scratch = []
    for r, w, k in zip(rows, widths, counts):
        scratch.append(pltpu.VMEM((2, grid.ny, grid.nx, r * grid.nz, w), BF16))
        scratch += reduce_bufs(grid, r, w, k)
    total = sum(counts)
    return pl.pallas_call(
        functools.partial(reduce_kernel, grid, widths),
        out_shape=[jax.ShapeDtypeStruct((r, p.shape[4]), F32) for r, p in zip(rows, parts)],
        in_specs=[pl.BlockSpec(memory_space=pl.ANY)] * len(parts),
        out_specs=[pl.BlockSpec(memory_space=pltpu.VMEM)] * len(parts),
        scratch_shapes=[
            pltpu.SemaphoreType.DMA((total * reduce_sems(grid),)),
            pltpu.SemaphoreType.DMA((total * reduce_sems(grid),)),
            pltpu.SemaphoreType.DMA((total,)),
            *scratch,
        ],
        compiler_params=pltpu.CompilerParams(collective_id=2, has_side_effects=True, vmem_limit_bytes=60 << 20),
        name="reduce_gradients",
    )(*parts)


def gathered_by_xla(grid, shards):
    return [lax.all_gather(s, ("dp", "seq"), axis=0, tiled=True) for s in shards]


def fits(grid, inputs, qkv_weight):
    return (
        inputs.shape[0] % SLOT == 0
        and qkv_weight.shape[0] % 32 == 0
        and grid.nc == 2
        and grid.nx > 1
        and grid.ny > 1
        and grid.nz > 1
    )


def shards(
    grid,
    inputs,
    timestep,
    context_len,
    out_grad,
    qkv_weight,
    out_weight,
    in_weight,
    back_weight,
    vectors,
    bias_ff,
):
    use_kernels = fits(grid, inputs, qkv_weight)
    rows = vectors.shape[0]
    width = inputs.shape[1]
    if use_kernels:
        small = jnp.concatenate([vectors.T.reshape(-1), bias_ff])
        small = jnp.pad(small, (0, 16 * LANES - small.size)).reshape(16, LANES)
        full = gather_all(
            grid, (small, qkv_weight, out_weight, in_weight, back_weight), (LANES, width, width, width, width // 4)
        )
        small_full, qkv_full, out_full, in_full, back_full = [f.reshape(-1, f.shape[-1]) for f in full]
        small_full = small_full.reshape(grid.count, 16 * LANES)
        vec_full = small_full[:, : 8 * rows].reshape(grid.count, 8, rows).transpose(0, 2, 1).reshape(width, 8)
        bias_full = small_full[:, 8 * rows : 8 * rows + bias_ff.size].reshape(-1)
    else:
        qkv_full, out_full, in_full, back_full, vec_full, bias_full = gathered_by_xla(
            grid, (qkv_weight, out_weight, in_weight, back_weight, vectors, bias_ff)
        )
    vec_all = vec_full.astype(jnp.float32)
    bias_all = bias_full.astype(jnp.float32)
    resid_in = inputs.astype(jnp.float32) + timestep.astype(jnp.float32)
    layer_in = resid_in.astype(jnp.bfloat16)
    qkv_proj = jnp.dot(layer_in, qkv_full, preferred_element_type=jnp.float32)
    queries = (qkv_proj[:, :width] + vec_all[:, 0]).astype(jnp.bfloat16)
    key_vecs = qkv_proj[:, width : 2 * width].astype(jnp.bfloat16)
    values = (qkv_proj[:, 2 * width :] + vec_all[:, 1]).astype(jnp.bfloat16)
    slot_count = inputs.shape[0] // SLOT
    slot_shape = (slot_count, SLOT, width // HEAD_DIM, HEAD_DIM)
    first = lax.axis_index("seq") * slot_count
    live_lens = lax.dynamic_slice(context_len[0], (first,), (slot_count,)) + BLOCK
    q_slots = queries.reshape(slot_shape)
    k_slots = key_vecs.reshape(slot_shape)
    v_slots = values.reshape(slot_shape)
    ctx_slots, log_totals = lax.map(slot_forward, (q_slots, k_slots, v_slots, live_lens))
    ctx_tokens = ctx_slots.reshape(slot_count * SLOT, width)
    attn_out = jnp.dot(ctx_tokens, out_full, preferred_element_type=jnp.float32) + vec_all[:, 2]
    normed_mid, unit_mid, inv_mid = norm_forward(resid_in + attn_out, vec_all[:, 4], vec_all[:, 5])
    mid_low = normed_mid.astype(jnp.bfloat16)
    pre_act = jnp.dot(mid_low, in_full, preferred_element_type=jnp.float32) + bias_all
    hidden = jax.nn.gelu(pre_act, approximate=False).astype(jnp.bfloat16)
    branch = jnp.dot(hidden, back_full, preferred_element_type=jnp.float32) + vec_all[:, 3]
    result, unit_out, inv_out = norm_forward(normed_mid + branch, vec_all[:, 6], vec_all[:, 7])
    grad_two, gain_out_grad, shift_out_grad = norm_backward(
        out_grad.astype(jnp.float32), unit_out, inv_out, vec_all[:, 6]
    )
    branch_low = grad_two.astype(jnp.bfloat16)
    grad_backw = jnp.einsum("tf,td->fd", hidden, branch_low, preferred_element_type=jnp.float32)
    grad_hidden = jnp.einsum("td,fd->tf", branch_low, back_full, preferred_element_type=jnp.float32)
    grad_pre = grad_hidden * gelu_slope(pre_act)
    bias_grad = jnp.sum(grad_pre, axis=0)
    pre_low = grad_pre.astype(jnp.bfloat16)
    grad_inw = jnp.einsum("td,tf->df", mid_low, pre_low, preferred_element_type=jnp.float32)
    grad_mid = grad_two + jnp.einsum(
        "tf,df->td", pre_low, in_full, preferred_element_type=jnp.float32
    )
    grad_one, gain_mid_grad, shift_mid_grad = norm_backward(
        grad_mid, unit_mid, inv_mid, vec_all[:, 4]
    )
    attn_low = grad_one.astype(jnp.bfloat16)
    grad_outw = jnp.einsum("td,te->de", ctx_tokens, attn_low, preferred_element_type=jnp.float32)
    grad_ctx = jnp.einsum(
        "te,de->td", attn_low, out_full, preferred_element_type=jnp.float32
    ).astype(jnp.bfloat16)
    grad_q, grad_k, grad_v = lax.map(
        slot_backward,
        (q_slots, k_slots, v_slots, live_lens, log_totals, grad_ctx.reshape(slot_shape)),
    )
    grad_proj = jnp.concatenate([g.reshape(slot_count * SLOT, width) for g in (grad_q, grad_k, grad_v)], axis=1)
    grad_qkvw = jnp.einsum("td,te->de", layer_in, grad_proj, preferred_element_type=jnp.float32)
    grad_input = grad_one + jnp.einsum(
        "te,de->td", grad_proj, qkv_full, preferred_element_type=jnp.float32
    )
    bias_rows = jnp.sum(grad_proj.astype(jnp.float32), axis=0)
    vec_rows = jnp.stack(
        [
            bias_rows[:width],
            bias_rows[2 * width :],
            jnp.sum(grad_one, axis=0),
            jnp.sum(grad_two, axis=0),
            gain_mid_grad,
            shift_mid_grad,
            gain_out_grad,
            shift_out_grad,
        ],
    )
    if use_kernels:
        by_owner = vec_rows.reshape(8, grid.count, rows).transpose(1, 0, 2).reshape(grid.count, 8 * rows)
        small = jnp.concatenate([by_owner, bias_grad.reshape(grid.count, -1)], axis=1)
        small = jnp.pad(small, ((0, 0), (0, 16 * LANES - small.shape[1]))).astype(jnp.bfloat16)
        parts = [g.astype(jnp.bfloat16) for g in (grad_backw, grad_inw, grad_outw, grad_qkvw)]
        parts.append(small.reshape(-1, LANES))
        parts = [p.reshape(grid.ny, grid.nx, grid.nc, -1, p.shape[1]) for p in parts]
        share_back, share_in, share_out, share_qkv, share_small = reduce_all(
            grid, parts, (width // 4, width, width, width, LANES)
        )
        share_small = share_small.reshape(-1)
        share_vec = share_small[: 8 * rows].reshape(8, rows).T
        share_bias = share_small[8 * rows : 8 * rows + bias_ff.size]
    else:
        share_qkv, share_out, share_in, share_back, share_vec, share_bias = [
            lax.psum_scatter(g, ("dp", "seq"), scatter_dimension=0, tiled=True)
            for g in (grad_qkvw, grad_outw, grad_inw, grad_backw, vec_rows.T, bias_grad)
        ]
    return (result, grad_input, share_qkv, share_out, share_in, share_back, share_vec, share_bias)


def solution(mesh):
    return jax.shard_map(
        functools.partial(shards, Grid(mesh)),
        mesh=mesh,
        in_specs=(
            P(("dp", "seq"), None),
            P("dp", None),
            P("dp", None),
            P(("dp", "seq"), None),
            P(("dp", "seq"), None),
            P(("dp", "seq"), None),
            P(("dp", "seq"), None),
            P(("dp", "seq"), None),
            P(("dp", "seq"), None),
            P(("dp", "seq")),
        ),
        out_specs=(
            P(("dp", "seq"), None),
            P(("dp", "seq"), None),
            P(("dp", "seq"), None),
            P(("dp", "seq"), None),
            P(("dp", "seq"), None),
            P(("dp", "seq"), None),
            P(("dp", "seq"), None),
            P(("dp", "seq")),
        ),
        check_vma=False,
    )
```

```python
import functools
import math

import jax
import jax.numpy as jnp
from jax import lax
from jax.experimental import pallas as pl
from jax.experimental.pallas import tpu as pltpu
from jax.sharding import PartitionSpec as P

HEAD_DIM = 64
SLOT = 512
BLOCK = 25


norm_eps = 1e-05


def norm_forward(resid, gain_vec, shift_vec):
    row_mean = jnp.mean(resid, axis=-1, keepdims=True)
    centered = resid - row_mean
    variance = jnp.mean(centered * centered, axis=-1, keepdims=True)
    inv_std = lax.rsqrt(variance + norm_eps)
    normed = centered * inv_std
    return (normed * gain_vec + shift_vec, normed, inv_std)


def norm_backward(grad_out, normed, inv_std, gain_vec):
    grad_norm = grad_out * gain_vec
    grad_resid = inv_std * (
        grad_norm
        - jnp.mean(grad_norm, axis=-1, keepdims=True)
        - normed * jnp.mean(grad_norm * normed, axis=-1, keepdims=True)
    )
    return (grad_resid, jnp.sum(grad_out * normed, axis=0), jnp.sum(grad_out, axis=0))


def gelu_slope(pre_act):
    return 0.5 * (1.0 + lax.erf(pre_act * math.sqrt(0.5))) + pre_act * jnp.exp(
        -0.5 * pre_act * pre_act
    ) / math.sqrt(2.0 * math.pi)


def slot_scores(queries, key_vecs, live_len):
    inv_root = 1.0 / math.sqrt(HEAD_DIM)
    raw_scores = (
        jnp.einsum("qhd,khd->hqk", queries, key_vecs, preferred_element_type=jnp.float32) * inv_root
    )
    key_valid = jnp.arange(SLOT, dtype=jnp.int32) < live_len
    return jnp.where(key_valid[None, None, :], raw_scores, -1e30)


def slot_forward(parts):
    queries, key_vecs, values, live_len = parts
    masked = slot_scores(queries, key_vecs, live_len)
    row_max = jnp.max(masked, axis=-1, keepdims=True)
    exp_scores = jnp.exp(masked - row_max)
    exp_total = jnp.sum(exp_scores, axis=-1, keepdims=True)
    attn_probs = (exp_scores / exp_total).astype(jnp.bfloat16)
    context = jnp.einsum("hqk,khd->qhd", attn_probs, values, preferred_element_type=jnp.float32)
    return (context.astype(jnp.bfloat16), (row_max + jnp.log(exp_total))[..., 0])


def slot_backward(parts):
    queries, key_vecs, values, live_len, log_total, grad_ctx = parts
    inv_root = 1.0 / math.sqrt(HEAD_DIM)
    masked = slot_scores(queries, key_vecs, live_len)
    attn_exact = jnp.exp(masked - log_total[..., None])
    attn_probs = attn_exact.astype(jnp.bfloat16)
    grad_probs = jnp.einsum("qhd,khd->hqk", grad_ctx, values, preferred_element_type=jnp.float32)
    row_dot = jnp.sum(attn_exact * grad_probs, axis=-1, keepdims=True)
    grad_scores = (attn_exact * (grad_probs - row_dot)).astype(jnp.bfloat16)
    grad_query = (
        jnp.einsum("hqk,khd->qhd", grad_scores, key_vecs, preferred_element_type=jnp.float32)
        * inv_root
    )
    grad_key = (
        jnp.einsum("hqk,qhd->khd", grad_scores, queries, preferred_element_type=jnp.float32)
        * inv_root
    )
    grad_value = jnp.einsum(
        "hqk,qhd->khd", attn_probs, grad_ctx, preferred_element_type=jnp.float32
    )
    return (
        grad_query.astype(jnp.bfloat16),
        grad_key.astype(jnp.bfloat16),
        grad_value.astype(jnp.bfloat16),
    )


def plain_shards(
    inputs,
    timestep,
    context_len,
    out_grad,
    qkv_weight,
    out_weight,
    in_weight,
    back_weight,
    vectors,
    bias_ff,
):
    qkv_full, out_full, in_full, back_full, vec_full, bias_full = (
        lax.all_gather(qkv_weight, ("dp", "seq"), axis=0, tiled=True),
        lax.all_gather(out_weight, ("dp", "seq"), axis=0, tiled=True),
        lax.all_gather(in_weight, ("dp", "seq"), axis=0, tiled=True),
        lax.all_gather(back_weight, ("dp", "seq"), axis=0, tiled=True),
        lax.all_gather(vectors, ("dp", "seq"), axis=0, tiled=True),
        lax.all_gather(bias_ff, ("dp", "seq"), axis=0, tiled=True),
    )
    vec_all = vec_full.astype(jnp.float32)
    bias_all = bias_full.astype(jnp.float32)
    width = inputs.shape[1]
    resid_in = inputs.astype(jnp.float32) + timestep.astype(jnp.float32)
    layer_in = resid_in.astype(jnp.bfloat16)
    qkv_proj = jnp.dot(layer_in, qkv_full, preferred_element_type=jnp.float32)
    queries = (qkv_proj[:, :width] + vec_all[:, 0]).astype(jnp.bfloat16)
    key_vecs = qkv_proj[:, width : 2 * width].astype(jnp.bfloat16)
    values = (qkv_proj[:, 2 * width :] + vec_all[:, 1]).astype(jnp.bfloat16)
    q_heads, k_heads, v_heads = (
        lax.all_to_all(queries, "seq", split_axis=1, concat_axis=0, tiled=True),
        lax.all_to_all(key_vecs, "seq", split_axis=1, concat_axis=0, tiled=True),
        lax.all_to_all(values, "seq", split_axis=1, concat_axis=0, tiled=True),
    )
    slot_count = context_len.shape[1]
    head_width = q_heads.shape[1]
    slot_shape = (slot_count, SLOT, head_width // HEAD_DIM, HEAD_DIM)
    live_lens = context_len[0] + BLOCK
    q_slots = q_heads.reshape(slot_shape)
    k_slots = k_heads.reshape(slot_shape)
    v_slots = v_heads.reshape(slot_shape)
    ctx_slots, log_totals = lax.map(slot_forward, (q_slots, k_slots, v_slots, live_lens))
    ctx_tokens = lax.all_to_all(
        ctx_slots.reshape(slot_count * SLOT, head_width),
        "seq",
        split_axis=0,
        concat_axis=1,
        tiled=True,
    )
    attn_out = jnp.dot(ctx_tokens, out_full, preferred_element_type=jnp.float32) + vec_all[:, 2]
    normed_mid, unit_mid, inv_mid = norm_forward(resid_in + attn_out, vec_all[:, 4], vec_all[:, 5])
    mid_low = normed_mid.astype(jnp.bfloat16)
    pre_act = jnp.dot(mid_low, in_full, preferred_element_type=jnp.float32) + bias_all
    hidden = jax.nn.gelu(pre_act, approximate=False).astype(jnp.bfloat16)
    branch = jnp.dot(hidden, back_full, preferred_element_type=jnp.float32) + vec_all[:, 3]
    result, unit_out, inv_out = norm_forward(normed_mid + branch, vec_all[:, 6], vec_all[:, 7])
    grad_two, gain_out_grad, shift_out_grad = norm_backward(
        out_grad.astype(jnp.float32), unit_out, inv_out, vec_all[:, 6]
    )
    branch_low = grad_two.astype(jnp.bfloat16)
    grad_backw = jnp.einsum("tf,td->fd", hidden, branch_low, preferred_element_type=jnp.float32)
    grad_hidden = jnp.einsum("td,fd->tf", branch_low, back_full, preferred_element_type=jnp.float32)
    grad_pre = grad_hidden * gelu_slope(pre_act)
    bias_grad = jnp.sum(grad_pre, axis=0)
    pre_low = grad_pre.astype(jnp.bfloat16)
    grad_inw = jnp.einsum("td,tf->df", mid_low, pre_low, preferred_element_type=jnp.float32)
    grad_mid = grad_two + jnp.einsum(
        "tf,df->td", pre_low, in_full, preferred_element_type=jnp.float32
    )
    grad_one, gain_mid_grad, shift_mid_grad = norm_backward(
        grad_mid, unit_mid, inv_mid, vec_all[:, 4]
    )
    attn_low = grad_one.astype(jnp.bfloat16)
    grad_outw = jnp.einsum("td,te->de", ctx_tokens, attn_low, preferred_element_type=jnp.float32)
    grad_ctx = jnp.einsum(
        "te,de->td", attn_low, out_full, preferred_element_type=jnp.float32
    ).astype(jnp.bfloat16)
    grad_ctx_heads = lax.all_to_all(grad_ctx, "seq", split_axis=1, concat_axis=0, tiled=True)
    grad_q, grad_k, grad_v = lax.map(
        slot_backward,
        (q_slots, k_slots, v_slots, live_lens, log_totals, grad_ctx_heads.reshape(slot_shape)),
    )
    token_shape = (slot_count * SLOT, head_width)
    grad_q_tok, grad_k_tok, grad_v_tok = (
        lax.all_to_all(grad_q.reshape(token_shape), "seq", split_axis=0, concat_axis=1, tiled=True),
        lax.all_to_all(grad_k.reshape(token_shape), "seq", split_axis=0, concat_axis=1, tiled=True),
        lax.all_to_all(grad_v.reshape(token_shape), "seq", split_axis=0, concat_axis=1, tiled=True),
    )
    grad_proj = jnp.concatenate([grad_q_tok, grad_k_tok, grad_v_tok], axis=1)
    grad_qkvw = jnp.einsum("td,te->de", layer_in, grad_proj, preferred_element_type=jnp.float32)
    grad_input = grad_one + jnp.einsum(
        "te,de->td", grad_proj, qkv_full, preferred_element_type=jnp.float32
    )
    vec_grads = jnp.stack(
        [
            jnp.sum(grad_q_tok.astype(jnp.float32), axis=0),
            jnp.sum(grad_v_tok.astype(jnp.float32), axis=0),
            jnp.sum(grad_one, axis=0),
            jnp.sum(grad_two, axis=0),
            gain_mid_grad,
            shift_mid_grad,
            gain_out_grad,
            shift_out_grad,
        ],
        axis=1,
    )
    share_qkv, share_out, share_in, share_back, share_vec, share_bias = (
        lax.psum_scatter(grad_qkvw, ("dp", "seq"), scatter_dimension=0, tiled=True),
        lax.psum_scatter(grad_outw, ("dp", "seq"), scatter_dimension=0, tiled=True),
        lax.psum_scatter(grad_inw, ("dp", "seq"), scatter_dimension=0, tiled=True),
        lax.psum_scatter(grad_backw, ("dp", "seq"), scatter_dimension=0, tiled=True),
        lax.psum_scatter(vec_grads, ("dp", "seq"), scatter_dimension=0, tiled=True),
        lax.psum_scatter(bias_grad, ("dp", "seq"), scatter_dimension=0, tiled=True),
    )
    return (result, grad_input, share_qkv, share_out, share_in, share_back, share_vec, share_bias)


MESH = pl.DeviceIdType.MESH
LANES = 128
F32 = jnp.float32
BF16 = jnp.bfloat16
NN = (((1,), (0,)), ((), ()))
NT = (((1,), (1,)), ((), ()))
TN = (((0,), (0,)), ((), ()))
ANY = pl.BlockSpec(memory_space=pl.ANY)
IN_VMEM = pl.BlockSpec(memory_space=pltpu.VMEM)
IN_SMEM = pl.BlockSpec(memory_space=pltpu.SMEM)
VMEM_BYTES = 62 << 20


def mm(a, b, dims):
    return lax.dot_general(a, b, dims, preferred_element_type=F32)


class Grid:
    def __init__(self, mesh):
        dp, self.nz = mesh.shape["dp"], mesh.shape["seq"]
        self.nc = 2 if dp % 2 == 0 else 1
        rest = dp // self.nc
        self.nx = max(k for k in range(1, math.isqrt(rest) + 1) if rest % k == 0)
        self.ny = rest // self.nx
        self.count = dp * self.nz
        self.groups = [(y, x, c) for y in range(self.ny) for x in range(self.nx) for c in range(self.nc)]

    def here(self):
        dp = lax.axis_index("dp")
        self.z = lax.axis_index("seq")
        self.c = dp % self.nc
        self.x = (dp // self.nc) % self.nx
        self.y = dp // (self.nc * self.nx)

    def off(self, axis, step):
        return (getattr(self, axis) + step) % getattr(self, "n" + axis)

    def peer(self, axis, step):
        at = {name: getattr(self, name) for name in "yxcz"}
        at[axis] = self.off(axis, step)
        return ((at["y"] * self.nx + at["x"]) * self.nc + at["c"], at["z"])

    def peers(self):
        return [self.peer(axis, step) for axis in "zxyc" for step in range(1, getattr(self, "n" + axis))]

    def copies(self):
        return self.nz - 1 + 2 * (self.nx - 1) + 2 * (self.ny - 1) + self.nc - 1


def greet(grid):
    barrier = pltpu.get_barrier_semaphore()
    peers = grid.peers()
    for peer in peers:
        pl.semaphore_signal(barrier, inc=1, device_id=peer, device_id_type=MESH)
    pl.semaphore_wait(barrier, len(peers))


class Sems:
    def __init__(self, send, recv):
        self.send, self.recv, self.used = send, recv, 0

    def remote(self, ends):
        k = self.used
        self.used += 1

        def copy():
            src, dst, device = ends()
            return pltpu.make_async_remote_copy(
                src_ref=src,
                dst_ref=dst,
                send_sem=self.send.at[k],
                recv_sem=self.recv.at[k],
                device_id=device,
                device_id_type=MESH,
            )

        return copy


class Locals:
    def __init__(self, sems):
        self.sems, self.used, self.open = sems, 0, []

    def start(self, ends):
        k = self.used
        self.used += 1

        def copy():
            src, dst = ends()
            return pltpu.make_async_copy(src, dst, self.sems.at[k])

        copy().start()
        self.open.append(copy)
        return copy

    def wait(self, copy):
        copy().wait()
        self.open.remove(copy)

    def drain(self):
        for copy in self.open:
            copy().wait()
        self.open = []


def block_rows(start, size):
    return pl.ds(pl.multiple_of(start * size, size), size)


class Travel:
    def go(self, copies):
        for copy in copies:
            copy().start()
        self.sent += copies
        self.flying = copies

    def landed(self):
        for copy in self.flying:
            copy().wait_recv()

    def drain(self):
        for copy in self.sent:
            copy().wait_send()
        self.sent = []


class Gather(Travel):
    def __init__(self, grid, sems, moves, shard, full, cols, keep=None):
        self.grid, self.sems, self.moves = grid, sems, moves
        self.shard, self.full, self.cols, self.keep = shard, full, cols, keep
        self.rows = shard.shape[0]
        self.half = self.rows * grid.nz // 2
        self.sent = []

    def start(self):
        g = self.grid
        src = lambda: self.shard.at[:, self.cols]
        own = lambda: self.full.at[g.y, g.x, g.c, block_rows(g.z, self.rows), self.cols]
        self.own = self.moves.start(lambda: (src(), own()))
        self.go([self.sems.remote(lambda k=k: (src(), own(), g.peer("z", k))) for k in range(1, g.nz)])

    def second(self):
        g = self.grid
        self.landed()
        self.moves.wait(self.own)
        a = lambda: self.full.at[g.y, g.x, g.c, pl.ds(0, self.half), self.cols]
        b = lambda: self.full.at[g.y, g.x, g.c, pl.ds(self.half, self.half), self.cols]
        self.go(
            [self.sems.remote(lambda k=k: (a(), a(), g.peer("x", k))) for k in range(1, g.nx)]
            + [self.sems.remote(lambda k=k: (b(), b(), g.peer("y", k))) for k in range(1, g.ny)]
        )

    def third(self):
        g = self.grid
        self.landed()
        a = lambda: self.full.at[g.y, :, g.c, pl.ds(0, self.half), self.cols]
        b = lambda: self.full.at[:, g.x, g.c, pl.ds(self.half, self.half), self.cols]
        self.go(
            [self.sems.remote(lambda k=k: (a(), a(), g.peer("y", k))) for k in range(1, g.ny)]
            + [self.sems.remote(lambda k=k: (b(), b(), g.peer("x", k))) for k in range(1, g.nx)]
        )

    def fourth(self):
        g = self.grid
        self.landed()
        a = lambda: self.full.at[:, :, g.c, :, self.cols]
        self.go([self.sems.remote(lambda k=k: (a(), a(), g.peer("c", k))) for k in range(1, g.nc)])

    def finish(self):
        self.landed()
        if self.keep is not None:
            every = lambda ref: ref.at[:, :, :, :, self.cols]
            self.moves.start(lambda: (every(self.full), every(self.keep)))


class Flow:
    STAGES = ("start", "second", "third", "fourth", "finish")

    def __init__(self, jobs, lags):
        steps = [
            (k + sum(lags[:s]), -s, k, name) for k in range(len(jobs)) for s, name in enumerate(self.STAGES)
        ]
        self.jobs, self.steps, self.done = jobs, sorted(steps), 0

    def tick(self):
        if self.done < len(self.steps):
            due = self.steps[self.done][0]
            while self.done < len(self.steps) and self.steps[self.done][0] == due:
                self.step()

    def step(self):
        _, _, k, name = self.steps[self.done]
        getattr(self.jobs[k], name)()
        self.done += 1

    def until(self, job):
        last = max(i for i, (_, _, k, name) in enumerate(self.steps) if name == "finish" and self.jobs[k] is job)
        while self.done <= last:
            self.step()

    def drain(self):
        while self.done < len(self.steps):
            self.step()
        for job in self.jobs:
            job.drain()


def head_lanes(h):
    return lax.broadcasted_iota(jnp.int32, (1, 2 * HEAD_DIM), 1) // HEAD_DIM == h


def only(lanes, block):
    return jnp.where(lanes, block, 0).astype(BF16)


def fold_small(grid, vectors, bias_ff):
    rows = vectors.shape[0]
    tiled = jnp.tile(vectors.T, (1, LANES // rows))
    mine = jnp.arange(LANES) // rows == lax.axis_index("seq")
    tiled = jnp.where(mine[None, :], tiled, 0).astype(BF16)
    return jnp.concatenate([tiled, bias_ff[None, :], jnp.zeros((7, LANES), BF16)], axis=0)


FWD_WIDTH = 512


def forward_kernel(
    grid,
    ctx_len,
    x_in,
    temb,
    small,
    wq_in,
    wo_in,
    wi_in,
    wb_in,
    wq_out,
    wo_out,
    wi_out,
    wb_out,
    vec_out,
    hin_out,
    qkv_out,
    lse_out,
    ctx_out,
    n1_out,
    inv_out,
    ub_out,
    hid_out,
    slope_out,
    r2_out,
    send,
    recv,
    move_sems,
    x,
    hin,
    qkv,
    ctx,
    n1,
    inv,
    ub,
    hid,
    slope,
    r2,
    lse,
    lse_rows,
    vec,
    bias_qkv,
    bias_ff,
    small_full,
    wq,
    wo,
    wi,
    wb,
):
    tokens, width = hin.shape
    hidden = hid.shape[1]
    slots = tokens // SLOT
    tile = FWD_WIDTH
    grid.here()
    moves = Locals(move_sems)
    x_copy = moves.start(lambda: (x_in, x))
    greet(grid)
    sems = Sems(send, recv)

    def gather(shard, full, at, wide, keep):
        return Gather(grid, sems, moves, shard, full, pl.ds(at, wide), keep)

    small_job = gather(small, small_full, 0, LANES, None)
    half = width // 2
    qkv_cols = [part * width + side * half for side in range(2) for part in range(3)]
    qkv_jobs = [gather(wq_in, wq, at, half, wq_out) for at in qkv_cols]
    out_jobs = [gather(wo_in, wo, at, half, wo_out) for at in range(0, width, half)]
    in_jobs = [gather(wi_in, wi, at, width, wi_out) for at in range(0, hidden, width)]
    back_wide = width * width // hidden
    back_jobs = [gather(wb_in, wb, at, back_wide, wb_out) for at in range(0, width, back_wide)]
    flow = Flow([small_job, *qkv_jobs, *out_jobs, *in_jobs, *back_jobs], FWD_LAGS)
    flow.tick()
    flow.tick()

    moves.wait(x_copy)

    @pl.loop(0, tokens // 128)
    def _(i):
        at = block_rows(i, 128)
        hin[at, :] = (x[at, :].astype(F32) + temb[...].astype(F32)).astype(BF16)

    moves.start(lambda: (hin, hin_out))
    flow.until(small_job)
    for i, (y, xx, c) in enumerate(grid.groups):
        tiles = [small_full[y, xx, c, pl.ds(16 * z, 16), :].astype(F32) for z in range(grid.nz)]
        vec[:, i * LANES : (i + 1) * LANES] = sum(t[:8] for t in tiles)
        for z, t in enumerate(tiles):
            at = (i * grid.nz + z) * LANES
            bias_ff[:, at : at + LANES] = t[8:9]
    moves.start(lambda: (vec, vec_out))
    bias_qkv[:, :width] = vec[0:1, :]
    bias_qkv[:, width : 2 * width] = jnp.zeros((1, width), F32)
    bias_qkv[:, 2 * width :] = vec[1:2, :]

    def project(at):
        @pl.loop(0, tokens // tile)
        def _(i):
            rows = block_rows(i, tile)
            w = wq[:, :, :, :, pl.ds(at, half)].reshape(width, half)
            qkv[rows, pl.ds(at, half)] = (mm(hin[rows, :], w, NN) + bias_qkv[:, at : at + half]).astype(BF16)

    first = grid.z * slots
    pairs = width // (2 * HEAD_DIM)
    lane = lax.broadcasted_iota(jnp.int32, (1, LANES), 1)
    key_at = lax.broadcasted_iota(jnp.int32, (1, SLOT), 1)

    def attend(side):
        steps = slots * pairs // 2

        @pl.loop(0, steps)
        def _(i):
            s = i // (pairs // 2)
            p = i % (pairs // 2) + side * (pairs // 2)
            rows = block_rows(s, SLOT)
            off = jnp.where(key_at < ctx_len[0, first + s] + BLOCK, 0.0, -1e30)
            at = pl.multiple_of(p * LANES, LANES)
            q2 = qkv[rows, pl.ds(at, LANES)]
            k2 = qkv[rows, pl.ds(at + width, LANES)]
            v2 = qkv[rows, pl.ds(at + 2 * width, LANES)]
            total = None
            logs = lse[rows, :]
            for h in range(2):
                mine = head_lanes(h)
                score = mm(only(mine, q2) * jnp.asarray(1.0 / math.sqrt(HEAD_DIM), BF16), k2, NT) + off
                high = jnp.max(score, axis=1, keepdims=True)
                e = jnp.exp(score - high)
                norm = jnp.sum(e, axis=1, keepdims=True)
                part = mm(e.astype(BF16), only(mine, v2), NN) * (1.0 / norm)
                total = part if total is None else total + part
                logs = jnp.where(lane == 2 * p + h, high + jnp.log(norm), logs)
            lse[rows, :] = logs
            ctx[rows, pl.ds(at, LANES)] = total.astype(BF16)
            for k in range(FWD_ATTEND_TICKS):

                @pl.when(i == (k + 1) * steps // FWD_ATTEND_TICKS - 1)
                def _():
                    flow.tick()

    lse[...] = jnp.zeros(lse.shape, F32)
    for side in range(2):
        for part in range(3):
            job = side * 3 + part
            flow.until(qkv_jobs[job])
            project(qkv_cols[job])
        attend(side)
    moves.start(lambda: (qkv, qkv_out))
    moves.start(lambda: (ctx, ctx_out))
    for s in range(slots):
        lse_rows[s] = lse[s * SLOT : (s + 1) * SLOT, :].T
    moves.start(lambda: (lse_rows, lse_out))
    for job in out_jobs:
        flow.until(job)

    @pl.loop(0, tokens // 256)
    def _(i):
        rows = block_rows(i, 256)
        attn = mm(ctx[rows, :], wo[...].reshape(width, width), NN) + vec[2:3, :]
        resid = x[rows, :].astype(F32) + temb[...].astype(F32) + attn
        centered = resid - jnp.mean(resid, axis=1, keepdims=True)
        spread = lax.rsqrt(jnp.mean(centered * centered, axis=1, keepdims=True) + norm_eps)
        unit = centered * spread
        n1[rows, :] = unit
        inv[rows, :] = jnp.broadcast_to(spread, (256, LANES))
        ub[rows, :] = (unit * vec[4:5, :] + vec[5:6, :]).astype(BF16)

    moves.start(lambda: (n1, n1_out))
    moves.start(lambda: (inv, inv_out))
    moves.start(lambda: (ub, ub_out))
    kept = [None, None]
    for j, at in enumerate(range(0, hidden, tile)):
        if at % width == 0:
            flow.until(in_jobs[at // width])
        if kept[j % 2] is not None:
            moves.wait(kept[j % 2])

        @pl.loop(0, tokens // tile)
        def _(i):
            rows = block_rows(i, tile)
            w = wi[:, :, :, :, pl.ds(at, tile)].reshape(width, tile)
            z = mm(ub[rows, :], w, NN) + bias_ff[:, at : at + tile]
            gate = 0.5 * (1.0 + lax.erf(z * math.sqrt(0.5)))
            hid[rows, pl.ds(at, tile)] = (z * gate).astype(BF16)
            bell = jnp.exp(-0.5 * z * z) * (1.0 / math.sqrt(2.0 * math.pi))
            slope[j % 2, rows, :] = (gate + z * bell).astype(BF16)

        kept[j % 2] = moves.start(lambda j=j, at=at: (slope.at[j % 2], slope_out.at[:, pl.ds(at, tile)]))
        if (at + tile) % width == 0:
            flow.tick()
    moves.start(lambda: (hid, hid_out))
    kept = [None, None]
    for j, job in enumerate(back_jobs):
        flow.until(job)
        if kept[j % 2] is not None:
            moves.wait(kept[j % 2])
        cols = slice(j * back_wide, (j + 1) * back_wide)

        @pl.loop(0, tokens // tile)
        def _(i):
            rows = block_rows(i, tile)
            w = wb[:, :, :, :, pl.ds(j * back_wide, back_wide)].reshape(hidden, back_wide)
            f = mm(hid[rows, :], w, NN) + vec[3:4, cols]
            r2[j % 2, rows, :] = n1[rows, cols] * vec[4:5, cols] + vec[5:6, cols] + f

        kept[j % 2] = moves.start(
            lambda j=j: (r2.at[j % 2], r2_out.at[:, pl.ds(j * back_wide, back_wide)])
        )
    flow.drain()
    moves.drain()


FWD_LAGS = (1, 1, 1, 1)
FWD_ATTEND_TICKS = 2


def forward(grid, context_len, inputs, timestep, small, qkv_weight, out_weight, in_weight, back_weight):
    tokens, width = inputs.shape
    hidden = in_weight.shape[1]
    slots = tokens // SLOT
    weights = (qkv_weight, out_weight, in_weight, back_weight)
    back_wide = width * width // hidden

    def whole(shard):
        return (grid.ny, grid.nx, grid.nc, grid.nz * shard.shape[0], shard.shape[1])

    out = [
        *[(whole(w), BF16) for w in weights],
        ((8, width), F32),
        ((tokens, width), BF16),
        ((tokens, 3 * width), BF16),
        ((slots, LANES, SLOT), F32),
        ((tokens, width), BF16),
        ((tokens, width), F32),
        ((tokens, LANES), F32),
        ((tokens, width), BF16),
        ((tokens, hidden), BF16),
        ((tokens, hidden), BF16),
        ((tokens, width), F32),
    ]
    jobs = 1 + 6 + 2 + hidden // width + width // back_wide
    scratch = [
        pltpu.SemaphoreType.DMA((jobs * grid.copies(),)),
        pltpu.SemaphoreType.DMA((jobs * grid.copies(),)),
        pltpu.SemaphoreType.DMA((64,)),
        pltpu.VMEM((tokens, width), BF16),
        pltpu.VMEM((tokens, width), BF16),
        pltpu.VMEM((tokens, 3 * width), BF16),
        pltpu.VMEM((tokens, width), BF16),
        pltpu.VMEM((tokens, width), F32),
        pltpu.VMEM((tokens, LANES), F32),
        pltpu.VMEM((tokens, width), BF16),
        pltpu.VMEM((tokens, hidden), BF16),
        pltpu.VMEM((2, tokens, FWD_WIDTH), BF16),
        pltpu.VMEM((2, tokens, back_wide), F32),
        pltpu.VMEM((tokens, LANES), F32),
        pltpu.VMEM((slots, LANES, SLOT), F32),
        pltpu.VMEM((8, width), F32),
        pltpu.VMEM((1, 3 * width), F32),
        pltpu.VMEM((1, hidden), F32),
        pltpu.VMEM(whole(small), BF16),
        *[pltpu.VMEM(whole(w), BF16) for w in weights],
    ]
    return pl.pallas_call(
        functools.partial(forward_kernel, grid),
        out_shape=[jax.ShapeDtypeStruct(*o) for o in out],
        in_specs=[IN_SMEM, ANY, IN_VMEM, ANY, ANY, ANY, ANY, ANY],
        out_specs=[ANY] * len(out),
        scratch_shapes=scratch,
        compiler_params=pltpu.CompilerParams(
            collective_id=1, has_side_effects=True, vmem_limit_bytes=VMEM_BYTES
        ),
        name="forward_pass",
    )(context_len, inputs, timestep, small, *weights)


def second_norm_kernel(r2, dy, vec, result, dr2, df, sums):
    resid = r2[...]
    centered = resid - jnp.mean(resid, axis=1, keepdims=True)
    spread = lax.rsqrt(jnp.mean(centered * centered, axis=1, keepdims=True) + norm_eps)
    unit = centered * spread
    result[...] = unit * vec[6:7, :] + vec[7:8, :]
    grad = dy[...].astype(F32)
    e = grad * vec[6:7, :]
    back = spread * (
        e - jnp.mean(e, axis=1, keepdims=True) - unit * jnp.mean(e * unit, axis=1, keepdims=True)
    )
    dr2[...] = back
    df[...] = back.astype(BF16)

    @pl.when(pl.program_id(0) == 0)
    def _():
        sums[...] = jnp.zeros(sums.shape, F32)

    sums[3:4, :] += jnp.sum(back, axis=0, keepdims=True)
    sums[6:7, :] += jnp.sum(grad * unit, axis=0, keepdims=True)
    sums[7:8, :] += jnp.sum(grad, axis=0, keepdims=True)


def second_norm(r2, out_grad, vec):
    tokens, width = r2.shape
    tile = 256
    rows = pl.BlockSpec((tile, width), lambda i: (i, 0))
    top = pl.BlockSpec((8, width), lambda i: (0, 0))
    return pl.pallas_call(
        second_norm_kernel,
        grid=(tokens // tile,),
        out_shape=[
            jax.ShapeDtypeStruct((tokens, width), F32),
            jax.ShapeDtypeStruct((tokens, width), F32),
            jax.ShapeDtypeStruct((tokens, width), BF16),
            jax.ShapeDtypeStruct((8, width), F32),
        ],
        in_specs=[rows, rows, top],
        out_specs=[rows, rows, rows, top],
        compiler_params=pltpu.CompilerParams(vmem_limit_bytes=VMEM_BYTES),
        name="second_norm",
    )(r2, out_grad, vec)


class Reduce(Travel):
    def __init__(self, grid, sems, bufs, other, product, out, cols):
        self.grid, self.sems, self.other, self.product, self.out, self.cols = grid, sems, other, product, out, cols
        self.sum, self.in2a, self.in2b, self.in3a, self.in3b, self.in4 = bufs
        self.half = self.sum.shape[2] // 2
        self.rows = self.sum.shape[2] // grid.nz
        self.sent = []

    def start(self):
        g = self.grid

        def store(y, x, cols, value):
            self.other[y, x, :, cols] = value.astype(BF16)

        self.product(g.off("c", 1), store)
        self.go([self.sems.remote(lambda: (self.other, self.sum, g.peer("c", 1)))])
        self.first = self.sent.pop()

    def freed(self):
        self.first().wait_send()
        self.first = None

    def second(self):
        g = self.grid
        self.landed()

        def add(y, x, cols, value):
            self.sum[y, x, :, cols] = (self.sum[y, x, :, cols].astype(F32) + value).astype(BF16)

        self.product(g.c, add)
        lo, hi = pl.ds(0, self.half), pl.ds(self.half, self.half)
        self.go(
            [
                self.sems.remote(
                    lambda k=k: (self.sum.at[g.off("y", k), :, lo], self.in2a.at[k - 1], g.peer("y", k))
                )
                for k in range(1, g.ny)
            ]
            + [
                self.sems.remote(
                    lambda k=k: (self.sum.at[:, g.off("x", k), hi], self.in2b.at[k - 1], g.peer("x", k))
                )
                for k in range(1, g.nx)
            ]
        )

    def third(self):
        g = self.grid
        self.landed()
        lo, hi = pl.ds(0, self.half), pl.ds(self.half, self.half)
        for x in range(g.nx):
            add_into(self.sum.at[g.y, x, lo], [self.in2a.at[k, x] for k in range(g.ny - 1)])
        for y in range(g.ny):
            add_into(self.sum.at[y, g.x, hi], [self.in2b.at[k, y] for k in range(g.nx - 1)])
        self.go(
            [
                self.sems.remote(
                    lambda k=k: (self.sum.at[g.y, g.off("x", k), lo], self.in3a.at[k - 1], g.peer("x", k))
                )
                for k in range(1, g.nx)
            ]
            + [
                self.sems.remote(
                    lambda k=k: (self.sum.at[g.off("y", k), g.x, hi], self.in3b.at[k - 1], g.peer("y", k))
                )
                for k in range(1, g.ny)
            ]
        )

    def fourth(self):
        g = self.grid
        self.landed()
        lo, hi = pl.ds(0, self.half), pl.ds(self.half, self.half)
        add_into(self.sum.at[g.y, g.x, lo], [self.in3a.at[k] for k in range(g.nx - 1)])
        add_into(self.sum.at[g.y, g.x, hi], [self.in3b.at[k] for k in range(g.ny - 1)])

        def part(k):
            return self.sum.at[g.y, g.x, block_rows(g.off("z", k), self.rows)]

        self.go(
            [self.sems.remote(lambda k=k: (part(k), self.in4.at[k - 1], g.peer("z", k))) for k in range(1, g.nz)]
        )

    def finish(self):
        g = self.grid
        self.landed()
        total = self.sum[g.y, g.x, block_rows(g.z, self.rows), :].astype(F32)
        for k in range(g.nz - 1):
            total += self.in4[k].astype(F32)
        self.out[:, self.cols] = total


def add_into(dst, srcs):
    total = dst[...].astype(F32)
    for src in srcs:
        total += src[...].astype(F32)
    dst[...] = total.astype(dst.dtype)


def reduce_bufs(grid, rows, width, count):
    group, half = rows * grid.nz, rows * grid.nz // 2
    ny, nx = grid.ny, grid.nx
    return [
        pltpu.VMEM((count, *shape, width), BF16)
        for shape in (
            (ny, nx, group),
            (ny - 1, nx, half),
            (nx - 1, ny, half),
            (nx - 1, half),
            (ny - 1, half),
            (grid.nz - 1, rows),
        )
    ]


class Line:
    def __init__(self):
        self.jobs, self.ticks = [], 0

    def start(self, job):
        self.jobs.append(job)
        job.start()

    def tick(self, count=1):
        for _ in range(count):
            for lag, name in ((2, "finish"), (1, "fourth"), (0, "third")):
                if 0 <= self.ticks - lag < len(self.jobs):
                    getattr(self.jobs[self.ticks - lag], name)()
            self.ticks += 1

    def drain(self):
        self.tick(len(self.jobs) + 2 - self.ticks)
        for job in self.jobs:
            job.drain()
            if job.first is not None:
                job.freed()


BWD_TILE = 512
QUERY_TILE = 256


def backward_kernel(
    grid,
    ctx_len,
    vec,
    sums_in,
    inv,
    lse,
    dr2,
    df_in,
    hid_in,
    slope_in,
    ub_in,
    n1_in,
    ctx_in,
    qkv_in,
    hin_in,
    wq_in,
    wo_in,
    wi_in,
    wb_in,
    grad_input,
    grad_qkv,
    grad_out,
    grad_in,
    grad_back,
    grad_small,
    send,
    recv,
    move_sems,
    pool,
    du,
    n1,
    sums,
    bias_sum,
    other_wide,
    other_back,
    other_small,
    *bufs,
):
    tokens, width = du.shape
    hidden = bias_sum.shape[1]
    slots = tokens // SLOT
    blocks = hidden // width
    tile = BWD_TILE
    grid.here()
    moves = Locals(move_sems)
    sems = Sems(send, recv)
    line = Line()

    def load(src, block):
        return moves.start(lambda: (src(), pool.at[block]))

    def columns(ref, j):
        return lambda: ref.at[:, pl.ds(j * width, width)]

    def weight_columns(ref, j):
        return lambda: ref.at[:, pl.ds(j * width, width)]

    hid, df, ub = [0, 1, 2, 3], 4, 5
    loads = [load(lambda: df_in, df)]
    loads += [load(columns(hid_in, j), hid[j]) for j in range(blocks)]
    du_copy = moves.start(lambda: (dr2, du))
    greet(grid)
    ff_blocks = [(6, 7, 8), (0, 1, 2)]
    dz_blocks = [3, 9]

    def load_ff(j):
        back, slope, inner = ff_blocks[j % 2]
        return [
            load(lambda: wb_in.at[pl.ds(j * width, width)], back),
            load(columns(slope_in, j), slope),
            load(weight_columns(wi_in, j), inner),
        ]

    ff_loads = {0: load_ff(0)}
    ub_load = load(lambda: ub_in, ub)
    norm_rows = n1.shape[1]

    def load_n1(i):
        return moves.start(lambda: (n1_in.at[pl.ds(i * norm_rows, norm_rows)], n1.at[i % 2]))

    n1_loads = [load_n1(0), load_n1(1)]
    sums[...] = sums_in[...]
    bias_sum[...] = jnp.zeros(bias_sum.shape, F32)

    places = [(y, x) for y in range(grid.ny) for x in range(grid.nx)]
    group = width // (len(places) * grid.nc)

    def token_product(lhs, rhs, wide):
        def product(c, take):
            @pl.loop(0, wide // tile)
            def _(n):
                cols = block_rows(n, tile)
                left = jnp.concatenate(
                    [pool[lhs, :, block_rows((y * grid.nx + x) * grid.nc + c, group)] for y, x in places], axis=1
                )
                value = mm(left, rhs(cols), TN)
                for i, (y, x) in enumerate(places):
                    take(y, x, cols, value[i * group : (i + 1) * group])

        return product

    def back_product(k, wide):
        def product(c, take):
            for i, (y, x) in enumerate(places):
                left = pool[hid[i], :, block_rows(c, width // grid.nc)]
                take(y, x, slice(None), mm(left, pool[df, :, k * wide : (k + 1) * wide], TN))

        return product

    bufs_back, bufs_wide, bufs_half, bufs_small = [bufs[6 * i : 6 * i + 6] for i in range(4)]
    back_wide = width // blocks
    back_jobs = [
        Reduce(
            grid,
            sems,
            [b.at[k] for b in bufs_back],
            other_back.at[k % 2],
            back_product(k, back_wide),
            grad_back,
            pl.ds(k * back_wide, back_wide),
        )
        for k in range(blocks)
    ]
    wide_jobs = 0

    def wide_job(lhs, rhs, out, at):
        nonlocal wide_jobs
        k = wide_jobs
        wide_jobs += 1
        return Reduce(
            grid,
            sems,
            [b.at[k] for b in bufs_wide],
            other_wide.at[k % 2],
            token_product(lhs, lambda cols: pool[rhs, :, cols], width),
            out,
            pl.ds(at, width),
        )

    for copy in loads:
        moves.wait(copy)
    line.start(back_jobs[0])
    line.start(back_jobs[1])
    for k in range(blocks):
        back_jobs[k].second()
        if k + 2 < blocks:
            back_jobs[k].freed()
            line.start(back_jobs[k + 2])

    in_jobs = []
    moves.wait(ub_load)
    moves.wait(du_copy)
    for j in range(blocks):
        back, slope, inner = ff_blocks[j % 2]
        dz = dz_blocks[j % 2]
        for copy in ff_loads.pop(j):
            moves.wait(copy)
        if j + 1 < blocks:
            ff_loads[j + 1] = load_ff(j + 1)

        @pl.loop(0, (tokens // tile) * (width // tile))
        def _(t):
            rows, cols = block_rows(t % (tokens // tile), tile), block_rows(t // (tokens // tile), tile)
            grad = mm(pool[df, rows, :], pool[back, cols, :], NT) * pool[slope, rows, cols].astype(F32)
            at = pl.ds(pl.multiple_of(j * width + t // (tokens // tile) * tile, tile), tile)
            bias_sum[:, at] += jnp.sum(grad, axis=0, keepdims=True)
            pool[dz, rows, cols] = grad.astype(BF16)

        job = wide_job(ub, dz, grad_in, j * width)
        if j >= 2:
            in_jobs[j - 2].freed()
        line.start(job)
        in_jobs.append(job)

        @pl.loop(0, (tokens // tile) * (width // tile))
        def _(t):
            rows, cols = block_rows(t % (tokens // tile), tile), block_rows(t // (tokens // tile), tile)
            du[rows, cols] += mm(pool[dz, rows, :], pool[inner, cols, :], NT)

        job.second()
        line.tick(BWD_FF_TICKS[j])

    da, out_weight, ctx, dctx = 4, 6, 7, 2
    q, k, v = 0, 8, 1
    dq, dk, dv = 3, 9, 5
    hin, wq = 4, (6, 7, 10)
    out_load = load(lambda: wo_in, out_weight)
    ctx_load = load(lambda: ctx_in, ctx)
    qkv_loads = [load(columns(qkv_in, i), block) for i, block in enumerate((q, k, v))]
    for n in range(tokens // norm_rows):
        moves.wait(n1_loads.pop(0))

        @pl.loop(0, norm_rows // 128)
        def _(i):
            rows = block_rows(n * (norm_rows // 128) + i, 128)
            unit, grad = n1[n % 2, block_rows(i, 128), :], du[rows, :]
            e = grad * vec[4:5, :]
            back = inv[rows, 0:1] * (
                e - jnp.mean(e, axis=1, keepdims=True) - unit * jnp.mean(e * unit, axis=1, keepdims=True)
            )
            sums[4:5, :] += jnp.sum(grad * unit, axis=0, keepdims=True)
            sums[5:6, :] += jnp.sum(grad, axis=0, keepdims=True)
            sums[2:3, :] += jnp.sum(back, axis=0, keepdims=True)
            du[rows, :] = back
            pool[da, rows, :] = back.astype(BF16)

        if (n + 2) * norm_rows < tokens:
            n1_loads.append(load_n1(n + 2))

    line.tick(BWD_NORM_TICKS)
    moves.wait(out_load)
    moves.wait(ctx_load)
    out_job = wide_job(ctx, da, grad_out, 0)
    in_jobs[-2].freed()
    line.start(out_job)

    @pl.loop(0, (tokens // tile) * (width // tile))
    def _(t):
        rows, cols = block_rows(t % (tokens // tile), tile), block_rows(t // (tokens // tile), tile)
        pool[dctx, rows, cols] = mm(pool[da, rows, :], pool[out_weight, cols, :], NT).astype(BF16)

    out_job.second()
    hin_load = load(lambda: hin_in, hin)
    wq_loads = [load(weight_columns(wq_in, i), block) for i, block in enumerate(wq)]
    for copy in qkv_loads:
        moves.wait(copy)
    first = grid.z * slots
    pairs = width // (2 * HEAD_DIM)
    key_at = lax.broadcasted_iota(jnp.int32, (SLOT, 1), 0)
    scale = 1.0 / math.sqrt(HEAD_DIM)

    def attend(side):
        steps = slots * pairs // 2

        @pl.loop(0, steps)
        def _(i):
            s = i // (pairs // 2)
            p = i % (pairs // 2) + side * (pairs // 2)
            keys = block_rows(s, SLOT)
            at = block_rows(p, 2 * HEAD_DIM)
            off = jnp.where(key_at < ctx_len[0, first + s] + BLOCK, 0.0, -1e30)
            k2, v2 = pool[k, keys, at], pool[v, keys, at]
            sum_k = sum_v = None
            for part in range(SLOT // QUERY_TILE):
                rows = pl.ds(pl.multiple_of(s * SLOT + part * QUERY_TILE, QUERY_TILE), QUERY_TILE)
                q2, c2 = pool[q, rows, at], pool[dctx, rows, at]
                sum_q = None
                for h in range(2):
                    mine = head_lanes(h)
                    qh = only(mine, q2) * jnp.asarray(scale, BF16)
                    ch = only(mine, c2)
                    log = lse[s, pl.ds(2 * p + h, 1), part * QUERY_TILE : (part + 1) * QUERY_TILE]
                    prob = jnp.exp(mm(k2, qh, NT) + off - log)
                    dprob = mm(v2, ch, NT)
                    dot = jnp.sum(prob * dprob, axis=0, keepdims=True)
                    dscore = (prob * (dprob - dot)).astype(BF16)
                    add_v = mm(prob.astype(BF16), ch, NN)
                    add_k = mm(dscore, qh, NN)
                    add_q = mm(dscore, only(mine, k2), TN)
                    sum_q = add_q if sum_q is None else sum_q + add_q
                    sum_k = add_k if sum_k is None else sum_k + add_k
                    sum_v = add_v if sum_v is None else sum_v + add_v
                pool[dq, rows, at] = (sum_q * scale).astype(BF16)
            pool[dk, keys, at] = sum_k.astype(BF16)
            pool[dv, keys, at] = sum_v.astype(BF16)
            for n in range(BWD_ATTEND_TICKS):

                @pl.when(i == (n + 1) * steps // BWD_ATTEND_TICKS - 1)
                def _():
                    line.tick()

    half = width // 2
    half_jobs = []

    def half_job(rhs, part, side):
        n = len(half_jobs)
        job = Reduce(
            grid,
            sems,
            [b.at[n] for b in bufs_half],
            other_wide.at[n % 2, :, :, :, pl.ds(0, half)],
            token_product(hin, lambda cols: pool[rhs, :, pl.ds(cols.start + side * half, tile)], half),
            grad_qkv,
            pl.ds(part * width + side * half, half),
        )
        half_jobs.append(job)
        return job

    out_job.freed()
    in_jobs[-1].freed()
    for side in range(2):
        attend(side)
        if side == 0:
            moves.wait(hin_load)
        else:
            sums[0:2, :] = jnp.zeros((2, width), F32)

            @pl.loop(0, tokens // 128)
            def _(i):
                rows = block_rows(i, 128)
                sums[0:1, :] += jnp.sum(pool[dq, rows, :].astype(F32), axis=0, keepdims=True)
                sums[1:2, :] += jnp.sum(pool[dv, rows, :].astype(F32), axis=0, keepdims=True)

            def small_product(c, take):
                for y, x in places:
                    at = (y * grid.nx + x) * grid.nc + c
                    eight = sums[:, block_rows(at, LANES)]
                    rows = []
                    for z in range(grid.nz):
                        rows += [eight, bias_sum[:, block_rows(at * grid.nz + z, LANES)], jnp.zeros((7, LANES), F32)]
                    take(y, x, slice(None), jnp.concatenate(rows, axis=0))

            small = Reduce(
                grid, sems, [b.at[0] for b in bufs_small], other_small, small_product, grad_small, slice(None)
            )
            line.start(small)
            small.second()
        for part, rhs in enumerate((dq, dk, dv)):
            job = half_job(rhs, part, side)
            if len(half_jobs) > 2:
                half_jobs[-3].freed()
            line.start(job)
            if part > 0:
                half_jobs[-2].second()
        half_jobs[-1].second()

    for copy in wq_loads:
        moves.wait(copy)
    for n in range(tokens // tile):
        rows = pl.ds(n * tile, tile)

        @pl.loop(0, width // tile)
        def _(t):
            cols = block_rows(t, tile)
            total = du[rows, cols]
            for block, weight in zip((dq, dk, dv), wq):
                total += mm(pool[block, rows, :], pool[weight, cols, :], NT)
            du[rows, cols] = total

        moves.start(lambda rows=rows: (du.at[rows], grad_input.at[rows]))
        line.tick(BWD_END_TICKS)
    line.drain()
    moves.drain()


BWD_FF_TICKS = (0, 1, 2, 2)
BWD_NORM_TICKS = 1
BWD_ATTEND_TICKS = 2
BWD_END_TICKS = 1


def backward(grid, context_len, vec, sums, inv, lse, dr2, df, hid, slope, ub, n1, ctx, qkv, hin, weights):
    tokens, width = n1.shape
    hidden = hid.shape[1]
    blocks = hidden // width
    count = grid.count
    rows = width // count
    jobs = blocks + blocks + 1 + 6 + 1
    out = [
        (tokens, width),
        (rows, 3 * width),
        (rows, width),
        (rows, hidden),
        (hidden // count, width),
        (16, LANES),
    ]
    scratch = [
        pltpu.SemaphoreType.DMA((jobs * grid.copies(),)),
        pltpu.SemaphoreType.DMA((jobs * grid.copies(),)),
        pltpu.SemaphoreType.DMA((64,)),
        pltpu.VMEM((11, tokens, width), BF16),
        pltpu.VMEM((tokens, width), F32),
        pltpu.VMEM((2, 256, width), F32),
        pltpu.VMEM((8, width), F32),
        pltpu.VMEM((1, hidden), F32),
        pltpu.VMEM((2, grid.ny, grid.nx, grid.nz * rows, width), BF16),
        pltpu.VMEM((2, grid.ny, grid.nx, hidden // count * grid.nz, width // blocks), BF16),
        pltpu.VMEM((grid.ny, grid.nx, 16 * grid.nz, LANES), BF16),
        *reduce_bufs(grid, hidden // count, width // blocks, blocks),
        *reduce_bufs(grid, rows, width, blocks + 1),
        *reduce_bufs(grid, rows, width // 2, 6),
        *reduce_bufs(grid, 16, LANES, 1),
    ]
    return pl.pallas_call(
        functools.partial(backward_kernel, grid),
        out_shape=[jax.ShapeDtypeStruct(o, F32) for o in out],
        in_specs=[IN_SMEM, *[IN_VMEM] * 4, *[ANY] * 13],
        out_specs=[ANY, *[IN_VMEM] * 5],
        scratch_shapes=scratch,
        compiler_params=pltpu.CompilerParams(
            collective_id=2, has_side_effects=True, vmem_limit_bytes=VMEM_BYTES
        ),
        name="backward_pass",
    )(context_len, vec, sums, inv, lse, dr2, df, hid, slope, ub, n1, ctx, qkv, hin, *weights)


def shards(
    grid, inputs, timestep, context_len, out_grad, qkv_weight, out_weight, in_weight, back_weight, vectors, bias_ff
):
    weights = (qkv_weight, out_weight, in_weight, back_weight)
    if not fits(grid, inputs, vectors, bias_ff, in_weight):
        return plain_shards(inputs, timestep, context_len, out_grad, *weights, vectors, bias_ff)
    small = fold_small(grid, vectors, bias_ff)
    *full, vec, hin, qkv, lse, ctx, n1, inv, ub, hid, slope, r2 = forward(
        grid, context_len, inputs, timestep, small, *weights
    )
    full = [f.reshape(-1, f.shape[-1]) for f in full]
    result, dr2, df, sums = second_norm(r2, out_grad, vec)
    grad_input, grad_qkv, grad_out, grad_in, grad_back, grad_small = backward(
        grid, context_len, vec, sums, inv, lse, dr2, df, hid, slope, ub, n1, ctx, qkv, hin, full
    )
    rows = vectors.shape[0]
    mine = lax.dynamic_slice(grad_small, (0, lax.axis_index("seq") * rows), (8, rows))
    return (result, grad_input, grad_qkv, grad_out, grad_in, grad_back, mine.T, grad_small[8])


def fits(grid, inputs, vectors, bias_ff, in_weight):
    tokens, width = inputs.shape
    return (
        tokens == width
        and tokens % SLOT == 0
        and vectors.shape[0] * grid.nz == LANES
        and bias_ff.shape[0] == LANES
        and in_weight.shape[1] % width == 0
        and vectors.shape[0] % 32 == 0
        and grid.nc == 2
        and grid.nx > 1
        and grid.ny > 1
        and grid.nz > 1
        and in_weight.shape[1] == grid.ny * grid.nx * width
    )


def specs():
    rows = P(("dp", "seq"), None)
    return dict(
        in_specs=(rows, P("dp", None), P("dp", None), *[rows] * 6, P(("dp", "seq"))),
        out_specs=(*[rows] * 7, P(("dp", "seq"))),
    )


def solution(mesh):
    return jax.shard_map(functools.partial(shards, Grid(mesh)), mesh=mesh, check_vma=False, **specs())
```

```python
import functools
import math

import jax
import jax.numpy as jnp
from jax import lax
from jax.experimental import pallas as pl
from jax.experimental.pallas import tpu as pltpu
from jax.sharding import PartitionSpec as P

HEAD_DIM = 64
SLOT = 512
BLOCK = 25


norm_eps = 1e-05


def norm_forward(resid, gain_vec, shift_vec):
    row_mean = jnp.mean(resid, axis=-1, keepdims=True)
    centered = resid - row_mean
    variance = jnp.mean(centered * centered, axis=-1, keepdims=True)
    inv_std = lax.rsqrt(variance + norm_eps)
    normed = centered * inv_std
    return (normed * gain_vec + shift_vec, normed, inv_std)


def norm_backward(grad_out, normed, inv_std, gain_vec):
    grad_norm = grad_out * gain_vec
    grad_resid = inv_std * (
        grad_norm
        - jnp.mean(grad_norm, axis=-1, keepdims=True)
        - normed * jnp.mean(grad_norm * normed, axis=-1, keepdims=True)
    )
    return (grad_resid, jnp.sum(grad_out * normed, axis=0), jnp.sum(grad_out, axis=0))


def gelu_slope(pre_act):
    return 0.5 * (1.0 + lax.erf(pre_act * math.sqrt(0.5))) + pre_act * jnp.exp(
        -0.5 * pre_act * pre_act
    ) / math.sqrt(2.0 * math.pi)


def slot_scores(queries, key_vecs, live_len):
    inv_root = 1.0 / math.sqrt(HEAD_DIM)
    raw_scores = (
        jnp.einsum("qhd,khd->hqk", queries, key_vecs, preferred_element_type=jnp.float32) * inv_root
    )
    key_valid = jnp.arange(SLOT, dtype=jnp.int32) < live_len
    return jnp.where(key_valid[None, None, :], raw_scores, -1e30)


def slot_forward(parts):
    queries, key_vecs, values, live_len = parts
    masked = slot_scores(queries, key_vecs, live_len)
    row_max = jnp.max(masked, axis=-1, keepdims=True)
    exp_scores = jnp.exp(masked - row_max)
    exp_total = jnp.sum(exp_scores, axis=-1, keepdims=True)
    attn_probs = (exp_scores / exp_total).astype(jnp.bfloat16)
    context = jnp.einsum("hqk,khd->qhd", attn_probs, values, preferred_element_type=jnp.float32)
    return (context.astype(jnp.bfloat16), (row_max + jnp.log(exp_total))[..., 0])


def slot_backward(parts):
    queries, key_vecs, values, live_len, log_total, grad_ctx = parts
    inv_root = 1.0 / math.sqrt(HEAD_DIM)
    masked = slot_scores(queries, key_vecs, live_len)
    attn_exact = jnp.exp(masked - log_total[..., None])
    attn_probs = attn_exact.astype(jnp.bfloat16)
    grad_probs = jnp.einsum("qhd,khd->hqk", grad_ctx, values, preferred_element_type=jnp.float32)
    row_dot = jnp.sum(attn_exact * grad_probs, axis=-1, keepdims=True)
    grad_scores = (attn_exact * (grad_probs - row_dot)).astype(jnp.bfloat16)
    grad_query = (
        jnp.einsum("hqk,khd->qhd", grad_scores, key_vecs, preferred_element_type=jnp.float32)
        * inv_root
    )
    grad_key = (
        jnp.einsum("hqk,qhd->khd", grad_scores, queries, preferred_element_type=jnp.float32)
        * inv_root
    )
    grad_value = jnp.einsum(
        "hqk,qhd->khd", attn_probs, grad_ctx, preferred_element_type=jnp.float32
    )
    return (
        grad_query.astype(jnp.bfloat16),
        grad_key.astype(jnp.bfloat16),
        grad_value.astype(jnp.bfloat16),
    )


def plain_shards(
    inputs,
    timestep,
    context_len,
    out_grad,
    qkv_weight,
    out_weight,
    in_weight,
    back_weight,
    vectors,
    bias_ff,
):
    qkv_full, out_full, in_full, back_full, vec_full, bias_full = (
        lax.all_gather(qkv_weight, ("dp", "seq"), axis=0, tiled=True),
        lax.all_gather(out_weight, ("dp", "seq"), axis=0, tiled=True),
        lax.all_gather(in_weight, ("dp", "seq"), axis=0, tiled=True),
        lax.all_gather(back_weight, ("dp", "seq"), axis=0, tiled=True),
        lax.all_gather(vectors, ("dp", "seq"), axis=0, tiled=True),
        lax.all_gather(bias_ff, ("dp", "seq"), axis=0, tiled=True),
    )
    vec_all = vec_full.astype(jnp.float32)
    bias_all = bias_full.astype(jnp.float32)
    width = inputs.shape[1]
    resid_in = inputs.astype(jnp.float32) + timestep.astype(jnp.float32)
    layer_in = resid_in.astype(jnp.bfloat16)
    qkv_proj = jnp.dot(layer_in, qkv_full, preferred_element_type=jnp.float32)
    queries = (qkv_proj[:, :width] + vec_all[:, 0]).astype(jnp.bfloat16)
    key_vecs = qkv_proj[:, width : 2 * width].astype(jnp.bfloat16)
    values = (qkv_proj[:, 2 * width :] + vec_all[:, 1]).astype(jnp.bfloat16)
    q_heads, k_heads, v_heads = (
        lax.all_to_all(queries, "seq", split_axis=1, concat_axis=0, tiled=True),
        lax.all_to_all(key_vecs, "seq", split_axis=1, concat_axis=0, tiled=True),
        lax.all_to_all(values, "seq", split_axis=1, concat_axis=0, tiled=True),
    )
    slot_count = context_len.shape[1]
    head_width = q_heads.shape[1]
    slot_shape = (slot_count, SLOT, head_width // HEAD_DIM, HEAD_DIM)
    live_lens = context_len[0] + BLOCK
    q_slots = q_heads.reshape(slot_shape)
    k_slots = k_heads.reshape(slot_shape)
    v_slots = v_heads.reshape(slot_shape)
    ctx_slots, log_totals = lax.map(slot_forward, (q_slots, k_slots, v_slots, live_lens))
    ctx_tokens = lax.all_to_all(
        ctx_slots.reshape(slot_count * SLOT, head_width),
        "seq",
        split_axis=0,
        concat_axis=1,
        tiled=True,
    )
    attn_out = jnp.dot(ctx_tokens, out_full, preferred_element_type=jnp.float32) + vec_all[:, 2]
    normed_mid, unit_mid, inv_mid = norm_forward(resid_in + attn_out, vec_all[:, 4], vec_all[:, 5])
    mid_low = normed_mid.astype(jnp.bfloat16)
    pre_act = jnp.dot(mid_low, in_full, preferred_element_type=jnp.float32) + bias_all
    hidden = jax.nn.gelu(pre_act, approximate=False).astype(jnp.bfloat16)
    branch = jnp.dot(hidden, back_full, preferred_element_type=jnp.float32) + vec_all[:, 3]
    result, unit_out, inv_out = norm_forward(normed_mid + branch, vec_all[:, 6], vec_all[:, 7])
    grad_two, gain_out_grad, shift_out_grad = norm_backward(
        out_grad.astype(jnp.float32), unit_out, inv_out, vec_all[:, 6]
    )
    branch_low = grad_two.astype(jnp.bfloat16)
    grad_backw = jnp.einsum("tf,td->fd", hidden, branch_low, preferred_element_type=jnp.float32)
    grad_hidden = jnp.einsum("td,fd->tf", branch_low, back_full, preferred_element_type=jnp.float32)
    grad_pre = grad_hidden * gelu_slope(pre_act)
    bias_grad = jnp.sum(grad_pre, axis=0)
    pre_low = grad_pre.astype(jnp.bfloat16)
    grad_inw = jnp.einsum("td,tf->df", mid_low, pre_low, preferred_element_type=jnp.float32)
    grad_mid = grad_two + jnp.einsum(
        "tf,df->td", pre_low, in_full, preferred_element_type=jnp.float32
    )
    grad_one, gain_mid_grad, shift_mid_grad = norm_backward(
        grad_mid, unit_mid, inv_mid, vec_all[:, 4]
    )
    attn_low = grad_one.astype(jnp.bfloat16)
    grad_outw = jnp.einsum("td,te->de", ctx_tokens, attn_low, preferred_element_type=jnp.float32)
    grad_ctx = jnp.einsum(
        "te,de->td", attn_low, out_full, preferred_element_type=jnp.float32
    ).astype(jnp.bfloat16)
    grad_ctx_heads = lax.all_to_all(grad_ctx, "seq", split_axis=1, concat_axis=0, tiled=True)
    grad_q, grad_k, grad_v = lax.map(
        slot_backward,
        (q_slots, k_slots, v_slots, live_lens, log_totals, grad_ctx_heads.reshape(slot_shape)),
    )
    token_shape = (slot_count * SLOT, head_width)
    grad_q_tok, grad_k_tok, grad_v_tok = (
        lax.all_to_all(grad_q.reshape(token_shape), "seq", split_axis=0, concat_axis=1, tiled=True),
        lax.all_to_all(grad_k.reshape(token_shape), "seq", split_axis=0, concat_axis=1, tiled=True),
        lax.all_to_all(grad_v.reshape(token_shape), "seq", split_axis=0, concat_axis=1, tiled=True),
    )
    grad_proj = jnp.concatenate([grad_q_tok, grad_k_tok, grad_v_tok], axis=1)
    grad_qkvw = jnp.einsum("td,te->de", layer_in, grad_proj, preferred_element_type=jnp.float32)
    grad_input = grad_one + jnp.einsum(
        "te,de->td", grad_proj, qkv_full, preferred_element_type=jnp.float32
    )
    vec_grads = jnp.stack(
        [
            jnp.sum(grad_q_tok.astype(jnp.float32), axis=0),
            jnp.sum(grad_v_tok.astype(jnp.float32), axis=0),
            jnp.sum(grad_one, axis=0),
            jnp.sum(grad_two, axis=0),
            gain_mid_grad,
            shift_mid_grad,
            gain_out_grad,
            shift_out_grad,
        ],
        axis=1,
    )
    share_qkv, share_out, share_in, share_back, share_vec, share_bias = (
        lax.psum_scatter(grad_qkvw, ("dp", "seq"), scatter_dimension=0, tiled=True),
        lax.psum_scatter(grad_outw, ("dp", "seq"), scatter_dimension=0, tiled=True),
        lax.psum_scatter(grad_inw, ("dp", "seq"), scatter_dimension=0, tiled=True),
        lax.psum_scatter(grad_backw, ("dp", "seq"), scatter_dimension=0, tiled=True),
        lax.psum_scatter(vec_grads, ("dp", "seq"), scatter_dimension=0, tiled=True),
        lax.psum_scatter(bias_grad, ("dp", "seq"), scatter_dimension=0, tiled=True),
    )
    return (result, grad_input, share_qkv, share_out, share_in, share_back, share_vec, share_bias)


MESH = pl.DeviceIdType.MESH
LANES = 128
F32 = jnp.float32
BF16 = jnp.bfloat16
NN = (((1,), (0,)), ((), ()))
NT = (((1,), (1,)), ((), ()))
TN = (((0,), (0,)), ((), ()))
ANY = pl.BlockSpec(memory_space=pl.ANY)
IN_VMEM = pl.BlockSpec(memory_space=pltpu.VMEM)
IN_SMEM = pl.BlockSpec(memory_space=pltpu.SMEM)
VMEM_BYTES = 62 << 20


def mm(a, b, dims):
    return lax.dot_general(a, b, dims, preferred_element_type=F32)


class Grid:
    def __init__(self, mesh):
        dp, self.nz = mesh.shape["dp"], mesh.shape["seq"]
        self.nc = 2 if dp % 2 == 0 else 1
        rest = dp // self.nc
        self.nx = max(k for k in range(1, math.isqrt(rest) + 1) if rest % k == 0)
        self.ny = rest // self.nx
        self.count = dp * self.nz
        self.groups = [(y, x, c) for y in range(self.ny) for x in range(self.nx) for c in range(self.nc)]

    def here(self):
        dp = lax.axis_index("dp")
        self.z = lax.axis_index("seq")
        self.c = dp % self.nc
        self.x = (dp // self.nc) % self.nx
        self.y = dp // (self.nc * self.nx)

    def off(self, axis, step):
        return (getattr(self, axis) + step) % getattr(self, "n" + axis)

    def peer(self, axis, step):
        at = {name: getattr(self, name) for name in "yxcz"}
        at[axis] = self.off(axis, step)
        return ((at["y"] * self.nx + at["x"]) * self.nc + at["c"], at["z"])

    def peers(self):
        return [self.peer(axis, step) for axis in "zxyc" for step in range(1, getattr(self, "n" + axis))]

    def copies(self):
        return 2 * (self.nz - 1) + 2 * (self.nx - 1) + 2 * (self.ny - 1) + self.nc - 1


def greet(grid):
    barrier = pltpu.get_barrier_semaphore()
    peers = grid.peers()
    for peer in peers:
        pl.semaphore_signal(barrier, inc=1, device_id=peer, device_id_type=MESH)
    pl.semaphore_wait(barrier, len(peers))


class Sems:
    def __init__(self, send, recv):
        self.send, self.recv, self.used = send, recv, 0

    def remote(self, ends):
        k = self.used
        self.used += 1

        def copy():
            src, dst, device = ends()
            return pltpu.make_async_remote_copy(
                src_ref=src,
                dst_ref=dst,
                send_sem=self.send.at[k],
                recv_sem=self.recv.at[k],
                device_id=device,
                device_id_type=MESH,
            )

        return copy


class Locals:
    def __init__(self, sems):
        self.sems, self.used, self.open = sems, 0, []

    def start(self, ends):
        k = self.used
        self.used += 1

        def copy():
            src, dst = ends()
            return pltpu.make_async_copy(src, dst, self.sems.at[k])

        copy().start()
        self.open.append(copy)
        return copy

    def wait(self, copy):
        copy().wait()
        self.open.remove(copy)

    def drain(self):
        for copy in self.open:
            copy().wait()
        self.open = []


def block_rows(start, size):
    return pl.ds(pl.multiple_of(start * size, size), size)


class Travel:
    def go(self, copies):
        for copy in copies:
            copy().start()
        self.sent += copies
        self.flying = copies

    def landed(self):
        for copy in self.flying:
            copy().wait_recv()

    def drain(self):
        for copy in self.sent:
            copy().wait_send()
        self.sent = []


class Gather(Travel):
    def __init__(self, grid, sems, moves, shard, full, cols, keep=None, late_z=False):
        self.grid, self.sems, self.moves = grid, sems, moves
        self.shard, self.full, self.cols, self.keep, self.late_z = shard, full, cols, keep, late_z
        self.half = shard.shape[0] // 2
        self.sent = []

    def place(self, half=None, y=None, x=None, z=None):
        g = self.grid
        take = lambda at, size: pl.ds(0, size) if at is None else at
        rows = pl.ds(0, 2 * self.half) if half is None else pl.ds(half * self.half, self.half)
        return self.full.at[take(y, g.ny), take(x, g.nx), g.c, take(z, g.nz), rows, self.cols]

    def to(self, axis, part):
        g = self.grid
        return [
            self.sems.remote(lambda k=k: (part(), part(), g.peer(axis, k)))
            for k in range(1, getattr(g, "n" + axis))
        ]

    def start(self):
        g = self.grid
        src = lambda: self.shard.at[:, self.cols]
        self.own = self.moves.start(lambda: (src(), self.place(y=g.y, x=g.x, z=g.z)))
        if self.late_z:
            self.go(
                [
                    self.sems.remote(
                        lambda k=k, axis=axis, half=half: (
                            self.shard.at[pl.ds(half * self.half, self.half), self.cols],
                            self.place(half, g.y, g.x, g.z),
                            g.peer(axis, k),
                        )
                    )
                    for half, axis in enumerate("xy")
                    for k in range(1, getattr(g, "n" + axis))
                ]
            )
        else:
            self.go(
                [
                    self.sems.remote(lambda k=k: (src(), self.place(y=g.y, x=g.x, z=g.z), g.peer("z", k)))
                    for k in range(1, g.nz)
                ]
            )

    def second(self):
        g = self.grid
        self.landed()
        self.moves.wait(self.own)
        if self.late_z:
            self.go(self.to("z", lambda: self.place(0, y=g.y, z=g.z)) + self.to("z", lambda: self.place(1, x=g.x, z=g.z)))
        else:
            self.go(self.to("x", lambda: self.place(0, g.y, g.x)) + self.to("y", lambda: self.place(1, g.y, g.x)))

    def third(self):
        g = self.grid
        self.landed()
        self.go(self.to("y", lambda: self.place(0, y=g.y)) + self.to("x", lambda: self.place(1, x=g.x)))

    def fourth(self):
        self.landed()
        self.go(self.to("c", self.place))

    def finish(self):
        self.landed()
        if self.keep is not None:
            every = lambda ref: ref.at[:, :, :, :, :, self.cols]
            self.moves.start(lambda: (every(self.full), every(self.keep)))


class Flow:
    STAGES = ("start", "second", "third", "fourth", "finish")

    def __init__(self, jobs, lags):
        steps = [
            (k + sum(lags[:s]), -s, k, name) for k in range(len(jobs)) for s, name in enumerate(self.STAGES)
        ]
        self.jobs, self.steps, self.done = jobs, sorted(steps), 0

    def tick(self):
        if self.done < len(self.steps):
            due = self.steps[self.done][0]
            while self.done < len(self.steps) and self.steps[self.done][0] == due:
                self.step()

    def step(self):
        _, _, k, name = self.steps[self.done]
        getattr(self.jobs[k], name)()
        self.done += 1

    def until(self, job):
        last = max(i for i, (_, _, k, name) in enumerate(self.steps) if name == "finish" and self.jobs[k] is job)
        while self.done <= last:
            self.step()

    def drain(self):
        while self.done < len(self.steps):
            self.step()
        for job in self.jobs:
            job.drain()


def head_lanes(h):
    return lax.broadcasted_iota(jnp.int32, (1, 2 * HEAD_DIM), 1) // HEAD_DIM == h


def only(lanes, block):
    return jnp.where(lanes, block, 0).astype(BF16)


def fold_small(grid, vectors, bias_ff):
    rows = vectors.shape[0]
    tiled = jnp.tile(vectors.T, (1, LANES // rows))
    mine = jnp.arange(LANES) // rows == lax.axis_index("seq")
    tiled = jnp.where(mine[None, :], tiled, 0).astype(BF16)
    return jnp.concatenate([tiled, bias_ff[None, :], jnp.zeros((23, LANES), BF16)], axis=0)


FWD_WIDTH = 512


LOG_LANES = 4


def forward_kernel(
    grid,
    ctx_len,
    x_in,
    temb,
    small,
    wq_in,
    wo_in,
    wi_in,
    wb_in,
    wq_out,
    wo_out,
    wi_out,
    wb_out,
    vec_out,
    hin_out,
    qkv_out,
    logs_out,
    ctx_out,
    n1_out,
    ub_out,
    hid_out,
    slope_out,
    r2_out,
    send,
    recv,
    move_sems,
    x,
    hin,
    qkv,
    ctx,
    n1,
    ub,
    hid,
    slope,
    r2,
    lse,
    logs_parts,
    vec,
    bias_qkv,
    bias_ff,
    small_full,
    wq,
    wo,
    wi,
    wb,
):
    tokens, width = hin.shape
    hidden = hid.shape[1]
    slots = tokens // SLOT
    tile = FWD_WIDTH
    grid.here()
    moves = Locals(move_sems)
    x_copy = moves.start(lambda: (x_in, x))
    greet(grid)
    sems = Sems(send, recv)

    def gather(shard, full, at, wide, keep, late_z=False):
        return Gather(grid, sems, moves, shard, full, pl.ds(at, wide), keep, late_z)

    small_job = gather(small, small_full, 0, LANES, None)
    half = width // 2
    qkv_cols = [part * width + side * half for side in range(2) for part in range(3)]
    qkv_jobs = [gather(wq_in, wq, at, half, wq_out) for at in qkv_cols]
    out_jobs = [gather(wo_in, wo, at, half, wo_out) for at in range(0, width, half)]
    in_jobs = [gather(wi_in, wi, at, width, wi_out) for at in range(0, hidden, width)]
    back_wide = width * width // hidden
    back_jobs = [gather(wb_in, wb, at, back_wide, wb_out) for at in range(0, width, back_wide)]
    for k in FWD_LATE_Z:
        ([*qkv_jobs, *out_jobs, *in_jobs, *back_jobs][k]).late_z = True
    flow = Flow([small_job, *qkv_jobs, *out_jobs, *in_jobs, *back_jobs], FWD_LAGS)
    flow.tick()
    flow.tick()

    moves.wait(x_copy)

    @pl.loop(0, tokens // 128)
    def _(i):
        at = block_rows(i, 128)
        hin[at, :] = (x[at, :].astype(F32) + temb[...].astype(F32)).astype(BF16)

    moves.start(lambda: (hin, hin_out))
    flow.until(small_job)
    for i, (y, xx, c) in enumerate(grid.groups):
        tiles = [small_full[y, xx, c, z, pl.ds(0, 16), :].astype(F32) for z in range(grid.nz)]
        vec[:, i * LANES : (i + 1) * LANES] = sum(t[:8] for t in tiles)
        for z, t in enumerate(tiles):
            at = (i * grid.nz + z) * LANES
            bias_ff[:, at : at + LANES] = t[8:9]
    moves.start(lambda: (vec, vec_out))
    bias_qkv[:, :width] = vec[0:1, :]
    bias_qkv[:, width : 2 * width] = jnp.zeros((1, width), F32)
    bias_qkv[:, 2 * width :] = vec[1:2, :]

    def project(at):
        @pl.loop(0, tokens // tile)
        def _(i):
            rows = block_rows(i, tile)
            w = wq[:, :, :, :, :, pl.ds(at, half)].reshape(width, half)
            qkv[rows, pl.ds(at, half)] = (mm(hin[rows, :], w, NN) + bias_qkv[:, at : at + half]).astype(BF16)

    first = grid.z * slots
    pairs = width // (2 * HEAD_DIM)
    lane = lax.broadcasted_iota(jnp.int32, (1, LANES), 1)
    key_at = lax.broadcasted_iota(jnp.int32, (1, SLOT), 1)

    def attend(side):
        steps = slots * pairs // 2

        @pl.loop(0, steps)
        def _(i):
            s = i // (pairs // 2)
            p = i % (pairs // 2) + side * (pairs // 2)
            rows = block_rows(s, SLOT)
            off = jnp.where(key_at < ctx_len[0, first + s] + BLOCK, 0.0, -1e30)
            at = pl.multiple_of(p * LANES, LANES)
            q2 = qkv[rows, pl.ds(at, LANES)]
            k2 = qkv[rows, pl.ds(at + width, LANES)]
            v2 = qkv[rows, pl.ds(at + 2 * width, LANES)]
            total = None
            logs = lse[rows, :]
            for h in range(2):
                mine = head_lanes(h)
                score = mm(only(mine, q2) * jnp.asarray(1.0 / math.sqrt(HEAD_DIM), BF16), k2, NT) + off
                high = jnp.max(score, axis=1, keepdims=True)
                e = jnp.exp(score - high)
                norm = jnp.sum(e, axis=1, keepdims=True)
                part = mm(e.astype(BF16), only(mine, v2), NN) * (1.0 / norm)
                total = part if total is None else total + part
                logs = jnp.where(lane // LOG_LANES == 2 * p + h, high + jnp.log(norm), logs)
            lse[rows, :] = logs
            ctx[rows, pl.ds(at, LANES)] = total.astype(BF16)
            for k in range(FWD_ATTEND_TICKS):

                @pl.when(i == (k + 1) * steps // FWD_ATTEND_TICKS - 1)
                def _():
                    flow.tick()

    lse[...] = jnp.zeros(lse.shape, F32)
    for side in range(2):
        for part in range(3):
            job = side * 3 + part
            flow.until(qkv_jobs[job])
            project(qkv_cols[job])
        attend(side)
    moves.start(lambda: (qkv, qkv_out))
    moves.start(lambda: (ctx, ctx_out))

    @pl.loop(0, tokens // 128)
    def _(i):
        rows = block_rows(i, 128)
        rest, parts = lse[rows, :], []
        for _ in range(LOG_LANES - 1):
            parts.append(rest.astype(BF16).astype(F32))
            rest = rest - parts[-1]
        value = jnp.ones((128, LANES), F32)
        for n, part in enumerate(parts):
            value = jnp.where(lane % LOG_LANES == n + 1, part, value)
        logs_parts[rows, :] = value.astype(BF16)

    moves.start(lambda: (logs_parts, logs_out))
    for job in out_jobs:
        flow.until(job)

    @pl.loop(0, tokens // 256)
    def _(i):
        rows = block_rows(i, 256)
        attn = mm(ctx[rows, :], wo[...].reshape(width, width), NN) + vec[2:3, :]
        resid = x[rows, :].astype(F32) + temb[...].astype(F32) + attn
        centered = resid - jnp.mean(resid, axis=1, keepdims=True)
        spread = lax.rsqrt(jnp.mean(centered * centered, axis=1, keepdims=True) + norm_eps)
        unit = centered * spread
        n1[rows, :width] = unit
        n1[rows, width:] = jnp.broadcast_to(spread, (256, LANES))
        ub[rows, :] = (unit * vec[4:5, :] + vec[5:6, :]).astype(BF16)

    moves.start(lambda: (n1, n1_out))
    moves.start(lambda: (ub, ub_out))
    kept = [None, None]
    for j, at in enumerate(range(0, hidden, tile)):
        if at % width == 0:
            flow.until(in_jobs[at // width])
        if kept[j % 2] is not None:
            moves.wait(kept[j % 2])

        @pl.loop(0, tokens // tile)
        def _(i):
            rows = block_rows(i, tile)
            w = wi[:, :, :, :, :, pl.ds(at, tile)].reshape(width, tile)
            z = mm(ub[rows, :], w, NN) + bias_ff[:, at : at + tile]
            gate = 0.5 * (1.0 + lax.erf(z * math.sqrt(0.5)))
            hid[rows, pl.ds(at, tile)] = (z * gate).astype(BF16)
            bell = jnp.exp(-0.5 * z * z) * (1.0 / math.sqrt(2.0 * math.pi))
            slope[j % 2, rows, :] = (gate + z * bell).astype(BF16)

        kept[j % 2] = moves.start(lambda j=j, at=at: (slope.at[j % 2], slope_out.at[:, pl.ds(at, tile)]))
        if (at + tile) % width == 0:
            flow.tick()
    moves.start(lambda: (hid, hid_out))
    kept = [None, None]
    for j, job in enumerate(back_jobs):
        flow.until(job)
        if kept[j % 2] is not None:
            moves.wait(kept[j % 2])
        cols = slice(j * back_wide, (j + 1) * back_wide)

        @pl.loop(0, tokens // tile)
        def _(i):
            rows = block_rows(i, tile)
            w = wb[:, :, :, :, :, pl.ds(j * back_wide, back_wide)].reshape(hidden, back_wide)
            f = mm(hid[rows, :], w, NN) + vec[3:4, cols]
            r2[j % 2, rows, :] = n1[rows, cols] * vec[4:5, cols] + vec[5:6, cols] + f

        kept[j % 2] = moves.start(
            lambda j=j: (r2.at[j % 2], r2_out.at[:, pl.ds(j * back_wide, back_wide)])
        )
    flow.drain()
    moves.drain()


FWD_LAGS = (2, 2, 2, 1)
FWD_LATE_Z = ()
FWD_ATTEND_TICKS = 2


def forward(grid, context_len, inputs, timestep, small, qkv_weight, out_weight, in_weight, back_weight):
    tokens, width = inputs.shape
    hidden = in_weight.shape[1]
    weights = (qkv_weight, out_weight, in_weight, back_weight)
    back_wide = width * width // hidden

    def whole(shard):
        return (grid.ny, grid.nx, grid.nc, grid.nz, *shard.shape)

    out = [
        *[(whole(w), BF16) for w in weights],
        ((8, width), F32),
        ((tokens, width), BF16),
        ((tokens, 3 * width), BF16),
        ((tokens, LANES), BF16),
        ((tokens, width), BF16),
        ((tokens, width + LANES), F32),
        ((tokens, width), BF16),
        ((tokens, hidden), BF16),
        ((tokens, hidden), BF16),
        ((tokens, width), F32),
    ]
    jobs = 1 + 6 + 2 + hidden // width + width // back_wide
    scratch = [
        pltpu.SemaphoreType.DMA((jobs * grid.copies(),)),
        pltpu.SemaphoreType.DMA((jobs * grid.copies(),)),
        pltpu.SemaphoreType.DMA((64,)),
        pltpu.VMEM((tokens, width), BF16),
        pltpu.VMEM((tokens, width), BF16),
        pltpu.VMEM((tokens, 3 * width), BF16),
        pltpu.VMEM((tokens, width), BF16),
        pltpu.VMEM((tokens, width + LANES), F32),
        pltpu.VMEM((tokens, width), BF16),
        pltpu.VMEM((tokens, hidden), BF16),
        pltpu.VMEM((2, tokens, FWD_WIDTH), BF16),
        pltpu.VMEM((2, tokens, back_wide), F32),
        pltpu.VMEM((tokens, LANES), F32),
        pltpu.VMEM((tokens, LANES), BF16),
        pltpu.VMEM((8, width), F32),
        pltpu.VMEM((1, 3 * width), F32),
        pltpu.VMEM((1, hidden), F32),
        pltpu.VMEM(whole(small), BF16),
        *[pltpu.VMEM(whole(w), BF16) for w in weights],
    ]
    return pl.pallas_call(
        functools.partial(forward_kernel, grid),
        out_shape=[jax.ShapeDtypeStruct(*o) for o in out],
        in_specs=[IN_SMEM, ANY, IN_VMEM, ANY, ANY, ANY, ANY, ANY],
        out_specs=[ANY] * len(out),
        scratch_shapes=scratch,
        compiler_params=pltpu.CompilerParams(
            collective_id=1, has_side_effects=True, vmem_limit_bytes=VMEM_BYTES
        ),
        name="forward_pass",
    )(context_len, inputs, timestep, small, *weights)


def second_norm_kernel(r2, dy, vec, result, dr2, df, sums):
    resid = r2[...]
    centered = resid - jnp.mean(resid, axis=1, keepdims=True)
    spread = lax.rsqrt(jnp.mean(centered * centered, axis=1, keepdims=True) + norm_eps)
    unit = centered * spread
    result[...] = unit * vec[6:7, :] + vec[7:8, :]
    grad = dy[...].astype(F32)
    e = grad * vec[6:7, :]
    back = spread * (
        e - jnp.mean(e, axis=1, keepdims=True) - unit * jnp.mean(e * unit, axis=1, keepdims=True)
    )
    dr2[...] = back
    df[...] = back.astype(BF16)

    @pl.when(pl.program_id(0) == 0)
    def _():
        sums[...] = jnp.zeros(sums.shape, F32)

    sums[3:4, :] += jnp.sum(back, axis=0, keepdims=True)
    sums[6:7, :] += jnp.sum(grad * unit, axis=0, keepdims=True)
    sums[7:8, :] += jnp.sum(grad, axis=0, keepdims=True)


def second_norm(r2, out_grad, vec):
    tokens, width = r2.shape
    tile = 256
    rows = pl.BlockSpec((tile, width), lambda i: (i, 0))
    top = pl.BlockSpec((8, width), lambda i: (0, 0))
    return pl.pallas_call(
        second_norm_kernel,
        grid=(tokens // tile,),
        out_shape=[
            jax.ShapeDtypeStruct((tokens, width), F32),
            jax.ShapeDtypeStruct((tokens, width), F32),
            jax.ShapeDtypeStruct((tokens, width), BF16),
            jax.ShapeDtypeStruct((8, width), F32),
        ],
        in_specs=[rows, rows, top],
        out_specs=[rows, rows, rows, top],
        compiler_params=pltpu.CompilerParams(vmem_limit_bytes=VMEM_BYTES),
        name="second_norm",
    )(r2, out_grad, vec)


class Reduce(Travel):
    def __init__(self, grid, sems, bufs, other, product, out, cols):
        self.grid, self.sems, self.other, self.product, self.out, self.cols = grid, sems, other, product, out, cols
        self.sum, self.in2a, self.in2b, self.in3a, self.in3b, self.in4 = bufs
        self.half = self.sum.shape[2] // 2
        self.rows = self.sum.shape[2] // grid.nz
        self.sent = []

    def start(self):
        g = self.grid

        def store(y, x, cols, value):
            self.other[y, x, :, cols] = value.astype(BF16)

        self.product(g.off("c", 1), store)
        self.go([self.sems.remote(lambda: (self.other, self.sum, g.peer("c", 1)))])
        self.first = self.sent.pop()

    def freed(self):
        self.first().wait_send()
        self.first = None

    def second(self):
        g = self.grid
        self.landed()

        def add(y, x, cols, value):
            self.sum[y, x, :, cols] = (self.sum[y, x, :, cols].astype(F32) + value).astype(BF16)

        self.product(g.c, add)
        lo, hi = pl.ds(0, self.half), pl.ds(self.half, self.half)
        self.go(
            [
                self.sems.remote(
                    lambda k=k: (self.sum.at[g.off("y", k), :, lo], self.in2a.at[k - 1], g.peer("y", k))
                )
                for k in range(1, g.ny)
            ]
            + [
                self.sems.remote(
                    lambda k=k: (self.sum.at[:, g.off("x", k), hi], self.in2b.at[k - 1], g.peer("x", k))
                )
                for k in range(1, g.nx)
            ]
        )

    def third(self):
        g = self.grid
        self.landed()
        lo, hi = pl.ds(0, self.half), pl.ds(self.half, self.half)
        for x in range(g.nx):
            add_into(self.sum.at[g.y, x, lo], [self.in2a.at[k, x] for k in range(g.ny - 1)])
        for y in range(g.ny):
            add_into(self.sum.at[y, g.x, hi], [self.in2b.at[k, y] for k in range(g.nx - 1)])
        self.go(
            [
                self.sems.remote(
                    lambda k=k: (self.sum.at[g.y, g.off("x", k), lo], self.in3a.at[k - 1], g.peer("x", k))
                )
                for k in range(1, g.nx)
            ]
            + [
                self.sems.remote(
                    lambda k=k: (self.sum.at[g.off("y", k), g.x, hi], self.in3b.at[k - 1], g.peer("y", k))
                )
                for k in range(1, g.ny)
            ]
        )

    def fourth(self):
        g = self.grid
        self.landed()
        lo, hi = pl.ds(0, self.half), pl.ds(self.half, self.half)
        add_into(self.sum.at[g.y, g.x, lo], [self.in3a.at[k] for k in range(g.nx - 1)])
        add_into(self.sum.at[g.y, g.x, hi], [self.in3b.at[k] for k in range(g.ny - 1)])

        def part(k):
            return self.sum.at[g.y, g.x, block_rows(g.off("z", k), self.rows)]

        self.go(
            [self.sems.remote(lambda k=k: (part(k), self.in4.at[k - 1], g.peer("z", k))) for k in range(1, g.nz)]
        )

    def finish(self):
        g = self.grid
        self.landed()
        total = self.sum[g.y, g.x, block_rows(g.z, self.rows), :].astype(F32)
        for k in range(g.nz - 1):
            total += self.in4[k].astype(F32)
        self.out[:, self.cols] = total


def add_into(dst, srcs):
    total = dst[...].astype(F32)
    for src in srcs:
        total += src[...].astype(F32)
    dst[...] = total.astype(dst.dtype)


def reduce_bufs(grid, rows, width, count):
    group, half = rows * grid.nz, rows * grid.nz // 2
    ny, nx = grid.ny, grid.nx
    return [
        pltpu.VMEM((count, *shape, width), BF16)
        for shape in (
            (ny, nx, group),
            (ny - 1, nx, half),
            (nx - 1, ny, half),
            (nx - 1, half),
            (ny - 1, half),
            (grid.nz - 1, rows),
        )
    ]


class Line:
    STAGES = {3: "third", 4: "fourth", 5: "finish"}

    def __init__(self, plan):
        self.jobs, self.plan, self.pumps, self.stage = [], plan, 0, []

    def start(self, job):
        self.jobs.append(job)
        self.stage.append(3)
        job.start()

    def step(self, k):
        getattr(self.jobs[k], self.STAGES[self.stage[k]])()
        self.stage[k] += 1

    def pump(self):
        if self.pumps < len(self.plan):
            for k, stage in self.plan[self.pumps]:
                assert self.stage[k] == stage
                self.step(k)
        self.pumps += 1

    def drain(self):
        for at in range(len(self.jobs) + 3):
            for lag, stage in ((2, 5), (1, 4), (0, 3)):
                k = at - lag
                if 0 <= k < len(self.jobs) and self.stage[k] == stage:
                    self.step(k)
        for job in self.jobs:
            job.drain()
            if job.first is not None:
                job.freed()


BWD_TILE = 512


def backward_kernel(
    grid,
    ctx_len,
    vec,
    sums_in,
    logs,
    dr2,
    df_in,
    hid_in,
    slope_in,
    ub_in,
    n1_in,
    ctx_in,
    qkv_in,
    hin_in,
    wq_in,
    wo_in,
    wi_in,
    wb_in,
    grad_input,
    grad_qkv,
    grad_out,
    grad_in,
    grad_back,
    grad_small,
    send,
    recv,
    move_sems,
    pool,
    du,
    n1,
    sums,
    bias_sum,
    other_wide,
    other_back,
    other_small,
    *bufs,
):
    tokens, width = du.shape
    hidden = bias_sum.shape[1]
    slots = tokens // SLOT
    blocks = hidden // width
    tile = BWD_TILE
    grid.here()
    moves = Locals(move_sems)
    sems = Sems(send, recv)
    line = Line(BWD_PLAN)

    def load(src, block):
        return moves.start(lambda: (src(), pool.at[block]))

    def columns(ref, j):
        return lambda: ref.at[:, pl.ds(j * width, width)]

    def weight_columns(ref, j):
        return lambda: ref.at[:, pl.ds(j * width, width)]

    hid, df, ub = [0, 1, 2, 3], 4, 5
    loads = [load(lambda: df_in, df)]
    loads += [load(columns(hid_in, j), hid[j]) for j in range(blocks)]
    du_copy = moves.start(lambda: (dr2, du))
    greet(grid)
    ff_blocks = [(6, 7, 8), (0, 1, 2)]
    dz_blocks = [3, 9]

    def load_ff(j):
        back, slope, inner = ff_blocks[j % 2]
        return [
            load(lambda: wb_in.at[pl.ds(j * width, width)], back),
            load(columns(slope_in, j), slope),
            load(weight_columns(wi_in, j), inner),
        ]

    ff_loads = {0: load_ff(0)}
    ub_load = load(lambda: ub_in, ub)
    norm_rows = n1.shape[1]

    def load_n1(i):
        return moves.start(lambda: (n1_in.at[pl.ds(i * norm_rows, norm_rows)], n1.at[i % 2]))

    n1_loads = [load_n1(0), load_n1(1)]
    sums[...] = sums_in[...]
    bias_sum[...] = jnp.zeros(bias_sum.shape, F32)

    places = [(y, x) for y in range(grid.ny) for x in range(grid.nx)]
    group = width // (len(places) * grid.nc)

    def token_product(lhs, rhs, wide):
        def product(c, take):
            @pl.loop(0, wide // tile, unroll=True)
            def _(n):
                cols = block_rows(n, tile)
                left = jnp.concatenate(
                    [pool[lhs, :, block_rows((y * grid.nx + x) * grid.nc + c, group)] for y, x in places], axis=1
                )
                value = mm(left, rhs(cols), TN)
                for i, (y, x) in enumerate(places):
                    take(y, x, cols, value[i * group : (i + 1) * group])

        return product

    def back_product(k, wide):
        def product(c, take):
            rows = width // grid.nc
            left = jnp.concatenate([pool[hid[i], :, block_rows(c, rows)] for i in range(len(places))], axis=1)
            value = mm(left, pool[df, :, k * wide : (k + 1) * wide], TN)
            for i, (y, x) in enumerate(places):
                take(y, x, slice(None), value[i * rows : (i + 1) * rows])

        return product

    bufs_back, bufs_wide, bufs_half, bufs_small = [bufs[6 * i : 6 * i + 6] for i in range(4)]
    back_wide = width // blocks
    back_jobs = [
        Reduce(
            grid,
            sems,
            [b.at[k] for b in bufs_back],
            other_back.at[k % 2],
            back_product(k, back_wide),
            grad_back,
            pl.ds(k * back_wide, back_wide),
        )
        for k in range(blocks)
    ]
    wide_jobs = 0

    def wide_job(lhs, rhs, out, at):
        nonlocal wide_jobs
        k = wide_jobs
        wide_jobs += 1
        return Reduce(
            grid,
            sems,
            [b.at[k] for b in bufs_wide],
            other_wide.at[k % 2],
            token_product(lhs, lambda cols: pool[rhs, :, cols], width),
            out,
            pl.ds(at, width),
        )

    for copy in loads:
        moves.wait(copy)
    line.start(back_jobs[0])
    line.start(back_jobs[1])
    for k in range(blocks):
        back_jobs[k].second()
        if k + 2 < blocks:
            back_jobs[k].freed()
            line.start(back_jobs[k + 2])
        line.pump()

    in_jobs = []
    moves.wait(ub_load)
    moves.wait(du_copy)
    for j in range(blocks):
        back, slope, inner = ff_blocks[j % 2]
        dz = dz_blocks[j % 2]
        for copy in ff_loads.pop(j):
            moves.wait(copy)
        if j + 1 < blocks:
            ff_loads[j + 1] = load_ff(j + 1)

        for n in range(width // tile):
            cols = pl.ds(n * tile, tile)
            at = slice(j * width + n * tile, j * width + (n + 1) * tile)

            @pl.loop(0, tokens // tile, unroll=True)
            def _(t):
                rows = block_rows(t, tile)
                grad = mm(pool[df, rows, :], pool[back, cols, :], NT) * pool[slope, rows, cols].astype(F32)
                bias_sum[:, at] += jnp.sum(grad, axis=0, keepdims=True)
                pool[dz, rows, cols] = grad.astype(BF16)

            if n == 0:
                line.pump()

        job = wide_job(ub, dz, grad_in, j * width)
        if j >= 2:
            in_jobs[j - 2].freed()
        line.start(job)
        in_jobs.append(job)
        line.pump()
        for n in range(tokens // tile):
            rows = pl.ds(n * tile, tile)

            @pl.loop(0, width // tile, unroll=True)
            def _(t):
                cols = block_rows(t, tile)
                du[rows, cols] += mm(pool[dz, rows, :], pool[inner, cols, :], NT)

            if n == 0:
                line.pump()

        job.second()
        line.pump()

    da, out_weight, ctx, dctx = 4, 6, 7, 2
    q, k, v = 0, 8, 1
    dq, dk, dv = 3, 9, 5
    hin, wq = 4, (6, 7, 10)
    out_load = load(lambda: wo_in, out_weight)
    ctx_load = load(lambda: ctx_in, ctx)
    qkv_loads = [load(columns(qkv_in, i), block) for i, block in enumerate((q, k, v))]
    for n in range(tokens // norm_rows):
        moves.wait(n1_loads.pop(0))

        @pl.loop(0, norm_rows // 128)
        def _(i):
            rows = block_rows(n * (norm_rows // 128) + i, 128)
            held = n1[n % 2, block_rows(i, 128), :]
            unit, grad = held[:, :width], du[rows, :]
            e = grad * vec[4:5, :]
            back = held[:, width : width + 1] * (
                e - jnp.mean(e, axis=1, keepdims=True) - unit * jnp.mean(e * unit, axis=1, keepdims=True)
            )
            sums[4:5, :] += jnp.sum(grad * unit, axis=0, keepdims=True)
            sums[5:6, :] += jnp.sum(grad, axis=0, keepdims=True)
            sums[2:3, :] += jnp.sum(back, axis=0, keepdims=True)
            du[rows, :] = back
            pool[da, rows, :] = back.astype(BF16)

        if (n + 2) * norm_rows < tokens:
            n1_loads.append(load_n1(n + 2))

    line.pump()
    moves.wait(out_load)
    moves.wait(ctx_load)
    out_job = wide_job(ctx, da, grad_out, 0)
    in_jobs[-2].freed()
    line.start(out_job)

    @pl.loop(0, (tokens // tile) * (width // tile), unroll=2)
    def _(t):
        rows, cols = block_rows(t % (tokens // tile), tile), block_rows(t // (tokens // tile), tile)
        pool[dctx, rows, cols] = mm(pool[da, rows, :], pool[out_weight, cols, :], NT).astype(BF16)

    out_job.second()
    line.pump()
    hin_load = load(lambda: hin_in, hin)
    wq_loads = [load(weight_columns(wq_in, i), block) for i, block in enumerate(wq)]
    for copy in qkv_loads:
        moves.wait(copy)
    first = grid.z * slots
    pairs = width // (2 * HEAD_DIM)
    key_at = lax.broadcasted_iota(jnp.int32, (SLOT, 1), 0)
    lane = lax.broadcasted_iota(jnp.int32, (1, LANES), 1)
    scale = 1.0 / math.sqrt(HEAD_DIM)

    def attend(side):
        steps = slots * pairs // 2

        @pl.loop(0, steps)
        def _(i):
            s = i // (pairs // 2)
            p = i % (pairs // 2) + side * (pairs // 2)
            rows = block_rows(s, SLOT)
            at = block_rows(p, 2 * HEAD_DIM)
            off = jnp.where(key_at < ctx_len[0, first + s] + BLOCK, 0.0, -1e30)
            extra = jnp.where(lane % LOG_LANES == 0, off, -1.0).astype(BF16)
            q2, k2, v2, c2 = pool[q, rows, at], pool[k, rows, at], pool[v, rows, at], pool[dctx, rows, at]
            keys = jnp.concatenate([k2, extra], axis=1)
            sum_q = sum_k = sum_v = None
            for h in range(2):
                mine = head_lanes(h)
                qh = only(mine, q2) * jnp.asarray(scale, BF16)
                ch = only(mine, c2)
                log = only(lane // LOG_LANES == 2 * p + h, logs[rows, :])
                prob = jnp.exp(mm(keys, jnp.concatenate([qh, log], axis=1), NT))
                dprob = mm(v2, ch, NT)
                dot = jnp.sum(prob * dprob, axis=0, keepdims=True)
                dscore = (prob * (dprob - dot)).astype(BF16)
                add_v = mm(prob.astype(BF16), ch, NN)
                add_k = mm(dscore, qh, NN)
                add_q = mm(dscore, only(mine, k2), TN)
                sum_q = add_q if sum_q is None else sum_q + add_q
                sum_k = add_k if sum_k is None else sum_k + add_k
                sum_v = add_v if sum_v is None else sum_v + add_v
            pool[dq, rows, at] = (sum_q * scale).astype(BF16)
            pool[dk, rows, at] = sum_k.astype(BF16)
            pool[dv, rows, at] = sum_v.astype(BF16)
            for n in range(BWD_ATTEND_PUMPS):

                @pl.when(i == (n + 1) * steps // BWD_ATTEND_PUMPS - 1)
                def _():
                    line.pump()

    half = width // 2
    half_jobs = []

    def half_job(rhs, part, side):
        n = len(half_jobs)
        job = Reduce(
            grid,
            sems,
            [b.at[n] for b in bufs_half],
            other_wide.at[n % 2, :, :, :, pl.ds(0, half)],
            token_product(hin, lambda cols: pool[rhs, :, pl.ds(cols.start + side * half, tile)], half),
            grad_qkv,
            pl.ds(part * width + side * half, half),
        )
        half_jobs.append(job)
        return job

    out_job.freed()
    in_jobs[-1].freed()
    for side in range(2):
        attend(side)
        if side == 0:
            moves.wait(hin_load)
        else:
            sums[0:2, :] = jnp.zeros((2, width), F32)

            @pl.loop(0, tokens // 128)
            def _(i):
                rows = block_rows(i, 128)
                sums[0:1, :] += jnp.sum(pool[dq, rows, :].astype(F32), axis=0, keepdims=True)
                sums[1:2, :] += jnp.sum(pool[dv, rows, :].astype(F32), axis=0, keepdims=True)

            def small_product(c, take):
                for y, x in places:
                    at = (y * grid.nx + x) * grid.nc + c
                    eight = sums[:, block_rows(at, LANES)]
                    rows = []
                    for z in range(grid.nz):
                        rows += [eight, bias_sum[:, block_rows(at * grid.nz + z, LANES)], jnp.zeros((7, LANES), F32)]
                    take(y, x, slice(None), jnp.concatenate(rows, axis=0))

            small = Reduce(
                grid, sems, [b.at[0] for b in bufs_small], other_small, small_product, grad_small, slice(None)
            )
            line.start(small)
            small.second()
        for part, rhs in enumerate((dq, dk, dv)):
            job = half_job(rhs, part, side)
            if len(half_jobs) > 2:
                half_jobs[-3].freed()
            line.start(job)
            if part > 0:
                half_jobs[-2].second()
        half_jobs[-1].second()
        line.pump()

    for copy in wq_loads:
        moves.wait(copy)
    for n in range(tokens // tile):
        rows = pl.ds(n * tile, tile)
        for m in range(width // tile):
            cols = pl.ds(m * tile, tile)
            total = du[rows, cols]
            for block, weight in zip((dq, dk, dv), wq):
                total += mm(pool[block, rows, :], pool[weight, cols, :], NT)
            du[rows, cols] = total
            line.pump()

        moves.start(lambda rows=rows: (du.at[rows], grad_input.at[rows]))
    line.drain()
    moves.drain()


BWD_ATTEND_PUMPS = 4
BWD_PLAN = (
    (),
    (),
    (),
    (),
    ((0, 3),),
    (),
    (),
    ((1, 3),),
    (),
    ((2, 3),),
    (),
    ((3, 3),),
    (),
    ((0, 4),),
    (),
    ((4, 3),),
    (),
    ((1, 4), (0, 5), (2, 4),),
    (),
    (),
    ((5, 3),),
    ((1, 5), (3, 4),),
    ((2, 5), (4, 4), (6, 3),),
    (),
    ((3, 5), (5, 4), (7, 3),),
    ((4, 5),),
    ((5, 5), (6, 4), (7, 4), (8, 3),),
    ((9, 3),),
    ((10, 3),),
    ((6, 5), (8, 4), (11, 3),),
    ((7, 5), (9, 4), (10, 4),),
    ((8, 5), (9, 5), (11, 4), (12, 3),),
    ((10, 5),),
    ((13, 3),),
    ((14, 3), (11, 5),),
    (),
)


def backward(grid, context_len, vec, sums, logs, dr2, df, hid, slope, ub, n1, ctx, qkv, hin, weights):
    tokens, width = ub.shape
    hidden = hid.shape[1]
    blocks = hidden // width
    count = grid.count
    rows = width // count
    jobs = blocks + blocks + 1 + 6 + 1
    out = [
        (tokens, width),
        (rows, 3 * width),
        (rows, width),
        (rows, hidden),
        (hidden // count, width),
        (16, LANES),
    ]
    scratch = [
        pltpu.SemaphoreType.DMA((jobs * grid.copies(),)),
        pltpu.SemaphoreType.DMA((jobs * grid.copies(),)),
        pltpu.SemaphoreType.DMA((64,)),
        pltpu.VMEM((11, tokens, width), BF16),
        pltpu.VMEM((tokens, width), F32),
        pltpu.VMEM((2, 128, width + LANES), F32),
        pltpu.VMEM((8, width), F32),
        pltpu.VMEM((1, hidden), F32),
        pltpu.VMEM((2, grid.ny, grid.nx, grid.nz * rows, width), BF16),
        pltpu.VMEM((2, grid.ny, grid.nx, hidden // count * grid.nz, width // blocks), BF16),
        pltpu.VMEM((grid.ny, grid.nx, 16 * grid.nz, LANES), BF16),
        *reduce_bufs(grid, hidden // count, width // blocks, blocks),
        *reduce_bufs(grid, rows, width, blocks + 1),
        *reduce_bufs(grid, rows, width // 2, 6),
        *reduce_bufs(grid, 16, LANES, 1),
    ]
    return pl.pallas_call(
        functools.partial(backward_kernel, grid),
        out_shape=[jax.ShapeDtypeStruct(o, F32) for o in out],
        in_specs=[IN_SMEM, *[IN_VMEM] * 3, *[ANY] * 13],
        out_specs=[ANY, *[IN_VMEM] * 5],
        scratch_shapes=scratch,
        compiler_params=pltpu.CompilerParams(
            collective_id=2, has_side_effects=True, vmem_limit_bytes=VMEM_BYTES
        ),
        name="backward_pass",
    )(context_len, vec, sums, logs, dr2, df, hid, slope, ub, n1, ctx, qkv, hin, *weights)


def shards(
    grid, inputs, timestep, context_len, out_grad, qkv_weight, out_weight, in_weight, back_weight, vectors, bias_ff
):
    weights = (qkv_weight, out_weight, in_weight, back_weight)
    if not fits(grid, inputs, vectors, bias_ff, in_weight):
        return plain_shards(inputs, timestep, context_len, out_grad, *weights, vectors, bias_ff)
    small = fold_small(grid, vectors, bias_ff)
    *full, vec, hin, qkv, logs, ctx, n1, ub, hid, slope, r2 = forward(
        grid, context_len, inputs, timestep, small, *weights
    )
    full = [f.reshape(-1, f.shape[-1]) for f in full]
    result, dr2, df, sums = second_norm(r2, out_grad, vec)
    grad_input, grad_qkv, grad_out, grad_in, grad_back, grad_small = backward(
        grid, context_len, vec, sums, logs, dr2, df, hid, slope, ub, n1, ctx, qkv, hin, full
    )
    rows = vectors.shape[0]
    mine = lax.dynamic_slice(grad_small, (0, lax.axis_index("seq") * rows), (8, rows))
    return (result, grad_input, grad_qkv, grad_out, grad_in, grad_back, mine.T, grad_small[8])


def fits(grid, inputs, vectors, bias_ff, in_weight):
    tokens, width = inputs.shape
    return (
        tokens == width
        and tokens % SLOT == 0
        and vectors.shape[0] * grid.nz == LANES
        and bias_ff.shape[0] == LANES
        and in_weight.shape[1] % width == 0
        and vectors.shape[0] % 32 == 0
        and width // HEAD_DIM * LOG_LANES <= LANES
        and grid.nc == 2
        and grid.nx > 1
        and grid.ny > 1
        and grid.nz > 1
        and in_weight.shape[1] == grid.ny * grid.nx * width
    )


def specs():
    rows = P(("dp", "seq"), None)
    return dict(
        in_specs=(rows, P("dp", None), P("dp", None), *[rows] * 6, P(("dp", "seq"))),
        out_specs=(*[rows] * 7, P(("dp", "seq"))),
    )


def solution(mesh):
    return jax.shard_map(functools.partial(shards, Grid(mesh)), mesh=mesh, check_vma=False, **specs())
```

```python
import functools
import math

import jax
import jax.numpy as jnp
from jax import lax
from jax.experimental import pallas as pl
from jax.experimental.pallas import tpu as pltpu
from jax.sharding import PartitionSpec as P

HEAD_DIM = 64
SLOT = 512
BLOCK = 25


norm_eps = 1e-05


def norm_forward(resid, gain_vec, shift_vec):
    row_mean = jnp.mean(resid, axis=-1, keepdims=True)
    centered = resid - row_mean
    variance = jnp.mean(centered * centered, axis=-1, keepdims=True)
    inv_std = lax.rsqrt(variance + norm_eps)
    normed = centered * inv_std
    return (normed * gain_vec + shift_vec, normed, inv_std)


def norm_backward(grad_out, normed, inv_std, gain_vec):
    grad_norm = grad_out * gain_vec
    grad_resid = inv_std * (
        grad_norm
        - jnp.mean(grad_norm, axis=-1, keepdims=True)
        - normed * jnp.mean(grad_norm * normed, axis=-1, keepdims=True)
    )
    return (grad_resid, jnp.sum(grad_out * normed, axis=0), jnp.sum(grad_out, axis=0))


def gelu_slope(pre_act):
    return 0.5 * (1.0 + lax.erf(pre_act * math.sqrt(0.5))) + pre_act * jnp.exp(
        -0.5 * pre_act * pre_act
    ) / math.sqrt(2.0 * math.pi)


def slot_scores(queries, key_vecs, live_len):
    inv_root = 1.0 / math.sqrt(HEAD_DIM)
    raw_scores = (
        jnp.einsum("qhd,khd->hqk", queries, key_vecs, preferred_element_type=jnp.float32) * inv_root
    )
    key_valid = jnp.arange(SLOT, dtype=jnp.int32) < live_len
    return jnp.where(key_valid[None, None, :], raw_scores, -1e30)


def slot_forward(parts):
    queries, key_vecs, values, live_len = parts
    masked = slot_scores(queries, key_vecs, live_len)
    row_max = jnp.max(masked, axis=-1, keepdims=True)
    exp_scores = jnp.exp(masked - row_max)
    exp_total = jnp.sum(exp_scores, axis=-1, keepdims=True)
    attn_probs = (exp_scores / exp_total).astype(jnp.bfloat16)
    context = jnp.einsum("hqk,khd->qhd", attn_probs, values, preferred_element_type=jnp.float32)
    return (context.astype(jnp.bfloat16), (row_max + jnp.log(exp_total))[..., 0])


def slot_backward(parts):
    queries, key_vecs, values, live_len, log_total, grad_ctx = parts
    inv_root = 1.0 / math.sqrt(HEAD_DIM)
    masked = slot_scores(queries, key_vecs, live_len)
    attn_exact = jnp.exp(masked - log_total[..., None])
    attn_probs = attn_exact.astype(jnp.bfloat16)
    grad_probs = jnp.einsum("qhd,khd->hqk", grad_ctx, values, preferred_element_type=jnp.float32)
    row_dot = jnp.sum(attn_exact * grad_probs, axis=-1, keepdims=True)
    grad_scores = (attn_exact * (grad_probs - row_dot)).astype(jnp.bfloat16)
    grad_query = (
        jnp.einsum("hqk,khd->qhd", grad_scores, key_vecs, preferred_element_type=jnp.float32)
        * inv_root
    )
    grad_key = (
        jnp.einsum("hqk,qhd->khd", grad_scores, queries, preferred_element_type=jnp.float32)
        * inv_root
    )
    grad_value = jnp.einsum(
        "hqk,qhd->khd", attn_probs, grad_ctx, preferred_element_type=jnp.float32
    )
    return (
        grad_query.astype(jnp.bfloat16),
        grad_key.astype(jnp.bfloat16),
        grad_value.astype(jnp.bfloat16),
    )


def plain_shards(
    inputs,
    timestep,
    context_len,
    out_grad,
    qkv_weight,
    out_weight,
    in_weight,
    back_weight,
    vectors,
    bias_ff,
):
    qkv_full, out_full, in_full, back_full, vec_full, bias_full = (
        lax.all_gather(qkv_weight, ("dp", "seq"), axis=0, tiled=True),
        lax.all_gather(out_weight, ("dp", "seq"), axis=0, tiled=True),
        lax.all_gather(in_weight, ("dp", "seq"), axis=0, tiled=True),
        lax.all_gather(back_weight, ("dp", "seq"), axis=0, tiled=True),
        lax.all_gather(vectors, ("dp", "seq"), axis=0, tiled=True),
        lax.all_gather(bias_ff, ("dp", "seq"), axis=0, tiled=True),
    )
    vec_all = vec_full.astype(jnp.float32)
    bias_all = bias_full.astype(jnp.float32)
    width = inputs.shape[1]
    resid_in = inputs.astype(jnp.float32) + timestep.astype(jnp.float32)
    layer_in = resid_in.astype(jnp.bfloat16)
    qkv_proj = jnp.dot(layer_in, qkv_full, preferred_element_type=jnp.float32)
    queries = (qkv_proj[:, :width] + vec_all[:, 0]).astype(jnp.bfloat16)
    key_vecs = qkv_proj[:, width : 2 * width].astype(jnp.bfloat16)
    values = (qkv_proj[:, 2 * width :] + vec_all[:, 1]).astype(jnp.bfloat16)
    q_heads, k_heads, v_heads = (
        lax.all_to_all(queries, "seq", split_axis=1, concat_axis=0, tiled=True),
        lax.all_to_all(key_vecs, "seq", split_axis=1, concat_axis=0, tiled=True),
        lax.all_to_all(values, "seq", split_axis=1, concat_axis=0, tiled=True),
    )
    slot_count = context_len.shape[1]
    head_width = q_heads.shape[1]
    slot_shape = (slot_count, SLOT, head_width // HEAD_DIM, HEAD_DIM)
    live_lens = context_len[0] + BLOCK
    q_slots = q_heads.reshape(slot_shape)
    k_slots = k_heads.reshape(slot_shape)
    v_slots = v_heads.reshape(slot_shape)
    ctx_slots, log_totals = lax.map(slot_forward, (q_slots, k_slots, v_slots, live_lens))
    ctx_tokens = lax.all_to_all(
        ctx_slots.reshape(slot_count * SLOT, head_width),
        "seq",
        split_axis=0,
        concat_axis=1,
        tiled=True,
    )
    attn_out = jnp.dot(ctx_tokens, out_full, preferred_element_type=jnp.float32) + vec_all[:, 2]
    normed_mid, unit_mid, inv_mid = norm_forward(resid_in + attn_out, vec_all[:, 4], vec_all[:, 5])
    mid_low = normed_mid.astype(jnp.bfloat16)
    pre_act = jnp.dot(mid_low, in_full, preferred_element_type=jnp.float32) + bias_all
    hidden = jax.nn.gelu(pre_act, approximate=False).astype(jnp.bfloat16)
    branch = jnp.dot(hidden, back_full, preferred_element_type=jnp.float32) + vec_all[:, 3]
    result, unit_out, inv_out = norm_forward(normed_mid + branch, vec_all[:, 6], vec_all[:, 7])
    grad_two, gain_out_grad, shift_out_grad = norm_backward(
        out_grad.astype(jnp.float32), unit_out, inv_out, vec_all[:, 6]
    )
    branch_low = grad_two.astype(jnp.bfloat16)
    grad_backw = jnp.einsum("tf,td->fd", hidden, branch_low, preferred_element_type=jnp.float32)
    grad_hidden = jnp.einsum("td,fd->tf", branch_low, back_full, preferred_element_type=jnp.float32)
    grad_pre = grad_hidden * gelu_slope(pre_act)
    bias_grad = jnp.sum(grad_pre, axis=0)
    pre_low = grad_pre.astype(jnp.bfloat16)
    grad_inw = jnp.einsum("td,tf->df", mid_low, pre_low, preferred_element_type=jnp.float32)
    grad_mid = grad_two + jnp.einsum(
        "tf,df->td", pre_low, in_full, preferred_element_type=jnp.float32
    )
    grad_one, gain_mid_grad, shift_mid_grad = norm_backward(
        grad_mid, unit_mid, inv_mid, vec_all[:, 4]
    )
    attn_low = grad_one.astype(jnp.bfloat16)
    grad_outw = jnp.einsum("td,te->de", ctx_tokens, attn_low, preferred_element_type=jnp.float32)
    grad_ctx = jnp.einsum(
        "te,de->td", attn_low, out_full, preferred_element_type=jnp.float32
    ).astype(jnp.bfloat16)
    grad_ctx_heads = lax.all_to_all(grad_ctx, "seq", split_axis=1, concat_axis=0, tiled=True)
    grad_q, grad_k, grad_v = lax.map(
        slot_backward,
        (q_slots, k_slots, v_slots, live_lens, log_totals, grad_ctx_heads.reshape(slot_shape)),
    )
    token_shape = (slot_count * SLOT, head_width)
    grad_q_tok, grad_k_tok, grad_v_tok = (
        lax.all_to_all(grad_q.reshape(token_shape), "seq", split_axis=0, concat_axis=1, tiled=True),
        lax.all_to_all(grad_k.reshape(token_shape), "seq", split_axis=0, concat_axis=1, tiled=True),
        lax.all_to_all(grad_v.reshape(token_shape), "seq", split_axis=0, concat_axis=1, tiled=True),
    )
    grad_proj = jnp.concatenate([grad_q_tok, grad_k_tok, grad_v_tok], axis=1)
    grad_qkvw = jnp.einsum("td,te->de", layer_in, grad_proj, preferred_element_type=jnp.float32)
    grad_input = grad_one + jnp.einsum(
        "te,de->td", grad_proj, qkv_full, preferred_element_type=jnp.float32
    )
    vec_grads = jnp.stack(
        [
            jnp.sum(grad_q_tok.astype(jnp.float32), axis=0),
            jnp.sum(grad_v_tok.astype(jnp.float32), axis=0),
            jnp.sum(grad_one, axis=0),
            jnp.sum(grad_two, axis=0),
            gain_mid_grad,
            shift_mid_grad,
            gain_out_grad,
            shift_out_grad,
        ],
        axis=1,
    )
    share_qkv, share_out, share_in, share_back, share_vec, share_bias = (
        lax.psum_scatter(grad_qkvw, ("dp", "seq"), scatter_dimension=0, tiled=True),
        lax.psum_scatter(grad_outw, ("dp", "seq"), scatter_dimension=0, tiled=True),
        lax.psum_scatter(grad_inw, ("dp", "seq"), scatter_dimension=0, tiled=True),
        lax.psum_scatter(grad_backw, ("dp", "seq"), scatter_dimension=0, tiled=True),
        lax.psum_scatter(vec_grads, ("dp", "seq"), scatter_dimension=0, tiled=True),
        lax.psum_scatter(bias_grad, ("dp", "seq"), scatter_dimension=0, tiled=True),
    )
    return (result, grad_input, share_qkv, share_out, share_in, share_back, share_vec, share_bias)


MESH = pl.DeviceIdType.MESH
LANES = 128
F32 = jnp.float32
BF16 = jnp.bfloat16
NN = (((1,), (0,)), ((), ()))
NT = (((1,), (1,)), ((), ()))
TN = (((0,), (0,)), ((), ()))
ANY = pl.BlockSpec(memory_space=pl.ANY)
IN_VMEM = pl.BlockSpec(memory_space=pltpu.VMEM)
IN_SMEM = pl.BlockSpec(memory_space=pltpu.SMEM)
VMEM_BYTES = 62 << 20


def mm(a, b, dims):
    return lax.dot_general(a, b, dims, preferred_element_type=F32)


class Grid:
    def __init__(self, mesh):
        dp, self.nz = mesh.shape["dp"], mesh.shape["seq"]
        self.nc = 2 if dp % 2 == 0 else 1
        rest = dp // self.nc
        self.nx = max(k for k in range(1, math.isqrt(rest) + 1) if rest % k == 0)
        self.ny = rest // self.nx
        self.count = dp * self.nz
        self.groups = [(y, x, c) for y in range(self.ny) for x in range(self.nx) for c in range(self.nc)]

    def here(self):
        dp = lax.axis_index("dp")
        self.z = lax.axis_index("seq")
        self.c = dp % self.nc
        self.x = (dp // self.nc) % self.nx
        self.y = dp // (self.nc * self.nx)

    def off(self, axis, step):
        return (getattr(self, axis) + step) % getattr(self, "n" + axis)

    def peer(self, axis, step):
        at = {name: getattr(self, name) for name in "yxcz"}
        at[axis] = self.off(axis, step)
        return ((at["y"] * self.nx + at["x"]) * self.nc + at["c"], at["z"])

    def peers(self):
        return [self.peer(axis, step) for axis in "zxyc" for step in range(1, getattr(self, "n" + axis))]

    def copies(self):
        return 2 * (self.nz - 1) + 2 * (self.nx - 1) + 2 * (self.ny - 1) + self.nc - 1

    def sums(self):
        return self.nz - 1 + 2 * (self.nx - 1) + 2 * (self.ny - 1) + self.nc - 1


def greet(grid):
    barrier = pltpu.get_barrier_semaphore()
    peers = grid.peers()
    for peer in peers:
        pl.semaphore_signal(barrier, inc=1, device_id=peer, device_id_type=MESH)
    pl.semaphore_wait(barrier, len(peers))


class Sems:
    def __init__(self, send, recv):
        self.send, self.recv, self.used = send, recv, 0

    def remote(self, ends):
        k = self.used
        self.used += 1

        def copy():
            src, dst, device = ends()
            return pltpu.make_async_remote_copy(
                src_ref=src,
                dst_ref=dst,
                send_sem=self.send.at[k],
                recv_sem=self.recv.at[k],
                device_id=device,
                device_id_type=MESH,
            )

        return copy


class Locals:
    def __init__(self, sems):
        self.sems, self.used, self.open = sems, 0, []

    def start(self, ends):
        k = self.used
        self.used += 1

        def copy():
            src, dst = ends()
            return pltpu.make_async_copy(src, dst, self.sems.at[k])

        copy().start()
        self.open.append(copy)
        return copy

    def wait(self, copy):
        copy().wait()
        self.open.remove(copy)

    def drain(self):
        for copy in self.open:
            copy().wait()
        self.open = []


def block_rows(start, size):
    return pl.ds(pl.multiple_of(start * size, size), size)


class Travel:
    def go(self, copies):
        for copy in copies:
            copy().start()
        self.sent += copies
        self.flying = copies

    def landed(self):
        for copy in self.flying:
            copy().wait_recv()

    def drain(self):
        for copy in self.sent:
            copy().wait_send()
        self.sent = []


class Gather(Travel):
    def __init__(self, grid, sems, moves, shard, full, cols, keep=None, late_z=False):
        self.grid, self.sems, self.moves = grid, sems, moves
        self.shard, self.full, self.cols, self.keep, self.late_z = shard, full, cols, keep, late_z
        self.half = shard.shape[0] // 2
        self.sent = []

    def place(self, half=None, y=None, x=None, z=None):
        g = self.grid
        take = lambda at, size: pl.ds(0, size) if at is None else at
        rows = pl.ds(0, 2 * self.half) if half is None else pl.ds(half * self.half, self.half)
        return self.full.at[take(y, g.ny), take(x, g.nx), g.c, take(z, g.nz), rows, self.cols]

    def to(self, axis, part):
        g = self.grid
        return [
            self.sems.remote(lambda k=k: (part(), part(), g.peer(axis, k)))
            for k in range(1, getattr(g, "n" + axis))
        ]

    def start(self):
        g = self.grid
        src = lambda: self.shard.at[:, self.cols]
        self.own = self.moves.start(lambda: (src(), self.place(y=g.y, x=g.x, z=g.z)))
        if self.late_z:
            self.go(
                [
                    self.sems.remote(
                        lambda k=k, axis=axis, half=half: (
                            self.shard.at[pl.ds(half * self.half, self.half), self.cols],
                            self.place(half, g.y, g.x, g.z),
                            g.peer(axis, k),
                        )
                    )
                    for half, axis in enumerate("xy")
                    for k in range(1, getattr(g, "n" + axis))
                ]
            )
        else:
            self.go(
                [
                    self.sems.remote(lambda k=k: (src(), self.place(y=g.y, x=g.x, z=g.z), g.peer("z", k)))
                    for k in range(1, g.nz)
                ]
            )

    def second(self):
        g = self.grid
        self.landed()
        self.moves.wait(self.own)
        if self.late_z:
            self.go(self.to("z", lambda: self.place(0, y=g.y, z=g.z)) + self.to("z", lambda: self.place(1, x=g.x, z=g.z)))
        else:
            self.go(self.to("x", lambda: self.place(0, g.y, g.x)) + self.to("y", lambda: self.place(1, g.y, g.x)))

    def third(self):
        g = self.grid
        self.landed()
        self.go(self.to("y", lambda: self.place(0, y=g.y)) + self.to("x", lambda: self.place(1, x=g.x)))

    def fourth(self):
        self.landed()
        self.go(self.to("c", self.place))

    def finish(self):
        self.landed()
        if self.keep is not None:
            every = lambda ref: ref.at[:, :, :, :, :, self.cols]
            self.moves.start(lambda: (every(self.full), every(self.keep)))


class Flow:
    STAGES = ("start", "second", "third", "fourth", "finish")

    def __init__(self, jobs, lags):
        steps = [
            (k + sum(lags[:s]), -s, k, name) for k in range(len(jobs)) for s, name in enumerate(self.STAGES)
        ]
        self.jobs, self.steps, self.done = jobs, sorted(steps), 0

    def tick(self):
        if self.done < len(self.steps):
            due = self.steps[self.done][0]
            while self.done < len(self.steps) and self.steps[self.done][0] == due:
                self.step()

    def step(self):
        _, _, k, name = self.steps[self.done]
        getattr(self.jobs[k], name)()
        self.done += 1

    def until(self, job):
        last = max(i for i, (_, _, k, name) in enumerate(self.steps) if name == "finish" and self.jobs[k] is job)
        while self.done <= last:
            self.step()

    def drain(self):
        while self.done < len(self.steps):
            self.step()
        for job in self.jobs:
            job.drain()


def head_lanes(h):
    return lax.broadcasted_iota(jnp.int32, (1, 2 * HEAD_DIM), 1) // HEAD_DIM == h


def only(lanes, block):
    return jnp.where(lanes, block, 0).astype(BF16)


def fold_small(grid, vectors, bias_ff):
    rows = vectors.shape[0]
    tiled = jnp.tile(vectors.T, (1, LANES // rows))
    mine = jnp.arange(LANES) // rows == lax.axis_index("seq")
    tiled = jnp.where(mine[None, :], tiled, 0).astype(BF16)
    return jnp.concatenate([tiled, bias_ff[None, :], jnp.zeros((23, LANES), BF16)], axis=0)


FWD_WIDTH = 512


LOG_LANES = 4


def forward_kernel(
    grid,
    ctx_len,
    x_in,
    temb,
    small,
    wq_in,
    wo_in,
    wi_in,
    wb_in,
    wq_out,
    wo_out,
    wi_out,
    wb_out,
    vec_out,
    hin_out,
    qkv_out,
    logs_out,
    ctx_out,
    n1_out,
    ub_out,
    hid_out,
    slope_out,
    r2_out,
    send,
    recv,
    move_sems,
    x,
    hin,
    qkv,
    ctx,
    n1,
    ub,
    hid,
    slope,
    r2,
    lse,
    logs_parts,
    vec,
    bias_qkv,
    bias_ff,
    small_full,
    wq,
    wo,
    wi,
    wb,
):
    tokens, width = hin.shape
    hidden = hid.shape[1]
    slots = tokens // SLOT
    tile = FWD_WIDTH
    grid.here()
    moves = Locals(move_sems)
    x_copy = moves.start(lambda: (x_in, x))
    greet(grid)
    sems = Sems(send, recv)

    def gather(shard, full, at, wide, keep, late_z=False):
        return Gather(grid, sems, moves, shard, full, pl.ds(at, wide), keep, late_z)

    small_job = gather(small, small_full, 0, LANES, None)
    half = width // 2
    qkv_cols = [part * width + side * half for side in range(2) for part in range(3)]
    qkv_jobs = [gather(wq_in, wq, at, half, wq_out) for at in qkv_cols]
    out_jobs = [gather(wo_in, wo, at, half, wo_out) for at in range(0, width, half)]
    in_jobs = [gather(wi_in, wi, at, width, wi_out) for at in range(0, hidden, width)]
    back_wide = width * width // hidden
    back_jobs = [gather(wb_in, wb, at, back_wide, wb_out) for at in range(0, width, back_wide)]
    for k in FWD_LATE_Z:
        ([*qkv_jobs, *out_jobs, *in_jobs, *back_jobs][k]).late_z = True
    flow = Flow([small_job, *qkv_jobs, *out_jobs, *in_jobs, *back_jobs], FWD_LAGS)
    flow.tick()
    flow.tick()

    moves.wait(x_copy)

    @pl.loop(0, tokens // 128)
    def _(i):
        at = block_rows(i, 128)
        hin[at, :] = (x[at, :].astype(F32) + temb[...].astype(F32)).astype(BF16)

    moves.start(lambda: (hin, hin_out))
    flow.until(small_job)
    for i, (y, xx, c) in enumerate(grid.groups):
        tiles = [small_full[y, xx, c, z, pl.ds(0, 16), :].astype(F32) for z in range(grid.nz)]
        vec[:, i * LANES : (i + 1) * LANES] = sum(t[:8] for t in tiles)
        for z, t in enumerate(tiles):
            at = (i * grid.nz + z) * LANES
            bias_ff[:, at : at + LANES] = t[8:9]
    moves.start(lambda: (vec, vec_out))
    bias_qkv[:, :width] = vec[0:1, :]
    bias_qkv[:, width : 2 * width] = jnp.zeros((1, width), F32)
    bias_qkv[:, 2 * width :] = vec[1:2, :]

    def project(at):
        @pl.loop(0, tokens // tile)
        def _(i):
            rows = block_rows(i, tile)
            w = wq[:, :, :, :, :, pl.ds(at, half)].reshape(width, half)
            qkv[rows, pl.ds(at, half)] = (mm(hin[rows, :], w, NN) + bias_qkv[:, at : at + half]).astype(BF16)

    first = grid.z * slots
    pairs = width // (2 * HEAD_DIM)
    lane = lax.broadcasted_iota(jnp.int32, (1, LANES), 1)
    key_at = lax.broadcasted_iota(jnp.int32, (1, SLOT), 1)

    def attend(side):
        steps = slots * pairs // 2

        @pl.loop(0, steps)
        def _(i):
            s = i // (pairs // 2)
            p = i % (pairs // 2) + side * (pairs // 2)
            rows = block_rows(s, SLOT)
            off = jnp.where(key_at < ctx_len[0, first + s] + BLOCK, 0.0, -1e30)
            at = pl.multiple_of(p * LANES, LANES)
            q2 = qkv[rows, pl.ds(at, LANES)]
            k2 = qkv[rows, pl.ds(at + width, LANES)]
            v2 = qkv[rows, pl.ds(at + 2 * width, LANES)]
            total = None
            logs = lse[rows, :]
            for h in range(2):
                mine = head_lanes(h)
                score = mm(only(mine, q2) * jnp.asarray(1.0 / math.sqrt(HEAD_DIM), BF16), k2, NT) + off
                high = jnp.max(score, axis=1, keepdims=True)
                e = jnp.exp(score - high)
                norm = jnp.sum(e, axis=1, keepdims=True)
                part = mm(e.astype(BF16), only(mine, v2), NN) * (1.0 / norm)
                total = part if total is None else total + part
                logs = jnp.where(lane // LOG_LANES == 2 * p + h, high + jnp.log(norm), logs)
            lse[rows, :] = logs
            ctx[rows, pl.ds(at, LANES)] = total.astype(BF16)
            for k in range(FWD_ATTEND_TICKS):

                @pl.when(i == (k + 1) * steps // FWD_ATTEND_TICKS - 1)
                def _():
                    flow.tick()

    lse[...] = jnp.zeros(lse.shape, F32)
    for side in range(2):
        for part in range(3):
            job = side * 3 + part
            flow.until(qkv_jobs[job])
            project(qkv_cols[job])
        attend(side)
    moves.start(lambda: (qkv, qkv_out))
    moves.start(lambda: (ctx, ctx_out))

    @pl.loop(0, tokens // 128)
    def _(i):
        rows = block_rows(i, 128)
        rest, parts = lse[rows, :], []
        for _ in range(LOG_LANES - 1):
            parts.append(rest.astype(BF16).astype(F32))
            rest = rest - parts[-1]
        value = jnp.ones((128, LANES), F32)
        for n, part in enumerate(parts):
            value = jnp.where(lane % LOG_LANES == n + 1, part, value)
        logs_parts[rows, :] = value.astype(BF16)

    moves.start(lambda: (logs_parts, logs_out))
    for job in out_jobs:
        flow.until(job)

    @pl.loop(0, tokens // 256)
    def _(i):
        rows = block_rows(i, 256)
        attn = mm(ctx[rows, :], wo[...].reshape(width, width), NN) + vec[2:3, :]
        resid = x[rows, :].astype(F32) + temb[...].astype(F32) + attn
        centered = resid - jnp.mean(resid, axis=1, keepdims=True)
        spread = lax.rsqrt(jnp.mean(centered * centered, axis=1, keepdims=True) + norm_eps)
        unit = centered * spread
        n1[rows, :width] = unit
        n1[rows, width:] = jnp.broadcast_to(spread, (256, LANES))
        ub[rows, :] = (unit * vec[4:5, :] + vec[5:6, :]).astype(BF16)

    moves.start(lambda: (n1, n1_out))
    moves.start(lambda: (ub, ub_out))
    kept = [None, None]
    for j, at in enumerate(range(0, hidden, tile)):
        if at % width == 0:
            flow.until(in_jobs[at // width])
        if kept[j % 2] is not None:
            moves.wait(kept[j % 2])

        @pl.loop(0, tokens // tile)
        def _(i):
            rows = block_rows(i, tile)
            w = wi[:, :, :, :, :, pl.ds(at, tile)].reshape(width, tile)
            z = mm(ub[rows, :], w, NN) + bias_ff[:, at : at + tile]
            gate = 0.5 * (1.0 + lax.erf(z * math.sqrt(0.5)))
            hid[rows, pl.ds(at, tile)] = (z * gate).astype(BF16)
            bell = jnp.exp(-0.5 * z * z) * (1.0 / math.sqrt(2.0 * math.pi))
            slope[j % 2, rows, :] = (gate + z * bell).astype(BF16)

        kept[j % 2] = moves.start(lambda j=j, at=at: (slope.at[j % 2], slope_out.at[:, pl.ds(at, tile)]))
        if (at + tile) % width == 0:
            flow.tick()
    moves.start(lambda: (hid, hid_out))
    kept = [None, None]
    for j, job in enumerate(back_jobs):
        flow.until(job)
        if kept[j % 2] is not None:
            moves.wait(kept[j % 2])
        cols = slice(j * back_wide, (j + 1) * back_wide)

        @pl.loop(0, tokens // tile)
        def _(i):
            rows = block_rows(i, tile)
            w = wb[:, :, :, :, :, pl.ds(j * back_wide, back_wide)].reshape(hidden, back_wide)
            f = mm(hid[rows, :], w, NN) + vec[3:4, cols]
            r2[j % 2, rows, :] = n1[rows, cols] * vec[4:5, cols] + vec[5:6, cols] + f

        kept[j % 2] = moves.start(
            lambda j=j: (r2.at[j % 2], r2_out.at[:, pl.ds(j * back_wide, back_wide)])
        )
    flow.drain()
    moves.drain()


FWD_LAGS = (2, 2, 2, 1)
FWD_LATE_Z = ()
FWD_ATTEND_TICKS = 2


def forward(grid, context_len, inputs, timestep, small, qkv_weight, out_weight, in_weight, back_weight):
    tokens, width = inputs.shape
    hidden = in_weight.shape[1]
    weights = (qkv_weight, out_weight, in_weight, back_weight)
    back_wide = width * width // hidden

    def whole(shard):
        return (grid.ny, grid.nx, grid.nc, grid.nz, *shard.shape)

    out = [
        *[(whole(w), BF16) for w in weights],
        ((8, width), F32),
        ((tokens, width), BF16),
        ((tokens, 3 * width), BF16),
        ((tokens, LANES), BF16),
        ((tokens, width), BF16),
        ((tokens, width + LANES), F32),
        ((tokens, width), BF16),
        ((tokens, hidden), BF16),
        ((tokens, hidden), BF16),
        ((tokens, width), F32),
    ]
    jobs = 1 + 6 + 2 + hidden // width + width // back_wide
    scratch = [
        pltpu.SemaphoreType.DMA((jobs * grid.copies(),)),
        pltpu.SemaphoreType.DMA((jobs * grid.copies(),)),
        pltpu.SemaphoreType.DMA((64,)),
        pltpu.VMEM((tokens, width), BF16),
        pltpu.VMEM((tokens, width), BF16),
        pltpu.VMEM((tokens, 3 * width), BF16),
        pltpu.VMEM((tokens, width), BF16),
        pltpu.VMEM((tokens, width + LANES), F32),
        pltpu.VMEM((tokens, width), BF16),
        pltpu.VMEM((tokens, hidden), BF16),
        pltpu.VMEM((2, tokens, FWD_WIDTH), BF16),
        pltpu.VMEM((2, tokens, back_wide), F32),
        pltpu.VMEM((tokens, LANES), F32),
        pltpu.VMEM((tokens, LANES), BF16),
        pltpu.VMEM((8, width), F32),
        pltpu.VMEM((1, 3 * width), F32),
        pltpu.VMEM((1, hidden), F32),
        pltpu.VMEM(whole(small), BF16),
        *[pltpu.VMEM(whole(w), BF16) for w in weights],
    ]
    return pl.pallas_call(
        functools.partial(forward_kernel, grid),
        out_shape=[jax.ShapeDtypeStruct(*o) for o in out],
        in_specs=[IN_SMEM, ANY, IN_VMEM, ANY, ANY, ANY, ANY, ANY],
        out_specs=[ANY] * len(out),
        scratch_shapes=scratch,
        compiler_params=pltpu.CompilerParams(
            collective_id=1, has_side_effects=True, vmem_limit_bytes=VMEM_BYTES
        ),
        name="forward_pass",
    )(context_len, inputs, timestep, small, *weights)


def second_norm_kernel(r2, dy, vec, result, dr2, df, sums):
    resid = r2[...]
    centered = resid - jnp.mean(resid, axis=1, keepdims=True)
    spread = lax.rsqrt(jnp.mean(centered * centered, axis=1, keepdims=True) + norm_eps)
    unit = centered * spread
    result[...] = unit * vec[6:7, :] + vec[7:8, :]
    grad = dy[...].astype(F32)
    e = grad * vec[6:7, :]
    back = spread * (
        e - jnp.mean(e, axis=1, keepdims=True) - unit * jnp.mean(e * unit, axis=1, keepdims=True)
    )
    dr2[...] = back
    df[...] = back.astype(BF16)

    @pl.when(pl.program_id(0) == 0)
    def _():
        sums[...] = jnp.zeros(sums.shape, F32)

    sums[3:4, :] += jnp.sum(back, axis=0, keepdims=True)
    sums[6:7, :] += jnp.sum(grad * unit, axis=0, keepdims=True)
    sums[7:8, :] += jnp.sum(grad, axis=0, keepdims=True)


def second_norm(r2, out_grad, vec):
    tokens, width = r2.shape
    tile = 256
    rows = pl.BlockSpec((tile, width), lambda i: (i, 0))
    top = pl.BlockSpec((8, width), lambda i: (0, 0))
    return pl.pallas_call(
        second_norm_kernel,
        grid=(tokens // tile,),
        out_shape=[
            jax.ShapeDtypeStruct((tokens, width), F32),
            jax.ShapeDtypeStruct((tokens, width), F32),
            jax.ShapeDtypeStruct((tokens, width), BF16),
            jax.ShapeDtypeStruct((8, width), F32),
        ],
        in_specs=[rows, rows, top],
        out_specs=[rows, rows, rows, top],
        compiler_params=pltpu.CompilerParams(vmem_limit_bytes=VMEM_BYTES),
        name="second_norm",
    )(r2, out_grad, vec)


class Reduce:
    def __init__(self, grid, sems, base, bufs, other, product, write):
        self.grid, self.sems, self.base = grid, sems, base
        self.other, self.product, self.write = other, product, write
        self.sum, self.in2a, self.in2b, self.in3a, self.in3b, self.in4 = bufs
        self.half = self.sum.shape[2] // 2
        self.rows = self.sum.shape[2] // grid.nz

    def copies(self, stage):
        g = self.grid
        lo, hi = pl.ds(0, self.half), pl.ds(self.half, self.half)
        ys, xs, zs = range(1, g.ny), range(1, g.nx), range(1, g.nz)
        if stage == 1:
            ends = [(self.other, self.sum, g.peer("c", 1))]
        elif stage == 2:
            ends = [(self.sum.at[g.off("y", k), :, lo], self.in2a.at[k - 1], g.peer("y", k)) for k in ys]
            ends += [(self.sum.at[:, g.off("x", k), hi], self.in2b.at[k - 1], g.peer("x", k)) for k in xs]
        elif stage == 3:
            ends = [(self.sum.at[g.y, g.off("x", k), lo], self.in3a.at[k - 1], g.peer("x", k)) for k in xs]
            ends += [(self.sum.at[g.off("y", k), g.x, hi], self.in3b.at[k - 1], g.peer("y", k)) for k in ys]
        else:
            mine = lambda k: self.sum.at[g.y, g.x, block_rows(g.off("z", k), self.rows)]
            ends = [(mine(k), self.in4.at[k - 1], g.peer("z", k)) for k in zs]
        plane = len(ys) + len(xs)
        base = self.base + (0, 0, 1, 1 + plane, 1 + 2 * plane)[stage]
        return [self.sems(base + i, *e) for i, e in enumerate(ends)]

    def send(self, stage):
        for copy in self.copies(stage):
            copy.start()

    def landed(self, stage):
        for copy in self.copies(stage):
            copy.wait_recv()

    def start(self):
        def store(y, x, cols, value):
            self.other[y, x, :, cols] = value.astype(BF16)

        self.product(self.grid.off("c", 1), store)
        self.send(1)

    def second(self):
        self.landed(1)

        def add(y, x, cols, value):
            self.sum[y, x, :, cols] = (self.sum[y, x, :, cols].astype(F32) + value).astype(BF16)

        self.product(self.grid.c, add)
        self.send(2)

    def third(self):
        g = self.grid
        self.landed(2)
        lo, hi = pl.ds(0, self.half), pl.ds(self.half, self.half)
        for x in range(g.nx):
            add_into(self.sum.at[g.y, x, lo], [self.in2a.at[k, x] for k in range(g.ny - 1)])
        for y in range(g.ny):
            add_into(self.sum.at[y, g.x, hi], [self.in2b.at[k, y] for k in range(g.nx - 1)])
        self.send(3)

    def fourth(self):
        g = self.grid
        self.landed(3)
        lo, hi = pl.ds(0, self.half), pl.ds(self.half, self.half)
        add_into(self.sum.at[g.y, g.x, lo], [self.in3a.at[k] for k in range(g.nx - 1)])
        add_into(self.sum.at[g.y, g.x, hi], [self.in3b.at[k] for k in range(g.ny - 1)])
        self.send(4)

    def finish(self):
        g = self.grid
        self.landed(4)
        total = self.sum[g.y, g.x, block_rows(g.z, self.rows), :].astype(F32)
        for k in range(g.nz - 1):
            total += self.in4[k].astype(F32)
        self.write(total)

    def freed(self):
        for copy in self.copies(1):
            copy.wait_send()

    def drain(self):
        for stage in (2, 3, 4):
            for copy in self.copies(stage):
                copy.wait_send()


def add_into(dst, srcs):
    total = dst[...].astype(F32)
    for src in srcs:
        total += src[...].astype(F32)
    dst[...] = total.astype(dst.dtype)


def reduce_bufs(grid, rows, width, count):
    group, half = rows * grid.nz, rows * grid.nz // 2
    ny, nx = grid.ny, grid.nx
    return [
        pltpu.VMEM((count, *shape, width), BF16)
        for shape in (
            (ny, nx, group),
            (ny - 1, nx, half),
            (nx - 1, ny, half),
            (nx - 1, half),
            (ny - 1, half),
            (grid.nz - 1, rows),
        )
    ]


class Line:
    STAGES = {3: "third", 4: "fourth", 5: "finish"}

    def __init__(self, plan):
        self.jobs, self.plan, self.pumps, self.stage = [], plan, 0, []

    def start(self, job):
        self.jobs.append(job)
        self.stage.append(3)
        job.start()

    def step(self, k):
        getattr(self.jobs[k], self.STAGES[self.stage[k]])()
        self.stage[k] += 1

    def pump(self):
        for k, stage in self.plan[self.pumps] if self.pumps < len(self.plan) else ():
            if self.stage[k] == stage:
                self.step(k)
        self.pumps += 1

    def drain(self):
        for at in range(len(self.jobs) + 3):
            for lag, stage in ((2, 5), (1, 4), (0, 3)):
                k = at - lag
                if 0 <= k < len(self.jobs) and self.stage[k] == stage:
                    self.step(k)
        for job in self.jobs:
            job.drain()


BWD_TILE = 512


def backward_kernel(
    grid,
    ctx_len,
    vec,
    sums_in,
    logs,
    dr2,
    df_in,
    hid_in,
    slope_in,
    ub_in,
    n1_in,
    ctx_in,
    qkv_in,
    hin_in,
    wq_in,
    wo_in,
    wi_in,
    wb_in,
    grad_input,
    grad_qkv,
    grad_out,
    grad_in,
    grad_back,
    grad_small,
    send,
    recv,
    move_sems,
    pool,
    du,
    n1,
    sums,
    bias_sum,
    other_wide,
    other_back,
    other_small,
    *bufs,
):
    tokens, width = du.shape
    hidden = bias_sum.shape[1]
    slots = tokens // SLOT
    blocks = hidden // width
    tile = BWD_TILE
    grid.here()
    moves = Locals(move_sems)
    line = Line(BWD_PLAN)

    def sems(k, src, dst, device):
        return pltpu.make_async_remote_copy(
            src_ref=src,
            dst_ref=dst,
            send_sem=send.at[k],
            recv_sem=recv.at[k],
            device_id=device,
            device_id_type=MESH,
        )

    def write_to(out, at, wide):
        def write(total):
            out[:, at : at + wide] = total

        return write


    def load(src, block):
        return moves.start(lambda: (src(), pool.at[block]))

    def columns(ref, j):
        return lambda: ref.at[:, pl.ds(j * width, width)]

    hid, df, ub = [0, 1, 2, 3], 4, 5
    ff_blocks = [(6, 7, 8), (10, 1, 2)]
    dz_blocks = [9, 3]

    def load_back(j):
        return load(lambda: wb_in.at[pl.ds(j * width, width)], ff_blocks[j % 2][0])

    def load_slope(j):
        return load(columns(slope_in, j), ff_blocks[j % 2][1])

    def load_inner(j):
        return load(columns(wi_in, j), ff_blocks[j % 2][2])

    first_loads = [load(lambda: df_in, df), load_back(0), load_slope(0)]
    hid_loads = [load(columns(hid_in, j), hid[j]) for j in range(blocks)]
    inner_load = load_inner(0)
    du_copy = moves.start(lambda: (dr2, du))
    greet(grid)
    back_loads = {1: load_back(1)}
    ub_load = load(lambda: ub_in, ub)
    norm_rows = n1.shape[1]

    def load_n1(i):
        return moves.start(lambda: (n1_in.at[pl.ds(i * norm_rows, norm_rows)], n1.at[i % 2]))

    n1_loads = [load_n1(0), load_n1(1)]
    sums[...] = sums_in[...]
    bias_sum[...] = jnp.zeros(bias_sum.shape, F32)

    places = [(y, x) for y in range(grid.ny) for x in range(grid.nx)]
    group = width // (len(places) * grid.nc)

    def token_product(lhs, rhs, wide, step):
        def product(c, take):
            left = jnp.concatenate(
                [pool[lhs, :, block_rows((y * grid.nx + x) * grid.nc + c, group)] for y, x in places], axis=1
            )
            for n in range(wide // step):
                cols = pl.ds(n * step, step)
                value = mm(left, rhs(cols), TN)
                for i, (y, x) in enumerate(places):
                    take(y, x, cols, value[i * group : (i + 1) * group])

        return product

    def back_product(k, wide):
        def product(c, take):
            rows = width // grid.nc
            left = jnp.concatenate([pool[hid[i], :, block_rows(c, rows)] for i in range(len(places))], axis=1)
            value = mm(left, pool[df, :, k * wide : (k + 1) * wide], TN)
            for i, (y, x) in enumerate(places):
                take(y, x, slice(None), value[i * rows : (i + 1) * rows])

        return product

    bufs_back, bufs_wide, bufs_pair, bufs_small = [bufs[6 * i : 6 * i + 6] for i in range(4)]
    back_wide = width // blocks
    back_jobs = [
        Reduce(
            grid,
            sems,
            k * grid.sums(),
            [b.at[k] for b in bufs_back],
            other_back.at[k % 2],
            back_product(k, back_wide),
            write_to(grad_back, k * back_wide, back_wide),
        )
        for k in range(blocks)
    ]
    wide_jobs = 0

    def wide_job(lhs, rhs, out, at):
        nonlocal wide_jobs
        k = wide_jobs
        wide_jobs += 1
        return Reduce(
            grid,
            sems,
            (blocks + k) * grid.sums(),
            [b.at[k] for b in bufs_wide],
            other_wide.at[k % 2],
            token_product(lhs, lambda cols: pool[rhs, :, cols], width, tile),
            write_to(out, at, width),
        )

    def slope_product(j, n):
        back, slope, _ = ff_blocks[j % 2]
        cols = pl.ds(n * tile, tile)
        at = slice(j * width + n * tile, j * width + (n + 1) * tile)

        @pl.loop(0, tokens // tile, unroll=True)
        def _(t):
            rows = block_rows(t, tile)
            grad = mm(pool[df, rows, :], pool[back, cols, :], NT) * pool[slope, rows, cols].astype(F32)
            bias_sum[:, at] += jnp.sum(grad, axis=0, keepdims=True)
            pool[dz_blocks[j % 2], rows, cols] = grad.astype(BF16)

    def inner_product(j, n):
        inner = ff_blocks[j % 2][2]
        rows = pl.ds(n * tile, tile)

        @pl.loop(0, width // tile, unroll=True)
        def _(t):
            cols = block_rows(t, tile)
            du[rows, cols] += mm(pool[dz_blocks[j % 2], rows, :], pool[inner, cols, :], NT)

    tiles = range(width // tile)
    for copy in first_loads:
        moves.wait(copy)
    for n in tiles:
        slope_product(0, n)
    for copy in hid_loads:
        moves.wait(copy)
    line.start(back_jobs[0])
    line.start(back_jobs[1])
    moves.wait(inner_load)
    moves.wait(du_copy)
    inner_product(0, 0)
    back_jobs[0].second()
    back_jobs[0].freed()
    line.start(back_jobs[2])
    back_jobs[1].second()
    back_jobs[1].freed()
    line.start(back_jobs[3])
    line.pump()
    moves.wait(ub_load)
    in_jobs = [wide_job(ub, dz_blocks[j % 2], grad_in, j * width) for j in range(blocks)]
    line.start(in_jobs[0])
    back_jobs[2].second()
    back_jobs[3].second()
    line.pump()
    ff_loads = {1: [load_slope(1), load_inner(1)]}
    for n in tiles[1:]:
        inner_product(0, n)
        line.pump()
    for j in range(1, blocks):
        if j + 1 < blocks:
            back_loads[j + 1] = load_back(j + 1)
            ff_loads[j + 1] = [load_slope(j + 1), load_inner(j + 1)]
        for copy in [back_loads.pop(j), *ff_loads.pop(j)]:
            moves.wait(copy)
        for n in tiles:
            slope_product(j, n)
            if n == 0:
                in_jobs[j - 1].second()
                line.pump()
        if j >= 2:
            in_jobs[j - 2].freed()
        line.start(in_jobs[j])
        line.pump()
        for n in tiles:
            inner_product(j, n)
            line.pump()

    da, out_weight, ctx, dctx = 4, 6, 7, 2
    q, k, v = 0, 8, 1
    dq, dk, dv = 3, 9, 5
    hin, wq = 4, (6, 7, 10)
    out_load = load(lambda: wo_in, out_weight)
    ctx_load = load(lambda: ctx_in, ctx)
    qkv_loads = [load(columns(qkv_in, i), block) for i, block in enumerate((q, k, v))]
    for n in range(tokens // norm_rows):
        moves.wait(n1_loads.pop(0))

        @pl.loop(0, norm_rows // 128)
        def _(i):
            rows = block_rows(n * (norm_rows // 128) + i, 128)
            held = n1[n % 2, block_rows(i, 128), :]
            unit, grad = held[:, :width], du[rows, :]
            e = grad * vec[4:5, :]
            back = held[:, width : width + 1] * (
                e - jnp.mean(e, axis=1, keepdims=True) - unit * jnp.mean(e * unit, axis=1, keepdims=True)
            )
            sums[4:5, :] += jnp.sum(grad * unit, axis=0, keepdims=True)
            sums[5:6, :] += jnp.sum(grad, axis=0, keepdims=True)
            sums[2:3, :] += jnp.sum(back, axis=0, keepdims=True)
            du[rows, :] = back
            pool[da, rows, :] = back.astype(BF16)

        if (n + 2) * norm_rows < tokens:
            n1_loads.append(load_n1(n + 2))

    in_jobs[-1].second()
    line.pump()
    moves.wait(out_load)
    moves.wait(ctx_load)
    out_job = wide_job(ctx, da, grad_out, 0)
    in_jobs[-2].freed()
    line.start(out_job)

    @pl.loop(0, (tokens // tile) * (width // tile), unroll=2)
    def _(t):
        rows, cols = block_rows(t % (tokens // tile), tile), block_rows(t // (tokens // tile), tile)
        pool[dctx, rows, cols] = mm(pool[da, rows, :], pool[out_weight, cols, :], NT).astype(BF16)

    line.pump()
    out_job.second()
    line.pump()
    hin_load = load(lambda: hin_in, hin)
    wq_loads = [load(columns(wq_in, i), block) for i, block in enumerate(wq)]
    for copy in qkv_loads:
        moves.wait(copy)
    first = grid.z * slots
    pairs = width // (2 * HEAD_DIM)
    key_at = lax.broadcasted_iota(jnp.int32, (SLOT, 1), 0)
    lane = lax.broadcasted_iota(jnp.int32, (1, LANES), 1)
    scale = 1.0 / math.sqrt(HEAD_DIM)

    def pair_job(p):
        at = block_rows(p, LANES)

        def rhs(_):
            return jnp.concatenate([pool[block, :, at] for block in (dq, dk, dv)], axis=1)

        def write(total):
            for i in range(3):
                grad_qkv[:, pl.ds(pl.multiple_of(i * width + p * LANES, LANES), LANES)] = total[
                    :, i * LANES : (i + 1) * LANES
                ]

        return Reduce(
            grid,
            sems,
            (2 * blocks + 1 + p) * grid.sums(),
            [b.at[p] for b in bufs_pair],
            other_wide.at[p % 2, :, :, :, pl.ds(0, 3 * LANES)],
            token_product(hin, rhs, 3 * LANES, 3 * LANES),
            write,
        )

    def follow(p, traced):
        for lag, name in zip(PAIR_LAGS, ("second", "third", "fourth", "finish")):
            if traced:

                @pl.when(p >= lag)
                def _():
                    getattr(pair_job(p - lag), name)()

            elif 0 <= p - lag < pairs:
                getattr(pair_job(p - lag), name)()

    for job in (back_jobs[-2], back_jobs[-1], in_jobs[-1], out_job):
        job.freed()
    moves.wait(hin_load)

    @pl.loop(0, pairs)
    def _(p):
        at = block_rows(p, LANES)

        @pl.loop(0, slots)
        def _(s):
            rows = block_rows(s, SLOT)
            off = jnp.where(key_at < ctx_len[0, first + s] + BLOCK, 0.0, -1e30)
            extra = jnp.where(lane % LOG_LANES == 0, off, -1.0).astype(BF16)
            q2, k2, v2, c2 = pool[q, rows, at], pool[k, rows, at], pool[v, rows, at], pool[dctx, rows, at]
            keys = jnp.concatenate([k2, extra], axis=1)
            sum_q = sum_k = sum_v = None
            for h in range(2):
                mine = head_lanes(h)
                qh = only(mine, q2) * jnp.asarray(scale, BF16)
                ch = only(mine, c2)
                log = only(lane // LOG_LANES == 2 * p + h, logs[rows, :])
                prob = jnp.exp(mm(keys, jnp.concatenate([qh, log], axis=1), NT))
                dprob = mm(v2, ch, NT)
                dot = jnp.sum(prob * dprob, axis=0, keepdims=True)
                dscore = (prob * (dprob - dot)).astype(BF16)
                add_v = mm(prob.astype(BF16), ch, NN)
                add_k = mm(dscore, qh, NN)
                add_q = mm(dscore, only(mine, k2), TN)
                sum_q = add_q if sum_q is None else sum_q + add_q
                sum_k = add_k if sum_k is None else sum_k + add_k
                sum_v = add_v if sum_v is None else sum_v + add_v
            pool[dq, rows, at] = (sum_q * scale).astype(BF16)
            pool[dk, rows, at] = sum_k.astype(BF16)
            pool[dv, rows, at] = sum_v.astype(BF16)

        for row, block in enumerate((dq, dv)):
            sums[row : row + 1, at] = jnp.sum(pool[block, :, at].astype(F32), axis=0, keepdims=True)

        @pl.when(p >= 2)
        def _():
            pair_job(p - 2).freed()

        pair_job(p).start()
        follow(p, True)
        for n in range(pairs):

            @pl.when(p == n)
            def _():
                line.pump()

    def small_product(c, take):
        for y, x in places:
            at = (y * grid.nx + x) * grid.nc + c
            eight = sums[:, block_rows(at, LANES)]
            rows = []
            for z in range(grid.nz):
                rows += [eight, bias_sum[:, block_rows(at * grid.nz + z, LANES)], jnp.zeros((7, LANES), F32)]
            take(y, x, slice(None), jnp.concatenate(rows, axis=0))

    small = Reduce(
        grid,
        sems,
        (2 * blocks + 1 + pairs) * grid.sums(),
        [b.at[0] for b in bufs_small],
        other_small,
        small_product,
        write_to(grad_small, 0, LANES),
    )
    small.start()
    follow(pairs, False)
    small.second()
    for copy in wq_loads:
        moves.wait(copy)
    tail = pairs + 1
    for n in range(tokens // tile):
        rows = pl.ds(n * tile, tile)
        for m in range(width // tile):
            cols = pl.ds(m * tile, tile)
            total = du[rows, cols]
            for block, weight in zip((dq, dk, dv), wq):
                total += mm(pool[block, rows, :], pool[weight, cols, :], NT)
            du[rows, cols] = total
            follow(tail, False)
            tail += 1

        moves.start(lambda rows=rows: (du.at[rows], grad_input.at[rows]))
    small.third()
    small.fourth()
    for p in range(tail, pairs + PAIR_LAGS[-1]):
        follow(p, False)
    small.finish()
    for p in range(pairs):
        pair_job(p).drain()
    for job in (pair_job(pairs - 2), pair_job(pairs - 1), small):
        job.freed()
    small.drain()
    line.drain()
    moves.drain()


PAIR_LAGS = (1, 3, 5, 9)
BWD_PLAN = (
    (),
    (),
    ((0, 3),),
    (),
    ((1, 3),),
    (),
    (),
    ((2, 3),),
    (),
    ((3, 3),),
    (),
    ((0, 4),),
    (),
    ((4, 3),),
    (),
    ((1, 4),),
    ((2, 4), (5, 3), (0, 5),),
    (),
    ((3, 4),),
    ((1, 5), (4, 4), (6, 3),),
    ((2, 5), (7, 3),),
    ((3, 5), (5, 4), (8, 3),),
    ((4, 5), (6, 4),),
    ((7, 4),),
    ((5, 5), (8, 4),),
    ((6, 5),),
)


def backward(grid, context_len, vec, sums, logs, dr2, df, hid, slope, ub, n1, ctx, qkv, hin, weights):
    tokens, width = ub.shape
    hidden = hid.shape[1]
    blocks = hidden // width
    count = grid.count
    rows = width // count
    pairs = width // LANES
    jobs = blocks + blocks + 1 + pairs + 1
    out = [
        (tokens, width),
        (rows, 3 * width),
        (rows, width),
        (rows, hidden),
        (hidden // count, width),
        (16, LANES),
    ]
    scratch = [
        pltpu.SemaphoreType.DMA((jobs * grid.sums(),)),
        pltpu.SemaphoreType.DMA((jobs * grid.sums(),)),
        pltpu.SemaphoreType.DMA((64,)),
        pltpu.VMEM((11, tokens, width), BF16),
        pltpu.VMEM((tokens, width), F32),
        pltpu.VMEM((2, 128, width + LANES), F32),
        pltpu.VMEM((8, width), F32),
        pltpu.VMEM((1, hidden), F32),
        pltpu.VMEM((2, grid.ny, grid.nx, grid.nz * rows, width), BF16),
        pltpu.VMEM((2, grid.ny, grid.nx, hidden // count * grid.nz, width // blocks), BF16),
        pltpu.VMEM((grid.ny, grid.nx, 16 * grid.nz, LANES), BF16),
        *reduce_bufs(grid, hidden // count, width // blocks, blocks),
        *reduce_bufs(grid, rows, width, blocks + 1),
        *reduce_bufs(grid, rows, 3 * LANES, pairs),
        *reduce_bufs(grid, 16, LANES, 1),
    ]
    return pl.pallas_call(
        functools.partial(backward_kernel, grid),
        out_shape=[jax.ShapeDtypeStruct(o, F32) for o in out],
        in_specs=[IN_SMEM, *[IN_VMEM] * 3, *[ANY] * 13],
        out_specs=[ANY, *[IN_VMEM] * 5],
        scratch_shapes=scratch,
        compiler_params=pltpu.CompilerParams(
            collective_id=2, has_side_effects=True, vmem_limit_bytes=VMEM_BYTES
        ),
        name="backward_pass",
    )(context_len, vec, sums, logs, dr2, df, hid, slope, ub, n1, ctx, qkv, hin, *weights)


def outputs_kernel(*refs):
    n = (len(refs) - 3) // 2
    arrays, small, copies, (vec, bias) = refs[:n], refs[n], refs[n + 1 : 2 * n + 1], refs[2 * n + 1 :]
    for src, dst in zip(arrays, copies):
        dst[...] = src[...]
    z = lax.axis_index("seq")
    rows = vec.shape[0]
    mine = [jnp.where(z == k, small[:8, k * rows : (k + 1) * rows], 0.0) for k in range(LANES // rows)]
    vec[...] = sum(mine).T
    bias[...] = small[8:9, :]


def outputs(arrays, small, rows):
    steps = 4
    like = [jax.ShapeDtypeStruct(a.shape, F32) for a in arrays]
    parts = [pl.BlockSpec((a.shape[0] // steps, a.shape[1]), lambda i: (i, 0)) for a in arrays]
    whole = [pl.BlockSpec(shape, lambda i: (0, 0)) for shape in (small.shape, (rows, 8), (1, LANES))]
    return pl.pallas_call(
        outputs_kernel,
        grid=(steps,),
        out_shape=[*like, jax.ShapeDtypeStruct((rows, 8), F32), jax.ShapeDtypeStruct((1, LANES), F32)],
        in_specs=[*parts, whole[0]],
        out_specs=[*parts, *whole[1:]],
        compiler_params=pltpu.CompilerParams(vmem_limit_bytes=VMEM_BYTES),
        name="outputs",
    )(*arrays, small)


def shards(
    grid, inputs, timestep, context_len, out_grad, qkv_weight, out_weight, in_weight, back_weight, vectors, bias_ff
):
    weights = (qkv_weight, out_weight, in_weight, back_weight)
    if not fits(grid, inputs, vectors, bias_ff, in_weight):
        return plain_shards(inputs, timestep, context_len, out_grad, *weights, vectors, bias_ff)
    small = fold_small(grid, vectors, bias_ff)
    *full, vec, hin, qkv, logs, ctx, n1, ub, hid, slope, r2 = forward(
        grid, context_len, inputs, timestep, small, *weights
    )
    full = [f.reshape(-1, f.shape[-1]) for f in full]
    result, dr2, df, sums = second_norm(r2, out_grad, vec)
    *grads, grad_small = backward(
        grid, context_len, vec, sums, logs, dr2, df, hid, slope, ub, n1, ctx, qkv, hin, full
    )
    *grads, vec_share, bias_share = outputs(grads, grad_small, vectors.shape[0])
    return (result, *grads, vec_share, bias_share.reshape(-1))


def fits(grid, inputs, vectors, bias_ff, in_weight):
    tokens, width = inputs.shape
    return (
        tokens == width
        and tokens % SLOT == 0
        and vectors.shape[0] * grid.nz == LANES
        and bias_ff.shape[0] == LANES
        and in_weight.shape[1] % width == 0
        and vectors.shape[0] % 32 == 0
        and width // HEAD_DIM * LOG_LANES <= LANES
        and grid.nc == 2
        and grid.nx > 1
        and grid.ny > 1
        and grid.nz > 1
        and in_weight.shape[1] == grid.ny * grid.nx * width
    )


def specs():
    rows = P(("dp", "seq"), None)
    return dict(
        in_specs=(rows, P("dp", None), P("dp", None), *[rows] * 6, P(("dp", "seq"))),
        out_specs=(*[rows] * 7, P(("dp", "seq"))),
    )


def solution(mesh):
    return jax.shard_map(functools.partial(shards, Grid(mesh)), mesh=mesh, check_vma=False, **specs())
```

```python
import functools
import math

import jax
import jax.numpy as jnp
from jax import lax
from jax.experimental import pallas as pl
from jax.experimental.pallas import tpu as pltpu
from jax.sharding import PartitionSpec as P

HEAD_DIM = 64
SLOT = 512
BLOCK = 25


norm_eps = 1e-05


def norm_forward(resid, gain_vec, shift_vec):
    row_mean = jnp.mean(resid, axis=-1, keepdims=True)
    centered = resid - row_mean
    variance = jnp.mean(centered * centered, axis=-1, keepdims=True)
    inv_std = lax.rsqrt(variance + norm_eps)
    normed = centered * inv_std
    return (normed * gain_vec + shift_vec, normed, inv_std)


def norm_backward(grad_out, normed, inv_std, gain_vec):
    grad_norm = grad_out * gain_vec
    grad_resid = inv_std * (
        grad_norm
        - jnp.mean(grad_norm, axis=-1, keepdims=True)
        - normed * jnp.mean(grad_norm * normed, axis=-1, keepdims=True)
    )
    return (grad_resid, jnp.sum(grad_out * normed, axis=0), jnp.sum(grad_out, axis=0))


def gelu_slope(pre_act):
    return 0.5 * (1.0 + lax.erf(pre_act * math.sqrt(0.5))) + pre_act * jnp.exp(
        -0.5 * pre_act * pre_act
    ) / math.sqrt(2.0 * math.pi)


def slot_scores(queries, key_vecs, live_len):
    inv_root = 1.0 / math.sqrt(HEAD_DIM)
    raw_scores = (
        jnp.einsum("qhd,khd->hqk", queries, key_vecs, preferred_element_type=jnp.float32) * inv_root
    )
    key_valid = jnp.arange(SLOT, dtype=jnp.int32) < live_len
    return jnp.where(key_valid[None, None, :], raw_scores, -1e30)


def slot_forward(parts):
    queries, key_vecs, values, live_len = parts
    masked = slot_scores(queries, key_vecs, live_len)
    row_max = jnp.max(masked, axis=-1, keepdims=True)
    exp_scores = jnp.exp(masked - row_max)
    exp_total = jnp.sum(exp_scores, axis=-1, keepdims=True)
    attn_probs = (exp_scores / exp_total).astype(jnp.bfloat16)
    context = jnp.einsum("hqk,khd->qhd", attn_probs, values, preferred_element_type=jnp.float32)
    return (context.astype(jnp.bfloat16), (row_max + jnp.log(exp_total))[..., 0])


def slot_backward(parts):
    queries, key_vecs, values, live_len, log_total, grad_ctx = parts
    inv_root = 1.0 / math.sqrt(HEAD_DIM)
    masked = slot_scores(queries, key_vecs, live_len)
    attn_exact = jnp.exp(masked - log_total[..., None])
    attn_probs = attn_exact.astype(jnp.bfloat16)
    grad_probs = jnp.einsum("qhd,khd->hqk", grad_ctx, values, preferred_element_type=jnp.float32)
    row_dot = jnp.sum(attn_exact * grad_probs, axis=-1, keepdims=True)
    grad_scores = (attn_exact * (grad_probs - row_dot)).astype(jnp.bfloat16)
    grad_query = (
        jnp.einsum("hqk,khd->qhd", grad_scores, key_vecs, preferred_element_type=jnp.float32)
        * inv_root
    )
    grad_key = (
        jnp.einsum("hqk,qhd->khd", grad_scores, queries, preferred_element_type=jnp.float32)
        * inv_root
    )
    grad_value = jnp.einsum(
        "hqk,qhd->khd", attn_probs, grad_ctx, preferred_element_type=jnp.float32
    )
    return (
        grad_query.astype(jnp.bfloat16),
        grad_key.astype(jnp.bfloat16),
        grad_value.astype(jnp.bfloat16),
    )


def plain_shards(
    inputs,
    timestep,
    context_len,
    out_grad,
    qkv_weight,
    out_weight,
    in_weight,
    back_weight,
    vectors,
    bias_ff,
):
    qkv_full, out_full, in_full, back_full, vec_full, bias_full = (
        lax.all_gather(qkv_weight, ("dp", "seq"), axis=0, tiled=True),
        lax.all_gather(out_weight, ("dp", "seq"), axis=0, tiled=True),
        lax.all_gather(in_weight, ("dp", "seq"), axis=0, tiled=True),
        lax.all_gather(back_weight, ("dp", "seq"), axis=0, tiled=True),
        lax.all_gather(vectors, ("dp", "seq"), axis=0, tiled=True),
        lax.all_gather(bias_ff, ("dp", "seq"), axis=0, tiled=True),
    )
    vec_all = vec_full.astype(jnp.float32)
    bias_all = bias_full.astype(jnp.float32)
    width = inputs.shape[1]
    resid_in = inputs.astype(jnp.float32) + timestep.astype(jnp.float32)
    layer_in = resid_in.astype(jnp.bfloat16)
    qkv_proj = jnp.dot(layer_in, qkv_full, preferred_element_type=jnp.float32)
    queries = (qkv_proj[:, :width] + vec_all[:, 0]).astype(jnp.bfloat16)
    key_vecs = qkv_proj[:, width : 2 * width].astype(jnp.bfloat16)
    values = (qkv_proj[:, 2 * width :] + vec_all[:, 1]).astype(jnp.bfloat16)
    q_heads, k_heads, v_heads = (
        lax.all_to_all(queries, "seq", split_axis=1, concat_axis=0, tiled=True),
        lax.all_to_all(key_vecs, "seq", split_axis=1, concat_axis=0, tiled=True),
        lax.all_to_all(values, "seq", split_axis=1, concat_axis=0, tiled=True),
    )
    slot_count = context_len.shape[1]
    head_width = q_heads.shape[1]
    slot_shape = (slot_count, SLOT, head_width // HEAD_DIM, HEAD_DIM)
    live_lens = context_len[0] + BLOCK
    q_slots = q_heads.reshape(slot_shape)
    k_slots = k_heads.reshape(slot_shape)
    v_slots = v_heads.reshape(slot_shape)
    ctx_slots, log_totals = lax.map(slot_forward, (q_slots, k_slots, v_slots, live_lens))
    ctx_tokens = lax.all_to_all(
        ctx_slots.reshape(slot_count * SLOT, head_width),
        "seq",
        split_axis=0,
        concat_axis=1,
        tiled=True,
    )
    attn_out = jnp.dot(ctx_tokens, out_full, preferred_element_type=jnp.float32) + vec_all[:, 2]
    normed_mid, unit_mid, inv_mid = norm_forward(resid_in + attn_out, vec_all[:, 4], vec_all[:, 5])
    mid_low = normed_mid.astype(jnp.bfloat16)
    pre_act = jnp.dot(mid_low, in_full, preferred_element_type=jnp.float32) + bias_all
    hidden = jax.nn.gelu(pre_act, approximate=False).astype(jnp.bfloat16)
    branch = jnp.dot(hidden, back_full, preferred_element_type=jnp.float32) + vec_all[:, 3]
    result, unit_out, inv_out = norm_forward(normed_mid + branch, vec_all[:, 6], vec_all[:, 7])
    grad_two, gain_out_grad, shift_out_grad = norm_backward(
        out_grad.astype(jnp.float32), unit_out, inv_out, vec_all[:, 6]
    )
    branch_low = grad_two.astype(jnp.bfloat16)
    grad_backw = jnp.einsum("tf,td->fd", hidden, branch_low, preferred_element_type=jnp.float32)
    grad_hidden = jnp.einsum("td,fd->tf", branch_low, back_full, preferred_element_type=jnp.float32)
    grad_pre = grad_hidden * gelu_slope(pre_act)
    bias_grad = jnp.sum(grad_pre, axis=0)
    pre_low = grad_pre.astype(jnp.bfloat16)
    grad_inw = jnp.einsum("td,tf->df", mid_low, pre_low, preferred_element_type=jnp.float32)
    grad_mid = grad_two + jnp.einsum(
        "tf,df->td", pre_low, in_full, preferred_element_type=jnp.float32
    )
    grad_one, gain_mid_grad, shift_mid_grad = norm_backward(
        grad_mid, unit_mid, inv_mid, vec_all[:, 4]
    )
    attn_low = grad_one.astype(jnp.bfloat16)
    grad_outw = jnp.einsum("td,te->de", ctx_tokens, attn_low, preferred_element_type=jnp.float32)
    grad_ctx = jnp.einsum(
        "te,de->td", attn_low, out_full, preferred_element_type=jnp.float32
    ).astype(jnp.bfloat16)
    grad_ctx_heads = lax.all_to_all(grad_ctx, "seq", split_axis=1, concat_axis=0, tiled=True)
    grad_q, grad_k, grad_v = lax.map(
        slot_backward,
        (q_slots, k_slots, v_slots, live_lens, log_totals, grad_ctx_heads.reshape(slot_shape)),
    )
    token_shape = (slot_count * SLOT, head_width)
    grad_q_tok, grad_k_tok, grad_v_tok = (
        lax.all_to_all(grad_q.reshape(token_shape), "seq", split_axis=0, concat_axis=1, tiled=True),
        lax.all_to_all(grad_k.reshape(token_shape), "seq", split_axis=0, concat_axis=1, tiled=True),
        lax.all_to_all(grad_v.reshape(token_shape), "seq", split_axis=0, concat_axis=1, tiled=True),
    )
    grad_proj = jnp.concatenate([grad_q_tok, grad_k_tok, grad_v_tok], axis=1)
    grad_qkvw = jnp.einsum("td,te->de", layer_in, grad_proj, preferred_element_type=jnp.float32)
    grad_input = grad_one + jnp.einsum(
        "te,de->td", grad_proj, qkv_full, preferred_element_type=jnp.float32
    )
    vec_grads = jnp.stack(
        [
            jnp.sum(grad_q_tok.astype(jnp.float32), axis=0),
            jnp.sum(grad_v_tok.astype(jnp.float32), axis=0),
            jnp.sum(grad_one, axis=0),
            jnp.sum(grad_two, axis=0),
            gain_mid_grad,
            shift_mid_grad,
            gain_out_grad,
            shift_out_grad,
        ],
        axis=1,
    )
    share_qkv, share_out, share_in, share_back, share_vec, share_bias = (
        lax.psum_scatter(grad_qkvw, ("dp", "seq"), scatter_dimension=0, tiled=True),
        lax.psum_scatter(grad_outw, ("dp", "seq"), scatter_dimension=0, tiled=True),
        lax.psum_scatter(grad_inw, ("dp", "seq"), scatter_dimension=0, tiled=True),
        lax.psum_scatter(grad_backw, ("dp", "seq"), scatter_dimension=0, tiled=True),
        lax.psum_scatter(vec_grads, ("dp", "seq"), scatter_dimension=0, tiled=True),
        lax.psum_scatter(bias_grad, ("dp", "seq"), scatter_dimension=0, tiled=True),
    )
    return (result, grad_input, share_qkv, share_out, share_in, share_back, share_vec, share_bias)


MESH = pl.DeviceIdType.MESH
LANES = 128
F32 = jnp.float32
BF16 = jnp.bfloat16
NN = (((1,), (0,)), ((), ()))
NT = (((1,), (1,)), ((), ()))
TN = (((0,), (0,)), ((), ()))
ANY = pl.BlockSpec(memory_space=pl.ANY)
IN_VMEM = pl.BlockSpec(memory_space=pltpu.VMEM)
IN_SMEM = pl.BlockSpec(memory_space=pltpu.SMEM)
VMEM_BYTES = 62 << 20


def mm(a, b, dims):
    return lax.dot_general(a, b, dims, preferred_element_type=F32)


class Grid:
    def __init__(self, mesh):
        dp, self.nz = mesh.shape["dp"], mesh.shape["seq"]
        self.nc = 2 if dp % 2 == 0 else 1
        rest = dp // self.nc
        self.nx = max(k for k in range(1, math.isqrt(rest) + 1) if rest % k == 0)
        self.ny = rest // self.nx
        self.count = dp * self.nz
        self.groups = [(y, x, c) for y in range(self.ny) for x in range(self.nx) for c in range(self.nc)]

    def here(self):
        dp = lax.axis_index("dp")
        self.z = lax.axis_index("seq")
        self.c = dp % self.nc
        self.x = (dp // self.nc) % self.nx
        self.y = dp // (self.nc * self.nx)
        self.inner = jnp.logical_or(self.z == 1, self.z == 2)
        self.outer = jnp.logical_not(self.inner)
        self.side = self.z % 2
        self.mate = self.z + 1 - 2 * self.side
        self.across = 2 - self.z // 2
        self.other_pair = 2 * self.across - 2

    def off(self, axis, step):
        return (getattr(self, axis) + step) % getattr(self, "n" + axis)

    def at_z(self, z):
        return ((self.y * self.nx + self.x) * self.nc + self.c, z)

    def peer(self, axis, step):
        at = {name: getattr(self, name) for name in "yxcz"}
        at[axis] = self.off(axis, step)
        return ((at["y"] * self.nx + at["x"]) * self.nc + at["c"], at["z"])

    def peers(self):
        return [self.peer(axis, step) for axis in "zxyc" for step in range(1, getattr(self, "n" + axis))]

    def copies(self):
        return 8 + 2 * (self.nx - 1) + 2 * (self.ny - 1) + self.nc - 1

    def sums(self):
        return self.nz - 1 + 2 * (self.nx - 1) + 2 * (self.ny - 1) + self.nc - 1


def greet(grid):
    barrier = pltpu.get_barrier_semaphore()
    peers = grid.peers()
    for peer in peers:
        pl.semaphore_signal(barrier, inc=1, device_id=peer, device_id_type=MESH)
    pl.semaphore_wait(barrier, len(peers))


def guarded(condition, act):
    if condition is None:
        act()
    else:
        pl.when(condition)(act)


class Leg:
    def __init__(self, sems, ends, sends=None, gets=None, slot=None, slots=1):
        self.sems, self.ends, self.sends, self.gets, self.slot, self.slots = sems, ends, sends, gets, slot, slots
        self.base = sems.used
        sems.used += slots

    def copy(self, slot):
        src, dst, device = self.ends()
        return pltpu.make_async_remote_copy(
            src_ref=src,
            dst_ref=dst,
            send_sem=self.sems.send.at[self.base],
            recv_sem=self.sems.recv.at[self.base + slot],
            device_id=device,
            device_id_type=MESH,
        )

    def start(self):
        guarded(self.sends, lambda: self.copy(0 if self.slot is None else self.slot).start())

    def wait_send(self):
        guarded(self.sends, lambda: self.copy(0).wait_send())

    def wait_recv(self):
        def every():
            for slot in range(self.slots):
                self.copy(slot).wait_recv()

        guarded(self.gets, every)


class Sems:
    def __init__(self, send, recv):
        self.send, self.recv, self.used = send, recv, 0


class Locals:
    def __init__(self, sems):
        self.sems, self.used, self.open = sems, 0, []

    def start(self, ends):
        k = self.used
        self.used += 1

        def copy():
            src, dst = ends()
            return pltpu.make_async_copy(src, dst, self.sems.at[k])

        copy().start()
        self.open.append(copy)
        return copy

    def wait(self, copy):
        copy().wait()
        self.open.remove(copy)

    def drain(self):
        for copy in self.open:
            copy().wait()
        self.open = []


def block_rows(start, size):
    return pl.ds(pl.multiple_of(start * size, size), size)


class Gather:
    STEPS = 6

    def __init__(self, grid, sems, moves, shard, full, cols, keep=None, late_z=False):
        self.grid, self.sems, self.moves = grid, sems, moves
        self.shard, self.full, self.cols, self.keep, self.late_z = shard, full, cols, keep, late_z
        self.half = shard.shape[0] // 2
        self.sent = []

    def place(self, half=None, y=None, x=None, z=None):
        g = self.grid
        take = lambda at, size: pl.ds(0, size) if at is None else at
        rows = pl.ds(0, 2 * self.half) if half is None else pl.ds(half * self.half, self.half)
        return self.full.at[take(y, g.ny), take(x, g.nx), g.c, take(z, g.nz), rows, self.cols]

    def to(self, axis, part):
        g = self.grid
        return [
            Leg(self.sems, lambda k=k: (part(), part(), g.peer(axis, k))) for k in range(1, getattr(g, "n" + axis))
        ]

    def first_z(self, part):
        g = self.grid
        return [
            Leg(self.sems, lambda: (part(g.z), part(g.z), g.at_z(g.mate))),
            Leg(self.sems, lambda: (part(g.z), part(g.z), g.at_z(g.across)), gets=g.inner, slot=g.side, slots=2),
        ]

    def last_z(self, part):
        g = self.grid
        pair = pl.ds(g.other_pair, 2)
        return [
            Leg(self.sems, lambda: (part(pair), part(pair), g.at_z(g.mate)), sends=g.inner, gets=g.outer)
        ]

    def legs(self, step):
        g = self.grid
        if step == 4:
            return self.to("c", self.place)
        if step == 3:
            return self.to("y", lambda: self.place(0, y=g.y)) + self.to("x", lambda: self.place(1, x=g.x))
        if not self.late_z:
            if step == 2:
                return self.to("x", lambda: self.place(0, g.y, g.x)) + self.to("y", lambda: self.place(1, g.y, g.x))
            along = (self.first_z, self.last_z)[step]
            return along(lambda z: self.place(y=g.y, x=g.x, z=z))
        if step == 0:
            return self.to("x", lambda: self.place(0, g.y, g.x, g.z)) + self.to(
                "y", lambda: self.place(1, g.y, g.x, g.z)
            )
        along = (self.first_z, self.last_z)[step - 1]
        return along(lambda z: self.place(0, y=g.y, z=z)) + along(lambda z: self.place(1, x=g.x, z=z))

    def load(self):
        g = self.grid
        self.own = self.moves.start(
            lambda: (self.shard.at[:, self.cols], self.place(y=g.y, x=g.x, z=g.z))
        )

    def step(self, step):
        if step == 0:
            self.moves.wait(self.own)
        else:
            for leg in self.flying:
                leg.wait_recv()
        if step < self.STEPS - 1:
            self.flying = self.legs(step)
            self.sent += self.flying
            for leg in self.flying:
                leg.start()
        elif self.keep is not None:
            every = lambda ref: ref.at[:, :, :, :, :, self.cols]
            self.moves.start(lambda: (every(self.full), every(self.keep)))

    def drain(self):
        for leg in self.sent:
            leg.wait_send()


class Flow:
    def __init__(self, jobs, plan):
        self.jobs, self.plan, self.pumps = jobs, plan, 0
        self.steps = [0] * len(jobs)

    def pump(self, job=None):
        for k in self.plan[self.pumps]:
            self.jobs[k].step(self.steps[k])
            self.steps[k] += 1
        self.pumps += 1
        if job is not None:
            assert self.steps[self.jobs.index(job)] == job.STEPS

    def drain(self):
        assert self.pumps == len(self.plan)
        for job in self.jobs:
            job.drain()


def head_lanes(h):
    return lax.broadcasted_iota(jnp.int32, (1, 2 * HEAD_DIM), 1) // HEAD_DIM == h


def only(lanes, block):
    return jnp.where(lanes, block, 0).astype(BF16)


def fold_small(grid, vectors, bias_ff):
    rows = vectors.shape[0]
    tiled = jnp.tile(vectors.T, (1, LANES // rows))
    mine = jnp.arange(LANES) // rows == lax.axis_index("seq")
    tiled = jnp.where(mine[None, :], tiled, 0).astype(BF16)
    return jnp.concatenate([tiled, bias_ff[None, :], jnp.zeros((23, LANES), BF16)], axis=0)


FWD_WIDTH = 512


LOG_LANES = 4


def forward_kernel(
    grid,
    ctx_len,
    x_in,
    temb,
    small,
    wq_in,
    wo_in,
    wi_in,
    wb_in,
    wq_out,
    wo_out,
    wi_out,
    wb_out,
    vec_out,
    hin_out,
    qkv_out,
    logs_out,
    ctx_out,
    n1_out,
    ub_out,
    hid_out,
    slope_out,
    r2_out,
    send,
    recv,
    move_sems,
    x,
    hin,
    qkv,
    ctx,
    n1,
    ub,
    hid,
    slope,
    r2,
    lse,
    logs_parts,
    vec,
    bias_qkv,
    bias_ff,
    small_full,
    wq,
    wo,
    wi,
    wb,
):
    tokens, width = hin.shape
    hidden = hid.shape[1]
    slots = tokens // SLOT
    tile = FWD_WIDTH
    grid.here()
    moves = Locals(move_sems)
    x_copy = moves.start(lambda: (x_in, x))
    greet(grid)
    sems = Sems(send, recv)

    def gather(shard, full, at, wide, keep, late_z=False):
        return Gather(grid, sems, moves, shard, full, pl.ds(at, wide), keep, late_z)

    small_job = gather(small, small_full, 0, LANES, None)
    half = width // 2
    qkv_cols = [part * width + side * half for side in range(2) for part in range(3)]
    qkv_jobs = [gather(wq_in, wq, at, half, wq_out) for at in qkv_cols]
    out_jobs = [gather(wo_in, wo, at, half, wo_out) for at in range(0, width, half)]
    in_jobs = [gather(wi_in, wi, at, width, wi_out) for at in range(0, hidden, width)]
    back_wide = width * width // hidden
    back_jobs = [gather(wb_in, wb, at, back_wide, wb_out) for at in range(0, width, back_wide)]
    for k in FWD_LATE_Z:
        ([*qkv_jobs, *out_jobs, *in_jobs, *back_jobs][k]).late_z = True
    for job in [small_job, *qkv_jobs, *out_jobs, *in_jobs, *back_jobs]:
        job.load()
    flow = Flow([small_job, *qkv_jobs, *out_jobs, *in_jobs, *back_jobs], FWD_PLAN)
    flow.pump()

    moves.wait(x_copy)

    @pl.loop(0, tokens // 128)
    def _(i):
        at = block_rows(i, 128)
        hin[at, :] = (x[at, :].astype(F32) + temb[...].astype(F32)).astype(BF16)

    moves.start(lambda: (hin, hin_out))
    flow.pump(small_job)
    for i, (y, xx, c) in enumerate(grid.groups):
        tiles = [small_full[y, xx, c, z, pl.ds(0, 16), :].astype(F32) for z in range(grid.nz)]
        vec[:, i * LANES : (i + 1) * LANES] = sum(t[:8] for t in tiles)
        for z, t in enumerate(tiles):
            at = (i * grid.nz + z) * LANES
            bias_ff[:, at : at + LANES] = t[8:9]
    moves.start(lambda: (vec, vec_out))
    bias_qkv[:, :width] = vec[0:1, :]
    bias_qkv[:, width : 2 * width] = jnp.zeros((1, width), F32)
    bias_qkv[:, 2 * width :] = vec[1:2, :]

    def project(at):
        @pl.loop(0, tokens // tile)
        def _(i):
            rows = block_rows(i, tile)
            w = wq[:, :, :, :, :, pl.ds(at, half)].reshape(width, half)
            qkv[rows, pl.ds(at, half)] = (mm(hin[rows, :], w, NN) + bias_qkv[:, at : at + half]).astype(BF16)

    def flow_at(i, steps):
        for n in range(steps):

            @pl.when(i == n)
            def _():
                flow.pump()

    first = grid.z * slots
    pairs = width // (2 * HEAD_DIM)
    lane = lax.broadcasted_iota(jnp.int32, (1, LANES), 1)
    key_at = lax.broadcasted_iota(jnp.int32, (1, SLOT), 1)

    def attend(side):
        steps = slots * pairs // 2

        @pl.loop(0, steps)
        def _(i):
            s = i // (pairs // 2)
            p = i % (pairs // 2) + side * (pairs // 2)
            rows = block_rows(s, SLOT)
            off = jnp.where(key_at < ctx_len[0, first + s] + BLOCK, 0.0, -1e30)
            at = pl.multiple_of(p * LANES, LANES)
            q2 = qkv[rows, pl.ds(at, LANES)]
            k2 = qkv[rows, pl.ds(at + width, LANES)]
            v2 = qkv[rows, pl.ds(at + 2 * width, LANES)]
            total = None
            logs = lse[rows, :]
            for h in range(2):
                mine = head_lanes(h)
                score = mm(only(mine, q2) * jnp.asarray(1.0 / math.sqrt(HEAD_DIM), BF16), k2, NT) + off
                high = jnp.max(score, axis=1, keepdims=True)
                e = jnp.exp(score - high)
                norm = jnp.sum(e, axis=1, keepdims=True)
                part = mm(e.astype(BF16), only(mine, v2), NN) * (1.0 / norm)
                total = part if total is None else total + part
                logs = jnp.where(lane // LOG_LANES == 2 * p + h, high + jnp.log(norm), logs)
            lse[rows, :] = logs
            ctx[rows, pl.ds(at, LANES)] = total.astype(BF16)
            flow_at(i, steps)

    lse[...] = jnp.zeros(lse.shape, F32)
    for side in range(2):
        for part in range(3):
            job = side * 3 + part
            flow.pump(qkv_jobs[job])
            project(qkv_cols[job])
        attend(side)
    moves.start(lambda: (qkv, qkv_out))
    moves.start(lambda: (ctx, ctx_out))

    @pl.loop(0, tokens // 128)
    def _(i):
        rows = block_rows(i, 128)
        rest, parts = lse[rows, :], []
        for _ in range(LOG_LANES - 1):
            parts.append(rest.astype(BF16).astype(F32))
            rest = rest - parts[-1]
        value = jnp.ones((128, LANES), F32)
        for n, part in enumerate(parts):
            value = jnp.where(lane % LOG_LANES == n + 1, part, value)
        logs_parts[rows, :] = value.astype(BF16)

    moves.start(lambda: (logs_parts, logs_out))
    for job in out_jobs:
        flow.pump(job)

    @pl.loop(0, tokens // 256)
    def _(i):
        rows = block_rows(i, 256)
        attn = mm(ctx[rows, :], wo[...].reshape(width, width), NN) + vec[2:3, :]
        resid = x[rows, :].astype(F32) + temb[...].astype(F32) + attn
        centered = resid - jnp.mean(resid, axis=1, keepdims=True)
        spread = lax.rsqrt(jnp.mean(centered * centered, axis=1, keepdims=True) + norm_eps)
        unit = centered * spread
        n1[rows, :width] = unit
        n1[rows, width:] = jnp.broadcast_to(spread, (256, LANES))
        ub[rows, :] = (unit * vec[4:5, :] + vec[5:6, :]).astype(BF16)
        flow_at(i, tokens // 256)

    moves.start(lambda: (n1, n1_out))
    moves.start(lambda: (ub, ub_out))
    kept = [None, None]
    for j, at in enumerate(range(0, hidden, tile)):
        if at % width == 0:
            flow.pump(in_jobs[at // width])
        if kept[j % 2] is not None:
            moves.wait(kept[j % 2])

        @pl.loop(0, tokens // tile)
        def _(i):
            rows = block_rows(i, tile)
            w = wi[:, :, :, :, :, pl.ds(at, tile)].reshape(width, tile)
            z = mm(ub[rows, :], w, NN) + bias_ff[:, at : at + tile]
            gate = 0.5 * (1.0 + lax.erf(z * math.sqrt(0.5)))
            hid[rows, pl.ds(at, tile)] = (z * gate).astype(BF16)
            bell = jnp.exp(-0.5 * z * z) * (1.0 / math.sqrt(2.0 * math.pi))
            slope[j % 2, rows, :] = (gate + z * bell).astype(BF16)

        kept[j % 2] = moves.start(lambda j=j, at=at: (slope.at[j % 2], slope_out.at[:, pl.ds(at, tile)]))
        flow.pump()
    moves.start(lambda: (hid, hid_out))
    kept = [None, None]
    for j, job in enumerate(back_jobs):
        flow.pump(job)
        if kept[j % 2] is not None:
            moves.wait(kept[j % 2])
        cols = slice(j * back_wide, (j + 1) * back_wide)

        @pl.loop(0, tokens // tile)
        def _(i):
            rows = block_rows(i, tile)
            w = wb[:, :, :, :, :, pl.ds(j * back_wide, back_wide)].reshape(hidden, back_wide)
            f = mm(hid[rows, :], w, NN) + vec[3:4, cols]
            r2[j % 2, rows, :] = n1[rows, cols] * vec[4:5, cols] + vec[5:6, cols] + f

        kept[j % 2] = moves.start(
            lambda j=j: (r2.at[j % 2], r2_out.at[:, pl.ds(j * back_wide, back_wide)])
        )
    flow.drain()
    moves.drain()


FWD_LATE_Z = (2, 5, 6, 8, 11, 12, 13, 14, 15)
FWD_PLAN = (
    (0, 1, 2, 3, 4, 5,),
    (0, 3, 1, 0, 2, 4, 0, 6, 5, 1, 0, 6, 2, 0,),
    (1, 7, 3, 4, 5, 2, 8, 6, 1, 7, 3, 9, 8, 4, 10, 1,),
    (5, 11, 6, 12, 7, 2, 8, 2,),
    (3, 9, 10, 11, 3,),
    (4, 7, 13,),
    (),
    (4, 5,),
    (9,),
    (5, 6, 10, 12,),
    (8, 14,),
    (6, 11,),
    (7,),
    (),
    (),
    (),
    (7, 9, 15, 10, 16, 13,),
    (8, 12, 14,),
    (),
    (8, 11,),
    (),
    (),
    (),
    (13,),
    (),
    (),
    (9, 12, 15,),
    (),
    (9, 14,),
    (),
    (),
    (10, 16,),
    (10, 13,),
    (),
    (11, 15,),
    (11,),
    (),
    (12, 14,),
    (12, 16,),
    (),
    (13,),
    (15, 13,),
    (),
    (14, 16, 14,),
    (15, 15,),
    (16, 16,),
)


def forward(grid, context_len, inputs, timestep, small, qkv_weight, out_weight, in_weight, back_weight):
    tokens, width = inputs.shape
    hidden = in_weight.shape[1]
    weights = (qkv_weight, out_weight, in_weight, back_weight)
    back_wide = width * width // hidden

    def whole(shard):
        return (grid.ny, grid.nx, grid.nc, grid.nz, *shard.shape)

    out = [
        *[(whole(w), BF16) for w in weights],
        ((8, width), F32),
        ((tokens, width), BF16),
        ((tokens, 3 * width), BF16),
        ((tokens, LANES), BF16),
        ((tokens, width), BF16),
        ((tokens, width + LANES), F32),
        ((tokens, width), BF16),
        ((tokens, hidden), BF16),
        ((tokens, hidden), BF16),
        ((tokens, width), F32),
    ]
    jobs = 1 + 6 + 2 + hidden // width + width // back_wide
    scratch = [
        pltpu.SemaphoreType.DMA((jobs * grid.copies(),)),
        pltpu.SemaphoreType.DMA((jobs * grid.copies(),)),
        pltpu.SemaphoreType.DMA((64,)),
        pltpu.VMEM((tokens, width), BF16),
        pltpu.VMEM((tokens, width), BF16),
        pltpu.VMEM((tokens, 3 * width), BF16),
        pltpu.VMEM((tokens, width), BF16),
        pltpu.VMEM((tokens, width + LANES), F32),
        pltpu.VMEM((tokens, width), BF16),
        pltpu.VMEM((tokens, hidden), BF16),
        pltpu.VMEM((2, tokens, FWD_WIDTH), BF16),
        pltpu.VMEM((2, tokens, back_wide), F32),
        pltpu.VMEM((tokens, LANES), F32),
        pltpu.VMEM((tokens, LANES), BF16),
        pltpu.VMEM((8, width), F32),
        pltpu.VMEM((1, 3 * width), F32),
        pltpu.VMEM((1, hidden), F32),
        pltpu.VMEM(whole(small), BF16),
        *[pltpu.VMEM(whole(w), BF16) for w in weights],
    ]
    return pl.pallas_call(
        functools.partial(forward_kernel, grid),
        out_shape=[jax.ShapeDtypeStruct(*o) for o in out],
        in_specs=[IN_SMEM, ANY, IN_VMEM, ANY, ANY, ANY, ANY, ANY],
        out_specs=[ANY] * len(out),
        scratch_shapes=scratch,
        compiler_params=pltpu.CompilerParams(
            collective_id=1, has_side_effects=True, vmem_limit_bytes=VMEM_BYTES
        ),
        name="forward_pass",
    )(context_len, inputs, timestep, small, *weights)


def second_norm_kernel(r2, dy, vec, result, dr2, df, sums):
    resid = r2[...]
    centered = resid - jnp.mean(resid, axis=1, keepdims=True)
    spread = lax.rsqrt(jnp.mean(centered * centered, axis=1, keepdims=True) + norm_eps)
    unit = centered * spread
    result[...] = unit * vec[6:7, :] + vec[7:8, :]
    grad = dy[...].astype(F32)
    e = grad * vec[6:7, :]
    back = spread * (
        e - jnp.mean(e, axis=1, keepdims=True) - unit * jnp.mean(e * unit, axis=1, keepdims=True)
    )
    dr2[...] = back
    df[...] = back.astype(BF16)

    @pl.when(pl.program_id(0) == 0)
    def _():
        sums[...] = jnp.zeros(sums.shape, F32)

    sums[3:4, :] += jnp.sum(back, axis=0, keepdims=True)
    sums[6:7, :] += jnp.sum(grad * unit, axis=0, keepdims=True)
    sums[7:8, :] += jnp.sum(grad, axis=0, keepdims=True)


def second_norm(r2, out_grad, vec):
    tokens, width = r2.shape
    tile = 256
    rows = pl.BlockSpec((tile, width), lambda i: (i, 0))
    top = pl.BlockSpec((8, width), lambda i: (0, 0))
    return pl.pallas_call(
        second_norm_kernel,
        grid=(tokens // tile,),
        out_shape=[
            jax.ShapeDtypeStruct((tokens, width), F32),
            jax.ShapeDtypeStruct((tokens, width), F32),
            jax.ShapeDtypeStruct((tokens, width), BF16),
            jax.ShapeDtypeStruct((8, width), F32),
        ],
        in_specs=[rows, rows, top],
        out_specs=[rows, rows, rows, top],
        compiler_params=pltpu.CompilerParams(vmem_limit_bytes=VMEM_BYTES),
        name="second_norm",
    )(r2, out_grad, vec)


class Reduce:
    def __init__(self, grid, sems, base, bufs, other, product, write):
        self.grid, self.sems, self.base = grid, sems, base
        self.other, self.product, self.write = other, product, write
        self.sum, self.in2a, self.in2b, self.in3a, self.in3b, self.in4 = bufs
        self.half = self.sum.shape[2] // 2
        self.rows = self.sum.shape[2] // grid.nz

    def copies(self, stage):
        g = self.grid
        lo, hi = pl.ds(0, self.half), pl.ds(self.half, self.half)
        ys, xs, zs = range(1, g.ny), range(1, g.nx), range(1, g.nz)
        if stage == 1:
            ends = [(self.other, self.sum, g.peer("c", 1))]
        elif stage == 2:
            ends = [(self.sum.at[g.off("y", k), :, lo], self.in2a.at[k - 1], g.peer("y", k)) for k in ys]
            ends += [(self.sum.at[:, g.off("x", k), hi], self.in2b.at[k - 1], g.peer("x", k)) for k in xs]
        elif stage == 3:
            ends = [(self.sum.at[g.y, g.off("x", k), lo], self.in3a.at[k - 1], g.peer("x", k)) for k in xs]
            ends += [(self.sum.at[g.off("y", k), g.x, hi], self.in3b.at[k - 1], g.peer("y", k)) for k in ys]
        else:
            mine = lambda k: self.sum.at[g.y, g.x, block_rows(g.off("z", k), self.rows)]
            ends = [(mine(k), self.in4.at[k - 1], g.peer("z", k)) for k in zs]
        plane = len(ys) + len(xs)
        base = self.base + (0, 0, 1, 1 + plane, 1 + 2 * plane)[stage]
        return [self.sems(base + i, *e) for i, e in enumerate(ends)]

    def send(self, stage):
        for copy in self.copies(stage):
            copy.start()

    def landed(self, stage):
        for copy in self.copies(stage):
            copy.wait_recv()

    def start(self):
        def store(y, x, cols, value):
            self.other[y, x, :, cols] = value.astype(BF16)

        self.product(self.grid.off("c", 1), store)
        self.send(1)

    def second(self):
        self.landed(1)

        def add(y, x, cols, value):
            self.sum[y, x, :, cols] = (self.sum[y, x, :, cols].astype(F32) + value).astype(BF16)

        self.product(self.grid.c, add)
        self.send(2)

    def third(self):
        g = self.grid
        self.landed(2)
        lo, hi = pl.ds(0, self.half), pl.ds(self.half, self.half)
        for x in range(g.nx):
            add_into(self.sum.at[g.y, x, lo], [self.in2a.at[k, x] for k in range(g.ny - 1)])
        for y in range(g.ny):
            add_into(self.sum.at[y, g.x, hi], [self.in2b.at[k, y] for k in range(g.nx - 1)])
        self.send(3)

    def fourth(self):
        g = self.grid
        self.landed(3)
        lo, hi = pl.ds(0, self.half), pl.ds(self.half, self.half)
        add_into(self.sum.at[g.y, g.x, lo], [self.in3a.at[k] for k in range(g.nx - 1)])
        add_into(self.sum.at[g.y, g.x, hi], [self.in3b.at[k] for k in range(g.ny - 1)])
        self.send(4)

    def finish(self):
        g = self.grid
        self.landed(4)
        total = self.sum[g.y, g.x, block_rows(g.z, self.rows), :].astype(F32)
        for k in range(g.nz - 1):
            total += self.in4[k].astype(F32)
        self.write(total)

    def freed(self):
        for copy in self.copies(1):
            copy.wait_send()

    def drain(self):
        for stage in (2, 3, 4):
            for copy in self.copies(stage):
                copy.wait_send()


def add_into(dst, srcs):
    total = dst[...].astype(F32)
    for src in srcs:
        total += src[...].astype(F32)
    dst[...] = total.astype(dst.dtype)


def reduce_bufs(grid, rows, width, count):
    group, half = rows * grid.nz, rows * grid.nz // 2
    ny, nx = grid.ny, grid.nx
    return [
        pltpu.VMEM((count, *shape, width), BF16)
        for shape in (
            (ny, nx, group),
            (ny - 1, nx, half),
            (nx - 1, ny, half),
            (nx - 1, half),
            (ny - 1, half),
            (grid.nz - 1, rows),
        )
    ]


class Line:
    STAGES = {3: "third", 4: "fourth", 5: "finish"}

    def __init__(self, plan):
        self.jobs, self.plan, self.pumps, self.stage = [], plan, 0, []

    def start(self, job):
        self.jobs.append(job)
        self.stage.append(3)
        job.start()

    def step(self, k):
        getattr(self.jobs[k], self.STAGES[self.stage[k]])()
        self.stage[k] += 1

    def pump(self):
        for k, stage in self.plan[self.pumps] if self.pumps < len(self.plan) else ():
            if self.stage[k] == stage:
                self.step(k)
        self.pumps += 1

    def drain(self):
        for at in range(len(self.jobs) + 3):
            for lag, stage in ((2, 5), (1, 4), (0, 3)):
                k = at - lag
                if 0 <= k < len(self.jobs) and self.stage[k] == stage:
                    self.step(k)
        for job in self.jobs:
            job.drain()


BWD_TILE = 512


def backward_kernel(
    grid,
    ctx_len,
    vec,
    sums_in,
    logs,
    dr2,
    df_in,
    hid_in,
    slope_in,
    ub_in,
    n1_in,
    ctx_in,
    qkv_in,
    hin_in,
    wq_in,
    wo_in,
    wi_in,
    wb_in,
    grad_input,
    grad_qkv,
    grad_out,
    grad_in,
    grad_back,
    grad_small,
    send,
    recv,
    move_sems,
    pool,
    du,
    n1,
    sums,
    bias_sum,
    other_wide,
    other_back,
    other_small,
    *bufs,
):
    tokens, width = du.shape
    hidden = bias_sum.shape[1]
    slots = tokens // SLOT
    blocks = hidden // width
    tile = BWD_TILE
    grid.here()
    moves = Locals(move_sems)
    line = Line(BWD_PLAN)

    def sems(k, src, dst, device):
        return pltpu.make_async_remote_copy(
            src_ref=src,
            dst_ref=dst,
            send_sem=send.at[k],
            recv_sem=recv.at[k],
            device_id=device,
            device_id_type=MESH,
        )

    def write_to(out, at, wide):
        def write(total):
            out[:, at : at + wide] = total

        return write


    def load(src, block):
        return moves.start(lambda: (src(), pool.at[block]))

    def columns(ref, j):
        return lambda: ref.at[:, pl.ds(j * width, width)]

    hid, df, ub = [0, 1, 2, 3], 4, 5
    ff_blocks = [(6, 7, 8), (10, 1, 2)]
    dz_blocks = [9, 3]

    def load_back(j):
        return load(lambda: wb_in.at[pl.ds(j * width, width)], ff_blocks[j % 2][0])

    def load_slope(j):
        return load(columns(slope_in, j), ff_blocks[j % 2][1])

    def load_inner(j):
        return load(columns(wi_in, j), ff_blocks[j % 2][2])

    first_loads = [load(lambda: df_in, df), load_back(0), load_slope(0)]
    hid_loads = [load(columns(hid_in, j), hid[j]) for j in range(blocks)]
    inner_load = load_inner(0)
    du_copy = moves.start(lambda: (dr2, du))
    greet(grid)
    back_loads = {1: load_back(1)}
    ub_load = load(lambda: ub_in, ub)
    norm_rows = n1.shape[1]

    def load_n1(i):
        return moves.start(lambda: (n1_in.at[pl.ds(i * norm_rows, norm_rows)], n1.at[i % 2]))

    n1_loads = [load_n1(0), load_n1(1)]
    sums[...] = sums_in[...]
    bias_sum[...] = jnp.zeros(bias_sum.shape, F32)

    places = [(y, x) for y in range(grid.ny) for x in range(grid.nx)]
    group = width // (len(places) * grid.nc)

    def token_product(lhs, rhs, wide, step):
        def product(c, take):
            left = jnp.concatenate(
                [pool[lhs, :, block_rows((y * grid.nx + x) * grid.nc + c, group)] for y, x in places], axis=1
            )
            for n in range(wide // step):
                cols = pl.ds(n * step, step)
                value = mm(left, rhs(cols), TN)
                for i, (y, x) in enumerate(places):
                    take(y, x, cols, value[i * group : (i + 1) * group])

        return product

    def back_product(k, wide):
        def product(c, take):
            rows = width // grid.nc
            left = jnp.concatenate([pool[hid[i], :, block_rows(c, rows)] for i in range(len(places))], axis=1)
            value = mm(left, pool[df, :, k * wide : (k + 1) * wide], TN)
            for i, (y, x) in enumerate(places):
                take(y, x, slice(None), value[i * rows : (i + 1) * rows])

        return product

    bufs_back, bufs_wide, bufs_pair, bufs_small = [bufs[6 * i : 6 * i + 6] for i in range(4)]
    back_wide = width // blocks
    back_jobs = [
        Reduce(
            grid,
            sems,
            k * grid.sums(),
            [b.at[k] for b in bufs_back],
            other_back.at[k % 2],
            back_product(k, back_wide),
            write_to(grad_back, k * back_wide, back_wide),
        )
        for k in range(blocks)
    ]
    wide_jobs = 0

    def wide_job(lhs, rhs, out, at):
        nonlocal wide_jobs
        k = wide_jobs
        wide_jobs += 1
        return Reduce(
            grid,
            sems,
            (blocks + k) * grid.sums(),
            [b.at[k] for b in bufs_wide],
            other_wide.at[k % 2],
            token_product(lhs, lambda cols: pool[rhs, :, cols], width, tile),
            write_to(out, at, width),
        )

    def slope_product(j, n):
        back, slope, _ = ff_blocks[j % 2]
        cols = pl.ds(n * tile, tile)
        at = slice(j * width + n * tile, j * width + (n + 1) * tile)

        @pl.loop(0, tokens // tile, unroll=True)
        def _(t):
            rows = block_rows(t, tile)
            grad = mm(pool[df, rows, :], pool[back, cols, :], NT) * pool[slope, rows, cols].astype(F32)
            bias_sum[:, at] += jnp.sum(grad, axis=0, keepdims=True)
            pool[dz_blocks[j % 2], rows, cols] = grad.astype(BF16)

    def inner_product(j, n):
        inner = ff_blocks[j % 2][2]
        rows = pl.ds(n * tile, tile)

        @pl.loop(0, width // tile, unroll=True)
        def _(t):
            cols = block_rows(t, tile)
            du[rows, cols] += mm(pool[dz_blocks[j % 2], rows, :], pool[inner, cols, :], NT)

    tiles = range(width // tile)
    for copy in first_loads:
        moves.wait(copy)
    for n in tiles:
        slope_product(0, n)
    for copy in hid_loads:
        moves.wait(copy)
    line.start(back_jobs[0])
    line.start(back_jobs[1])
    moves.wait(inner_load)
    moves.wait(du_copy)
    inner_product(0, 0)
    back_jobs[0].second()
    back_jobs[0].freed()
    line.start(back_jobs[2])
    back_jobs[1].second()
    back_jobs[1].freed()
    line.start(back_jobs[3])
    line.pump()
    moves.wait(ub_load)
    in_jobs = [wide_job(ub, dz_blocks[j % 2], grad_in, j * width) for j in range(blocks)]
    line.start(in_jobs[0])
    back_jobs[2].second()
    back_jobs[3].second()
    line.pump()
    ff_loads = {1: [load_slope(1), load_inner(1)]}
    for n in tiles[1:]:
        inner_product(0, n)
        line.pump()
    for j in range(1, blocks):
        if j + 1 < blocks:
            back_loads[j + 1] = load_back(j + 1)
            ff_loads[j + 1] = [load_slope(j + 1), load_inner(j + 1)]
        for copy in [back_loads.pop(j), *ff_loads.pop(j)]:
            moves.wait(copy)
        for n in tiles:
            slope_product(j, n)
            if n == 0:
                in_jobs[j - 1].second()
                line.pump()
        if j >= 2:
            in_jobs[j - 2].freed()
        line.start(in_jobs[j])
        line.pump()
        for n in tiles:
            inner_product(j, n)
            line.pump()

    da, out_weight, ctx, dctx = 4, 6, 7, 2
    q, k, v = 0, 8, 1
    dq, dk, dv = 3, 9, 5
    hin, wq = 4, (6, 7, 10)
    out_load = load(lambda: wo_in, out_weight)
    ctx_load = load(lambda: ctx_in, ctx)
    qkv_loads = [load(columns(qkv_in, i), block) for i, block in enumerate((q, k, v))]
    for n in range(tokens // norm_rows):
        moves.wait(n1_loads.pop(0))

        @pl.loop(0, norm_rows // 128)
        def _(i):
            rows = block_rows(n * (norm_rows // 128) + i, 128)
            held = n1[n % 2, block_rows(i, 128), :]
            unit, grad = held[:, :width], du[rows, :]
            e = grad * vec[4:5, :]
            back = held[:, width : width + 1] * (
                e - jnp.mean(e, axis=1, keepdims=True) - unit * jnp.mean(e * unit, axis=1, keepdims=True)
            )
            sums[4:5, :] += jnp.sum(grad * unit, axis=0, keepdims=True)
            sums[5:6, :] += jnp.sum(grad, axis=0, keepdims=True)
            sums[2:3, :] += jnp.sum(back, axis=0, keepdims=True)
            du[rows, :] = back
            pool[da, rows, :] = back.astype(BF16)

        if (n + 2) * norm_rows < tokens:
            n1_loads.append(load_n1(n + 2))

    in_jobs[-1].second()
    line.pump()
    moves.wait(out_load)
    moves.wait(ctx_load)
    out_job = wide_job(ctx, da, grad_out, 0)
    in_jobs[-2].freed()
    line.start(out_job)

    @pl.loop(0, (tokens // tile) * (width // tile), unroll=2)
    def _(t):
        rows, cols = block_rows(t % (tokens // tile), tile), block_rows(t // (tokens // tile), tile)
        pool[dctx, rows, cols] = mm(pool[da, rows, :], pool[out_weight, cols, :], NT).astype(BF16)

    line.pump()
    out_job.second()
    line.pump()
    hin_load = load(lambda: hin_in, hin)
    wq_loads = [load(columns(wq_in, i), block) for i, block in enumerate(wq)]
    for copy in qkv_loads:
        moves.wait(copy)
    first = grid.z * slots
    pairs = width // (2 * HEAD_DIM)
    key_at = lax.broadcasted_iota(jnp.int32, (SLOT, 1), 0)
    lane = lax.broadcasted_iota(jnp.int32, (1, LANES), 1)
    scale = 1.0 / math.sqrt(HEAD_DIM)

    def pair_job(p):
        at = block_rows(p, LANES)

        def rhs(_):
            return jnp.concatenate([pool[block, :, at] for block in (dq, dk, dv)], axis=1)

        def write(total):
            for i in range(3):
                grad_qkv[:, pl.ds(pl.multiple_of(i * width + p * LANES, LANES), LANES)] = total[
                    :, i * LANES : (i + 1) * LANES
                ]

        return Reduce(
            grid,
            sems,
            (2 * blocks + 1 + p) * grid.sums(),
            [b.at[p] for b in bufs_pair],
            other_wide.at[p % 2, :, :, :, pl.ds(0, 3 * LANES)],
            token_product(hin, rhs, 3 * LANES, 3 * LANES),
            write,
        )

    def follow(p, traced):
        for lag, name in zip(PAIR_LAGS, ("second", "third", "fourth", "finish")):
            if traced:

                @pl.when(p >= lag)
                def _():
                    getattr(pair_job(p - lag), name)()

            elif 0 <= p - lag < pairs:
                getattr(pair_job(p - lag), name)()

    for job in (back_jobs[-2], back_jobs[-1], in_jobs[-1], out_job):
        job.freed()
    moves.wait(hin_load)

    @pl.loop(0, pairs)
    def _(p):
        at = block_rows(p, LANES)

        @pl.loop(0, slots)
        def _(s):
            rows = block_rows(s, SLOT)
            off = jnp.where(key_at < ctx_len[0, first + s] + BLOCK, 0.0, -1e30)
            extra = jnp.where(lane % LOG_LANES == 0, off, -1.0).astype(BF16)
            q2, k2, v2, c2 = pool[q, rows, at], pool[k, rows, at], pool[v, rows, at], pool[dctx, rows, at]
            keys = jnp.concatenate([k2, extra], axis=1)
            sum_q = sum_k = sum_v = None
            for h in range(2):
                mine = head_lanes(h)
                qh = only(mine, q2) * jnp.asarray(scale, BF16)
                ch = only(mine, c2)
                log = only(lane // LOG_LANES == 2 * p + h, logs[rows, :])
                prob = jnp.exp(mm(keys, jnp.concatenate([qh, log], axis=1), NT))
                dprob = mm(v2, ch, NT)
                dot = jnp.sum(prob * dprob, axis=0, keepdims=True)
                dscore = (prob * (dprob - dot)).astype(BF16)
                add_v = mm(prob.astype(BF16), ch, NN)
                add_k = mm(dscore, qh, NN)
                add_q = mm(dscore, only(mine, k2), TN)
                sum_q = add_q if sum_q is None else sum_q + add_q
                sum_k = add_k if sum_k is None else sum_k + add_k
                sum_v = add_v if sum_v is None else sum_v + add_v
            pool[dq, rows, at] = (sum_q * scale).astype(BF16)
            pool[dk, rows, at] = sum_k.astype(BF16)
            pool[dv, rows, at] = sum_v.astype(BF16)

        for row, block in enumerate((dq, dv)):
            sums[row : row + 1, at] = jnp.sum(pool[block, :, at].astype(F32), axis=0, keepdims=True)

        @pl.when(p >= 2)
        def _():
            pair_job(p - 2).freed()

        pair_job(p).start()
        follow(p, True)
        for n in range(pairs):

            @pl.when(p == n)
            def _():
                line.pump()

    def small_product(c, take):
        for y, x in places:
            at = (y * grid.nx + x) * grid.nc + c
            eight = sums[:, block_rows(at, LANES)]
            rows = []
            for z in range(grid.nz):
                rows += [eight, bias_sum[:, block_rows(at * grid.nz + z, LANES)], jnp.zeros((7, LANES), F32)]
            take(y, x, slice(None), jnp.concatenate(rows, axis=0))

    small = Reduce(
        grid,
        sems,
        (2 * blocks + 1 + pairs) * grid.sums(),
        [b.at[0] for b in bufs_small],
        other_small,
        small_product,
        write_to(grad_small, 0, LANES),
    )
    small.start()
    follow(pairs, False)
    small.second()
    for copy in wq_loads:
        moves.wait(copy)
    tail = pairs + 1
    for n in range(tokens // tile):
        rows = pl.ds(n * tile, tile)
        for m in range(width // tile):
            cols = pl.ds(m * tile, tile)
            total = du[rows, cols]
            for block, weight in zip((dq, dk, dv), wq):
                total += mm(pool[block, rows, :], pool[weight, cols, :], NT)
            du[rows, cols] = total
            follow(tail, False)
            tail += 1

        moves.start(lambda rows=rows: (du.at[rows], grad_input.at[rows]))
    small.third()
    small.fourth()
    for p in range(tail, pairs + PAIR_LAGS[-1]):
        follow(p, False)
    small.finish()
    for p in range(pairs):
        pair_job(p).drain()
    for job in (pair_job(pairs - 2), pair_job(pairs - 1), small):
        job.freed()
    small.drain()
    line.drain()
    moves.drain()


PAIR_LAGS = (1, 3, 5, 9)
BWD_PLAN = (
    (),
    (),
    ((0, 3),),
    (),
    ((1, 3),),
    (),
    (),
    ((2, 3),),
    (),
    ((3, 3),),
    (),
    ((0, 4),),
    (),
    ((4, 3),),
    (),
    ((1, 4),),
    ((2, 4), (5, 3), (0, 5),),
    (),
    ((3, 4),),
    ((1, 5), (4, 4), (6, 3),),
    ((2, 5), (7, 3),),
    ((3, 5), (5, 4), (8, 3),),
    ((4, 5), (6, 4),),
    ((7, 4),),
    ((5, 5), (8, 4),),
    ((6, 5),),
)


def backward(grid, context_len, vec, sums, logs, dr2, df, hid, slope, ub, n1, ctx, qkv, hin, weights):
    tokens, width = ub.shape
    hidden = hid.shape[1]
    blocks = hidden // width
    count = grid.count
    rows = width // count
    pairs = width // LANES
    jobs = blocks + blocks + 1 + pairs + 1
    out = [
        (tokens, width),
        (rows, 3 * width),
        (rows, width),
        (rows, hidden),
        (hidden // count, width),
        (16, LANES),
    ]
    scratch = [
        pltpu.SemaphoreType.DMA((jobs * grid.sums(),)),
        pltpu.SemaphoreType.DMA((jobs * grid.sums(),)),
        pltpu.SemaphoreType.DMA((64,)),
        pltpu.VMEM((11, tokens, width), BF16),
        pltpu.VMEM((tokens, width), F32),
        pltpu.VMEM((2, 128, width + LANES), F32),
        pltpu.VMEM((8, width), F32),
        pltpu.VMEM((1, hidden), F32),
        pltpu.VMEM((2, grid.ny, grid.nx, grid.nz * rows, width), BF16),
        pltpu.VMEM((2, grid.ny, grid.nx, hidden // count * grid.nz, width // blocks), BF16),
        pltpu.VMEM((grid.ny, grid.nx, 16 * grid.nz, LANES), BF16),
        *reduce_bufs(grid, hidden // count, width // blocks, blocks),
        *reduce_bufs(grid, rows, width, blocks + 1),
        *reduce_bufs(grid, rows, 3 * LANES, pairs),
        *reduce_bufs(grid, 16, LANES, 1),
    ]
    return pl.pallas_call(
        functools.partial(backward_kernel, grid),
        out_shape=[jax.ShapeDtypeStruct(o, F32) for o in out],
        in_specs=[IN_SMEM, *[IN_VMEM] * 3, *[ANY] * 13],
        out_specs=[ANY, *[IN_VMEM] * 5],
        scratch_shapes=scratch,
        compiler_params=pltpu.CompilerParams(
            collective_id=2, has_side_effects=True, vmem_limit_bytes=VMEM_BYTES
        ),
        name="backward_pass",
    )(context_len, vec, sums, logs, dr2, df, hid, slope, ub, n1, ctx, qkv, hin, *weights)


def outputs_kernel(*refs):
    n = (len(refs) - 3) // 2
    arrays, small, copies, (vec, bias) = refs[:n], refs[n], refs[n + 1 : 2 * n + 1], refs[2 * n + 1 :]
    for src, dst in zip(arrays, copies):
        dst[...] = src[...]
    z = lax.axis_index("seq")
    rows = vec.shape[0]
    mine = [jnp.where(z == k, small[:8, k * rows : (k + 1) * rows], 0.0) for k in range(LANES // rows)]
    vec[...] = sum(mine).T
    bias[...] = small[8:9, :]


def outputs(arrays, small, rows):
    steps = 4
    like = [jax.ShapeDtypeStruct(a.shape, F32) for a in arrays]
    parts = [pl.BlockSpec((a.shape[0] // steps, a.shape[1]), lambda i: (i, 0)) for a in arrays]
    whole = [pl.BlockSpec(shape, lambda i: (0, 0)) for shape in (small.shape, (rows, 8), (1, LANES))]
    return pl.pallas_call(
        outputs_kernel,
        grid=(steps,),
        out_shape=[*like, jax.ShapeDtypeStruct((rows, 8), F32), jax.ShapeDtypeStruct((1, LANES), F32)],
        in_specs=[*parts, whole[0]],
        out_specs=[*parts, *whole[1:]],
        compiler_params=pltpu.CompilerParams(vmem_limit_bytes=VMEM_BYTES),
        name="outputs",
    )(*arrays, small)


def shards(
    grid, inputs, timestep, context_len, out_grad, qkv_weight, out_weight, in_weight, back_weight, vectors, bias_ff
):
    weights = (qkv_weight, out_weight, in_weight, back_weight)
    if not fits(grid, inputs, vectors, bias_ff, in_weight):
        return plain_shards(inputs, timestep, context_len, out_grad, *weights, vectors, bias_ff)
    small = fold_small(grid, vectors, bias_ff)
    *full, vec, hin, qkv, logs, ctx, n1, ub, hid, slope, r2 = forward(
        grid, context_len, inputs, timestep, small, *weights
    )
    full = [f.reshape(-1, f.shape[-1]) for f in full]
    result, dr2, df, sums = second_norm(r2, out_grad, vec)
    *grads, grad_small = backward(
        grid, context_len, vec, sums, logs, dr2, df, hid, slope, ub, n1, ctx, qkv, hin, full
    )
    *grads, vec_share, bias_share = outputs(grads, grad_small, vectors.shape[0])
    return (result, *grads, vec_share, bias_share.reshape(-1))


def fits(grid, inputs, vectors, bias_ff, in_weight):
    tokens, width = inputs.shape
    return (
        tokens == width
        and tokens % SLOT == 0
        and vectors.shape[0] * grid.nz == LANES
        and bias_ff.shape[0] == LANES
        and in_weight.shape[1] % width == 0
        and vectors.shape[0] % 32 == 0
        and width // HEAD_DIM * LOG_LANES <= LANES
        and grid.nc == 2
        and grid.nx > 1
        and grid.ny > 1
        and grid.nz == 4
        and in_weight.shape[1] == grid.ny * grid.nx * width
    )


def specs():
    rows = P(("dp", "seq"), None)
    return dict(
        in_specs=(rows, P("dp", None), P("dp", None), *[rows] * 6, P(("dp", "seq"))),
        out_specs=(*[rows] * 7, P(("dp", "seq"))),
    )


def solution(mesh):
    return jax.shard_map(functools.partial(shards, Grid(mesh)), mesh=mesh, check_vma=False, **specs())
```

```python
import functools
import math

import jax
import jax.numpy as jnp
from jax import lax
from jax.experimental import pallas as pl
from jax.experimental.pallas import tpu as pltpu
from jax.sharding import PartitionSpec as P

HEAD_DIM = 64
SLOT = 512
BLOCK = 25


norm_eps = 1e-05


def norm_forward(resid, gain_vec, shift_vec):
    row_mean = jnp.mean(resid, axis=-1, keepdims=True)
    centered = resid - row_mean
    variance = jnp.mean(centered * centered, axis=-1, keepdims=True)
    inv_std = lax.rsqrt(variance + norm_eps)
    normed = centered * inv_std
    return (normed * gain_vec + shift_vec, normed, inv_std)


def norm_backward(grad_out, normed, inv_std, gain_vec):
    grad_norm = grad_out * gain_vec
    grad_resid = inv_std * (
        grad_norm
        - jnp.mean(grad_norm, axis=-1, keepdims=True)
        - normed * jnp.mean(grad_norm * normed, axis=-1, keepdims=True)
    )
    return (grad_resid, jnp.sum(grad_out * normed, axis=0), jnp.sum(grad_out, axis=0))


def gelu_slope(pre_act):
    return 0.5 * (1.0 + lax.erf(pre_act * math.sqrt(0.5))) + pre_act * jnp.exp(
        -0.5 * pre_act * pre_act
    ) / math.sqrt(2.0 * math.pi)


def slot_scores(queries, key_vecs, live_len):
    inv_root = 1.0 / math.sqrt(HEAD_DIM)
    raw_scores = (
        jnp.einsum("qhd,khd->hqk", queries, key_vecs, preferred_element_type=jnp.float32) * inv_root
    )
    key_valid = jnp.arange(SLOT, dtype=jnp.int32) < live_len
    return jnp.where(key_valid[None, None, :], raw_scores, -1e30)


def slot_forward(parts):
    queries, key_vecs, values, live_len = parts
    masked = slot_scores(queries, key_vecs, live_len)
    row_max = jnp.max(masked, axis=-1, keepdims=True)
    exp_scores = jnp.exp(masked - row_max)
    exp_total = jnp.sum(exp_scores, axis=-1, keepdims=True)
    attn_probs = (exp_scores / exp_total).astype(jnp.bfloat16)
    context = jnp.einsum("hqk,khd->qhd", attn_probs, values, preferred_element_type=jnp.float32)
    return (context.astype(jnp.bfloat16), (row_max + jnp.log(exp_total))[..., 0])


def slot_backward(parts):
    queries, key_vecs, values, live_len, log_total, grad_ctx = parts
    inv_root = 1.0 / math.sqrt(HEAD_DIM)
    masked = slot_scores(queries, key_vecs, live_len)
    attn_exact = jnp.exp(masked - log_total[..., None])
    attn_probs = attn_exact.astype(jnp.bfloat16)
    grad_probs = jnp.einsum("qhd,khd->hqk", grad_ctx, values, preferred_element_type=jnp.float32)
    row_dot = jnp.sum(attn_exact * grad_probs, axis=-1, keepdims=True)
    grad_scores = (attn_exact * (grad_probs - row_dot)).astype(jnp.bfloat16)
    grad_query = (
        jnp.einsum("hqk,khd->qhd", grad_scores, key_vecs, preferred_element_type=jnp.float32)
        * inv_root
    )
    grad_key = (
        jnp.einsum("hqk,qhd->khd", grad_scores, queries, preferred_element_type=jnp.float32)
        * inv_root
    )
    grad_value = jnp.einsum(
        "hqk,qhd->khd", attn_probs, grad_ctx, preferred_element_type=jnp.float32
    )
    return (
        grad_query.astype(jnp.bfloat16),
        grad_key.astype(jnp.bfloat16),
        grad_value.astype(jnp.bfloat16),
    )


def plain_shards(
    inputs,
    timestep,
    context_len,
    out_grad,
    qkv_weight,
    out_weight,
    in_weight,
    back_weight,
    vectors,
    bias_ff,
):
    qkv_full, out_full, in_full, back_full, vec_full, bias_full = (
        lax.all_gather(qkv_weight, ("dp", "seq"), axis=0, tiled=True),
        lax.all_gather(out_weight, ("dp", "seq"), axis=0, tiled=True),
        lax.all_gather(in_weight, ("dp", "seq"), axis=0, tiled=True),
        lax.all_gather(back_weight, ("dp", "seq"), axis=0, tiled=True),
        lax.all_gather(vectors, ("dp", "seq"), axis=0, tiled=True),
        lax.all_gather(bias_ff, ("dp", "seq"), axis=0, tiled=True),
    )
    vec_all = vec_full.astype(jnp.float32)
    bias_all = bias_full.astype(jnp.float32)
    width = inputs.shape[1]
    resid_in = inputs.astype(jnp.float32) + timestep.astype(jnp.float32)
    layer_in = resid_in.astype(jnp.bfloat16)
    qkv_proj = jnp.dot(layer_in, qkv_full, preferred_element_type=jnp.float32)
    queries = (qkv_proj[:, :width] + vec_all[:, 0]).astype(jnp.bfloat16)
    key_vecs = qkv_proj[:, width : 2 * width].astype(jnp.bfloat16)
    values = (qkv_proj[:, 2 * width :] + vec_all[:, 1]).astype(jnp.bfloat16)
    q_heads, k_heads, v_heads = (
        lax.all_to_all(queries, "seq", split_axis=1, concat_axis=0, tiled=True),
        lax.all_to_all(key_vecs, "seq", split_axis=1, concat_axis=0, tiled=True),
        lax.all_to_all(values, "seq", split_axis=1, concat_axis=0, tiled=True),
    )
    slot_count = context_len.shape[1]
    head_width = q_heads.shape[1]
    slot_shape = (slot_count, SLOT, head_width // HEAD_DIM, HEAD_DIM)
    live_lens = context_len[0] + BLOCK
    q_slots = q_heads.reshape(slot_shape)
    k_slots = k_heads.reshape(slot_shape)
    v_slots = v_heads.reshape(slot_shape)
    ctx_slots, log_totals = lax.map(slot_forward, (q_slots, k_slots, v_slots, live_lens))
    ctx_tokens = lax.all_to_all(
        ctx_slots.reshape(slot_count * SLOT, head_width),
        "seq",
        split_axis=0,
        concat_axis=1,
        tiled=True,
    )
    attn_out = jnp.dot(ctx_tokens, out_full, preferred_element_type=jnp.float32) + vec_all[:, 2]
    normed_mid, unit_mid, inv_mid = norm_forward(resid_in + attn_out, vec_all[:, 4], vec_all[:, 5])
    mid_low = normed_mid.astype(jnp.bfloat16)
    pre_act = jnp.dot(mid_low, in_full, preferred_element_type=jnp.float32) + bias_all
    hidden = jax.nn.gelu(pre_act, approximate=False).astype(jnp.bfloat16)
    branch = jnp.dot(hidden, back_full, preferred_element_type=jnp.float32) + vec_all[:, 3]
    result, unit_out, inv_out = norm_forward(normed_mid + branch, vec_all[:, 6], vec_all[:, 7])
    grad_two, gain_out_grad, shift_out_grad = norm_backward(
        out_grad.astype(jnp.float32), unit_out, inv_out, vec_all[:, 6]
    )
    branch_low = grad_two.astype(jnp.bfloat16)
    grad_backw = jnp.einsum("tf,td->fd", hidden, branch_low, preferred_element_type=jnp.float32)
    grad_hidden = jnp.einsum("td,fd->tf", branch_low, back_full, preferred_element_type=jnp.float32)
    grad_pre = grad_hidden * gelu_slope(pre_act)
    bias_grad = jnp.sum(grad_pre, axis=0)
    pre_low = grad_pre.astype(jnp.bfloat16)
    grad_inw = jnp.einsum("td,tf->df", mid_low, pre_low, preferred_element_type=jnp.float32)
    grad_mid = grad_two + jnp.einsum(
        "tf,df->td", pre_low, in_full, preferred_element_type=jnp.float32
    )
    grad_one, gain_mid_grad, shift_mid_grad = norm_backward(
        grad_mid, unit_mid, inv_mid, vec_all[:, 4]
    )
    attn_low = grad_one.astype(jnp.bfloat16)
    grad_outw = jnp.einsum("td,te->de", ctx_tokens, attn_low, preferred_element_type=jnp.float32)
    grad_ctx = jnp.einsum(
        "te,de->td", attn_low, out_full, preferred_element_type=jnp.float32
    ).astype(jnp.bfloat16)
    grad_ctx_heads = lax.all_to_all(grad_ctx, "seq", split_axis=1, concat_axis=0, tiled=True)
    grad_q, grad_k, grad_v = lax.map(
        slot_backward,
        (q_slots, k_slots, v_slots, live_lens, log_totals, grad_ctx_heads.reshape(slot_shape)),
    )
    token_shape = (slot_count * SLOT, head_width)
    grad_q_tok, grad_k_tok, grad_v_tok = (
        lax.all_to_all(grad_q.reshape(token_shape), "seq", split_axis=0, concat_axis=1, tiled=True),
        lax.all_to_all(grad_k.reshape(token_shape), "seq", split_axis=0, concat_axis=1, tiled=True),
        lax.all_to_all(grad_v.reshape(token_shape), "seq", split_axis=0, concat_axis=1, tiled=True),
    )
    grad_proj = jnp.concatenate([grad_q_tok, grad_k_tok, grad_v_tok], axis=1)
    grad_qkvw = jnp.einsum("td,te->de", layer_in, grad_proj, preferred_element_type=jnp.float32)
    grad_input = grad_one + jnp.einsum(
        "te,de->td", grad_proj, qkv_full, preferred_element_type=jnp.float32
    )
    vec_grads = jnp.stack(
        [
            jnp.sum(grad_q_tok.astype(jnp.float32), axis=0),
            jnp.sum(grad_v_tok.astype(jnp.float32), axis=0),
            jnp.sum(grad_one, axis=0),
            jnp.sum(grad_two, axis=0),
            gain_mid_grad,
            shift_mid_grad,
            gain_out_grad,
            shift_out_grad,
        ],
        axis=1,
    )
    share_qkv, share_out, share_in, share_back, share_vec, share_bias = (
        lax.psum_scatter(grad_qkvw, ("dp", "seq"), scatter_dimension=0, tiled=True),
        lax.psum_scatter(grad_outw, ("dp", "seq"), scatter_dimension=0, tiled=True),
        lax.psum_scatter(grad_inw, ("dp", "seq"), scatter_dimension=0, tiled=True),
        lax.psum_scatter(grad_backw, ("dp", "seq"), scatter_dimension=0, tiled=True),
        lax.psum_scatter(vec_grads, ("dp", "seq"), scatter_dimension=0, tiled=True),
        lax.psum_scatter(bias_grad, ("dp", "seq"), scatter_dimension=0, tiled=True),
    )
    return (result, grad_input, share_qkv, share_out, share_in, share_back, share_vec, share_bias)


MESH = pl.DeviceIdType.MESH
LANES = 128
F32 = jnp.float32
BF16 = jnp.bfloat16
NN = (((1,), (0,)), ((), ()))
NT = (((1,), (1,)), ((), ()))
TN = (((0,), (0,)), ((), ()))
ANY = pl.BlockSpec(memory_space=pl.ANY)
IN_VMEM = pl.BlockSpec(memory_space=pltpu.VMEM)
IN_SMEM = pl.BlockSpec(memory_space=pltpu.SMEM)
VMEM_BYTES = 62 << 20


def mm(a, b, dims):
    return lax.dot_general(a, b, dims, preferred_element_type=F32)


class Grid:
    def __init__(self, mesh):
        dp, self.nz = mesh.shape["dp"], mesh.shape["seq"]
        self.nc = 2 if dp % 2 == 0 else 1
        rest = dp // self.nc
        self.nx = max(k for k in range(1, math.isqrt(rest) + 1) if rest % k == 0)
        self.ny = rest // self.nx
        self.count = dp * self.nz
        self.groups = [(y, x, c) for y in range(self.ny) for x in range(self.nx) for c in range(self.nc)]

    def here(self):
        dp = lax.axis_index("dp")
        self.z = lax.axis_index("seq")
        self.c = dp % self.nc
        self.x = (dp // self.nc) % self.nx
        self.y = dp // (self.nc * self.nx)
        self.offs = {
            (axis, step): (getattr(self, axis) + step) % getattr(self, "n" + axis)
            for axis in "zxyc"
            for step in range(1, getattr(self, "n" + axis))
        }
        self.inner = jnp.logical_or(self.z == 1, self.z == 2)
        self.outer = jnp.logical_not(self.inner)
        self.side = self.z % 2
        self.mate = self.z + 1 - 2 * self.side
        self.across = 2 - self.z // 2
        self.other_pair = 2 * self.across - 2
        self.devices = {}
        for axis, step in self.offs:
            at = {name: getattr(self, name) for name in "yxcz"}
            at[axis] = self.offs[axis, step]
            self.devices[axis, step] = ((at["y"] * self.nx + at["x"]) * self.nc + at["c"], at["z"])
        self.dp = (self.y * self.nx + self.x) * self.nc + self.c

    def off(self, axis, step):
        return self.offs[axis, step]

    def at_z(self, z):
        return (self.dp, z)

    def peer(self, axis, step):
        return self.devices[axis, step]

    def peers(self):
        return [self.peer(axis, step) for axis in "zxyc" for step in range(1, getattr(self, "n" + axis))]

    def copies(self):
        return 8 + 2 * (self.nx - 1) + 2 * (self.ny - 1) + self.nc - 1

    def sums(self):
        return self.nz - 1 + 2 * (self.nx - 1) + 2 * (self.ny - 1) + self.nc - 1


def greet(grid):
    barrier = pltpu.get_barrier_semaphore()
    peers = grid.peers()
    for peer in peers:
        pl.semaphore_signal(barrier, inc=1, device_id=peer, device_id_type=MESH)
    pl.semaphore_wait(barrier, len(peers))


def guarded(condition, act):
    if condition is None:
        act()
    else:
        pl.when(condition)(act)


class Leg:
    def __init__(self, sems, ends, sends=None, gets=None, slot=None, slots=1):
        self.sems, self.ends, self.sends, self.gets, self.slot, self.slots = sems, ends, sends, gets, slot, slots
        self.base = sems.used
        sems.used += slots

    def copy(self, slot):
        src, dst, device = self.ends()
        return pltpu.make_async_remote_copy(
            src_ref=src,
            dst_ref=dst,
            send_sem=self.sems.send.at[self.base],
            recv_sem=self.sems.recv.at[self.base + slot],
            device_id=device,
            device_id_type=MESH,
        )

    def start(self):
        guarded(self.sends, lambda: self.copy(0 if self.slot is None else self.slot).start())

    def wait_send(self):
        guarded(self.sends, lambda: self.copy(0).wait_send())

    def wait_recv(self):
        def every():
            for slot in range(self.slots):
                self.copy(slot).wait_recv()

        guarded(self.gets, every)


class Sems:
    def __init__(self, send, recv):
        self.send, self.recv, self.used = send, recv, 0


class Locals:
    def __init__(self, sems):
        self.sems, self.used, self.open = sems, 0, []

    def start(self, ends):
        k = self.used
        self.used += 1

        def copy():
            src, dst = ends()
            return pltpu.make_async_copy(src, dst, self.sems.at[k])

        copy().start()
        self.open.append(copy)
        return copy

    def wait(self, copy):
        copy().wait()
        self.open.remove(copy)

    def drain(self):
        for copy in self.open:
            copy().wait()
        self.open = []


def block_rows(start, size):
    return pl.ds(pl.multiple_of(start * size, size), size)


class Gather:
    STEPS = 6

    def __init__(self, grid, sems, moves, shard, full, cols, keep=None, late_z=False):
        self.grid, self.sems, self.moves = grid, sems, moves
        self.shard, self.full, self.cols, self.keep, self.late_z = shard, full, cols, keep, late_z
        self.half = shard.shape[0] // 2
        self.sent = []

    def place(self, half=None, y=None, x=None, z=None):
        g = self.grid
        take = lambda at, size: pl.ds(0, size) if at is None else at
        rows = pl.ds(0, 2 * self.half) if half is None else pl.ds(half * self.half, self.half)
        return self.full.at[take(y, g.ny), take(x, g.nx), g.c, take(z, g.nz), rows, self.cols]

    def to(self, axis, part):
        g = self.grid
        return [
            Leg(self.sems, lambda k=k: (part(), part(), g.peer(axis, k))) for k in range(1, getattr(g, "n" + axis))
        ]

    def first_z(self, part):
        g = self.grid
        return [
            Leg(self.sems, lambda: (part(g.z), part(g.z), g.at_z(g.mate))),
            Leg(self.sems, lambda: (part(g.z), part(g.z), g.at_z(g.across)), gets=g.inner, slot=g.side, slots=2),
        ]

    def last_z(self, part):
        g = self.grid
        pair = pl.ds(g.other_pair, 2)
        return [
            Leg(self.sems, lambda: (part(pair), part(pair), g.at_z(g.mate)), sends=g.inner, gets=g.outer)
        ]

    def legs(self, step):
        g = self.grid
        if step == 4:
            return self.to("c", self.place)
        if step == 3:
            return self.to("y", lambda: self.place(0, y=g.y)) + self.to("x", lambda: self.place(1, x=g.x))
        if not self.late_z:
            if step == 2:
                return self.to("x", lambda: self.place(0, g.y, g.x)) + self.to("y", lambda: self.place(1, g.y, g.x))
            along = (self.first_z, self.last_z)[step]
            return along(lambda z: self.place(y=g.y, x=g.x, z=z))
        if step == 0:
            return self.to("x", lambda: self.place(0, g.y, g.x, g.z)) + self.to(
                "y", lambda: self.place(1, g.y, g.x, g.z)
            )
        along = (self.first_z, self.last_z)[step - 1]
        return along(lambda z: self.place(0, y=g.y, z=z)) + along(lambda z: self.place(1, x=g.x, z=z))

    def load(self):
        g = self.grid
        self.own = self.moves.start(
            lambda: (self.shard.at[:, self.cols], self.place(y=g.y, x=g.x, z=g.z))
        )

    def step(self, step):
        if step == 0:
            self.moves.wait(self.own)
        else:
            for leg in self.flying:
                leg.wait_recv()
        if step < self.STEPS - 1:
            self.flying = self.legs(step)
            self.sent += self.flying
            for leg in self.flying:
                leg.start()
        elif self.keep is not None:
            every = lambda ref: ref.at[:, :, :, :, :, self.cols]
            self.moves.start(lambda: (every(self.full), every(self.keep)))

    def drain(self):
        for leg in self.sent:
            leg.wait_send()


class Flow:
    def __init__(self, jobs, plan):
        self.jobs, self.plan, self.pumps = jobs, plan, 0
        self.steps = [0] * len(jobs)

    def pump(self, job=None):
        for k in self.plan[self.pumps]:
            self.jobs[k].step(self.steps[k])
            self.steps[k] += 1
        self.pumps += 1
        if job is not None:
            assert self.steps[self.jobs.index(job)] == job.STEPS

    def drain(self):
        assert self.pumps == len(self.plan)
        for job in self.jobs:
            job.drain()


def head_lanes(h):
    return lax.broadcasted_iota(jnp.int32, (1, 2 * HEAD_DIM), 1) // HEAD_DIM == h


def only(lanes, block):
    return jnp.where(lanes, block, 0).astype(BF16)


def fold_small(z, vectors, bias_ff):
    rows = vectors.shape[0]
    lanes = lax.broadcasted_iota(jnp.int32, (rows, LANES), 1)
    mine = lanes == z * rows + lax.broadcasted_iota(jnp.int32, (rows, LANES), 0)
    turned = mm(vectors, jnp.where(mine, 1.0, 0.0).astype(BF16), TN)
    return jnp.concatenate([turned, bias_ff.astype(F32), jnp.zeros((7, LANES), F32)], axis=0).astype(BF16)


FWD_WIDTH = 512


LOG_LANES = 4


def forward_kernel(
    grid,
    ctx_len,
    x_in,
    temb,
    vectors,
    biases,
    wq_in,
    wo_in,
    wi_in,
    wb_in,
    wq_out,
    wo_out,
    wi_out,
    wb_out,
    vec_out,
    hin_out,
    qkv_out,
    logs_out,
    ctx_out,
    n1_out,
    ub_out,
    hid_out,
    slope_out,
    r2_out,
    send,
    recv,
    move_sems,
    x,
    hin,
    qkv,
    ctx,
    n1,
    ub,
    hid,
    slope,
    r2,
    lse,
    logs_parts,
    vec,
    bias_qkv,
    bias_ff,
    small_full,
    small,
    wq,
    wo,
    wi,
    wb,
):
    tokens, width = hin.shape
    hidden = hid.shape[1]
    slots = tokens // SLOT
    tile = FWD_WIDTH
    grid.here()
    moves = Locals(move_sems)
    x_copy = moves.start(lambda: (x_in, x))
    greet(grid)
    sems = Sems(send, recv)

    def gather(shard, full, at, wide, keep, late_z=False):
        return Gather(grid, sems, moves, shard, full, pl.ds(at, wide), keep, late_z)

    small_job = gather(small, small_full, 0, LANES, None)
    half = width // 2
    qkv_cols = [part * width + side * half for side in range(2) for part in range(3)]
    qkv_jobs = [gather(wq_in, wq, at, half, wq_out) for at in qkv_cols]
    out_jobs = [gather(wo_in, wo, at, half, wo_out) for at in range(0, width, half)]
    in_jobs = [gather(wi_in, wi, at, width, wi_out) for at in range(0, hidden, width)]
    back_wide = width * width // hidden
    back_jobs = [gather(wb_in, wb, at, back_wide, wb_out) for at in range(0, width, back_wide)]
    for k in FWD_LATE_Z:
        ([*qkv_jobs, *out_jobs, *in_jobs, *back_jobs][k]).late_z = True
    small[:16, :] = fold_small(grid.z, vectors[...], biases[...])
    small[16:, :] = jnp.zeros((16, LANES), BF16)
    for job in [small_job, *qkv_jobs, *out_jobs, *in_jobs, *back_jobs]:
        job.load()
    flow = Flow([small_job, *qkv_jobs, *out_jobs, *in_jobs, *back_jobs], FWD_PLAN)
    flow.pump()

    moves.wait(x_copy)

    @pl.loop(0, tokens // 128)
    def _(i):
        at = block_rows(i, 128)
        hin[at, :] = (x[at, :].astype(F32) + temb[...].astype(F32)).astype(BF16)

    moves.start(lambda: (hin, hin_out))
    flow.pump(small_job)
    for i, (y, xx, c) in enumerate(grid.groups):
        tiles = [small_full[y, xx, c, z, pl.ds(0, 16), :].astype(F32) for z in range(grid.nz)]
        vec[:, i * LANES : (i + 1) * LANES] = sum(t[:8] for t in tiles)
        for z, t in enumerate(tiles):
            at = (i * grid.nz + z) * LANES
            bias_ff[:, at : at + LANES] = t[8:9]
    moves.start(lambda: (vec, vec_out))
    bias_qkv[:, :width] = vec[0:1, :]
    bias_qkv[:, width : 2 * width] = jnp.zeros((1, width), F32)
    bias_qkv[:, 2 * width :] = vec[1:2, :]

    def project(at):
        @pl.loop(0, tokens // tile)
        def _(i):
            rows = block_rows(i, tile)
            w = wq[:, :, :, :, :, pl.ds(at, half)].reshape(width, half)
            qkv[rows, pl.ds(at, half)] = (mm(hin[rows, :], w, NN) + bias_qkv[:, at : at + half]).astype(BF16)

    def flow_at(i, steps):
        for n in range(steps):

            @pl.when(i == n)
            def _():
                flow.pump()

    first = grid.z * slots
    pairs = width // (2 * HEAD_DIM)
    lane = lax.broadcasted_iota(jnp.int32, (1, LANES), 1)
    key_at = lax.broadcasted_iota(jnp.int32, (1, SLOT), 1)

    def attend(side):
        steps = slots * pairs // 2

        @pl.loop(0, steps)
        def _(i):
            s = i // (pairs // 2)
            p = i % (pairs // 2) + side * (pairs // 2)
            rows = block_rows(s, SLOT)
            off = jnp.where(key_at < ctx_len[0, first + s] + BLOCK, 0.0, -1e30)
            at = pl.multiple_of(p * LANES, LANES)
            q2 = qkv[rows, pl.ds(at, LANES)]
            k2 = qkv[rows, pl.ds(at + width, LANES)]
            v2 = qkv[rows, pl.ds(at + 2 * width, LANES)]
            total = None
            logs = lse[rows, :]
            for h in range(2):
                mine = head_lanes(h)
                score = mm(only(mine, q2) * jnp.asarray(1.0 / math.sqrt(HEAD_DIM), BF16), k2, NT) + off
                high = jnp.max(score, axis=1, keepdims=True)
                e = jnp.exp(score - high)
                norm = jnp.sum(e, axis=1, keepdims=True)
                part = mm(e.astype(BF16), only(mine, v2), NN) * (1.0 / norm)
                total = part if total is None else total + part
                logs = jnp.where(lane // LOG_LANES == 2 * p + h, high + jnp.log(norm), logs)
            lse[rows, :] = logs
            ctx[rows, pl.ds(at, LANES)] = total.astype(BF16)
            flow_at(i, steps)

    lse[...] = jnp.zeros(lse.shape, F32)
    for side in range(2):
        for part in range(3):
            job = side * 3 + part
            flow.pump(qkv_jobs[job])
            project(qkv_cols[job])
        attend(side)
    moves.start(lambda: (qkv, qkv_out))
    moves.start(lambda: (ctx, ctx_out))

    @pl.loop(0, tokens // 128)
    def _(i):
        rows = block_rows(i, 128)
        rest, parts = lse[rows, :], []
        for _ in range(LOG_LANES - 1):
            parts.append(rest.astype(BF16).astype(F32))
            rest = rest - parts[-1]
        value = jnp.ones((128, LANES), F32)
        for n, part in enumerate(parts):
            value = jnp.where(lane % LOG_LANES == n + 1, part, value)
        logs_parts[rows, :] = value.astype(BF16)

    moves.start(lambda: (logs_parts, logs_out))
    for job in out_jobs:
        flow.pump(job)

    @pl.loop(0, tokens // 256)
    def _(i):
        rows = block_rows(i, 256)
        attn = mm(ctx[rows, :], wo[...].reshape(width, width), NN) + vec[2:3, :]
        resid = x[rows, :].astype(F32) + temb[...].astype(F32) + attn
        centered = resid - jnp.mean(resid, axis=1, keepdims=True)
        spread = lax.rsqrt(jnp.mean(centered * centered, axis=1, keepdims=True) + norm_eps)
        unit = centered * spread
        n1[rows, :width] = unit
        n1[rows, width:] = jnp.broadcast_to(spread, (256, LANES))
        ub[rows, :] = (unit * vec[4:5, :] + vec[5:6, :]).astype(BF16)
        flow_at(i, tokens // 256)

    moves.start(lambda: (n1, n1_out))
    moves.start(lambda: (ub, ub_out))
    kept = [None, None]
    for j, at in enumerate(range(0, hidden, tile)):
        if at % width == 0:
            flow.pump(in_jobs[at // width])
        if kept[j % 2] is not None:
            moves.wait(kept[j % 2])

        @pl.loop(0, tokens // tile)
        def _(i):
            rows = block_rows(i, tile)
            w = wi[:, :, :, :, :, pl.ds(at, tile)].reshape(width, tile)
            z = mm(ub[rows, :], w, NN) + bias_ff[:, at : at + tile]
            gate = 0.5 * (1.0 + lax.erf(z * math.sqrt(0.5)))
            hid[rows, pl.ds(at, tile)] = (z * gate).astype(BF16)
            bell = jnp.exp(-0.5 * z * z) * (1.0 / math.sqrt(2.0 * math.pi))
            slope[j % 2, rows, :] = (gate + z * bell).astype(BF16)

        kept[j % 2] = moves.start(lambda j=j, at=at: (slope.at[j % 2], slope_out.at[:, pl.ds(at, tile)]))
        flow.pump()
    moves.start(lambda: (hid, hid_out))
    kept = [None, None]
    for j, job in enumerate(back_jobs):
        flow.pump(job)
        if kept[j % 2] is not None:
            moves.wait(kept[j % 2])
        cols = slice(j * back_wide, (j + 1) * back_wide)

        @pl.loop(0, tokens // tile)
        def _(i):
            rows = block_rows(i, tile)
            w = wb[:, :, :, :, :, pl.ds(j * back_wide, back_wide)].reshape(hidden, back_wide)
            f = mm(hid[rows, :], w, NN) + vec[3:4, cols]
            r2[j % 2, rows, :] = n1[rows, cols] * vec[4:5, cols] + vec[5:6, cols] + f

        kept[j % 2] = moves.start(
            lambda j=j: (r2.at[j % 2], r2_out.at[:, pl.ds(j * back_wide, back_wide)])
        )
    flow.drain()
    moves.drain()


FWD_LATE_Z = (2, 5, 6, 8, 11, 12, 13, 14, 15)
FWD_PLAN = (
    (0, 1, 2, 3, 4, 5,),
    (0, 3, 1, 0, 2, 4, 0, 6, 5, 1, 0, 6, 2, 0,),
    (1, 7, 3, 4, 5, 2, 8, 6, 1, 7, 3, 9, 8, 4, 10, 1,),
    (5, 11, 6, 12, 7, 2, 8, 2,),
    (3, 9, 10, 11, 3,),
    (4, 7, 13,),
    (),
    (4, 5,),
    (9,),
    (5, 6, 10, 12,),
    (8, 14,),
    (6, 11,),
    (7,),
    (),
    (),
    (),
    (7, 9, 15, 10, 16, 13,),
    (8, 12, 14,),
    (),
    (8, 11,),
    (),
    (),
    (),
    (13,),
    (),
    (),
    (9, 12, 15,),
    (),
    (9, 14,),
    (),
    (),
    (10, 16,),
    (10, 13,),
    (),
    (11, 15,),
    (11,),
    (),
    (12, 14,),
    (12, 16,),
    (),
    (13,),
    (15, 13,),
    (),
    (14, 16, 14,),
    (15, 15,),
    (16, 16,),
)


def forward(grid, context_len, inputs, timestep, vectors, bias_ff, qkv_weight, out_weight, in_weight, back_weight):
    tokens, width = inputs.shape
    hidden = in_weight.shape[1]
    weights = (qkv_weight, out_weight, in_weight, back_weight)
    back_wide = width * width // hidden

    def whole(shard):
        return (grid.ny, grid.nx, grid.nc, grid.nz, *shard.shape)

    out = [
        *[(whole(w), BF16) for w in weights],
        ((8, width), F32),
        ((tokens, width), BF16),
        ((tokens, 3 * width), BF16),
        ((tokens, LANES), BF16),
        ((tokens, width), BF16),
        ((tokens, width + LANES), F32),
        ((tokens, width), BF16),
        ((tokens, hidden), BF16),
        ((tokens, hidden), BF16),
        ((tokens, width), F32),
    ]
    jobs = 1 + 6 + 2 + hidden // width + width // back_wide
    scratch = [
        pltpu.SemaphoreType.DMA((jobs * grid.copies(),)),
        pltpu.SemaphoreType.DMA((jobs * grid.copies(),)),
        pltpu.SemaphoreType.DMA((64,)),
        pltpu.VMEM((tokens, width), BF16),
        pltpu.VMEM((tokens, width), BF16),
        pltpu.VMEM((tokens, 3 * width), BF16),
        pltpu.VMEM((tokens, width), BF16),
        pltpu.VMEM((tokens, width + LANES), F32),
        pltpu.VMEM((tokens, width), BF16),
        pltpu.VMEM((tokens, hidden), BF16),
        pltpu.VMEM((2, tokens, FWD_WIDTH), BF16),
        pltpu.VMEM((2, tokens, back_wide), F32),
        pltpu.VMEM((tokens, LANES), F32),
        pltpu.VMEM((tokens, LANES), BF16),
        pltpu.VMEM((8, width), F32),
        pltpu.VMEM((1, 3 * width), F32),
        pltpu.VMEM((1, hidden), F32),
        pltpu.VMEM((grid.ny, grid.nx, grid.nc, grid.nz, 32, LANES), BF16),
        pltpu.VMEM((32, LANES), BF16),
        *[pltpu.VMEM(whole(w), BF16) for w in weights],
    ]
    return pl.pallas_call(
        functools.partial(forward_kernel, grid),
        out_shape=[jax.ShapeDtypeStruct(*o) for o in out],
        in_specs=[IN_SMEM, ANY, *[IN_VMEM] * 3, *[ANY] * 4],
        out_specs=[ANY] * len(out),
        scratch_shapes=scratch,
        compiler_params=pltpu.CompilerParams(
            collective_id=1, has_side_effects=True, vmem_limit_bytes=VMEM_BYTES
        ),
        name="forward_pass",
    )(context_len, inputs, timestep, vectors, bias_ff.reshape(1, LANES), *weights)


def second_norm_kernel(r2, dy, vec, result, dr2, df, sums):
    resid = r2[...]
    centered = resid - jnp.mean(resid, axis=1, keepdims=True)
    spread = lax.rsqrt(jnp.mean(centered * centered, axis=1, keepdims=True) + norm_eps)
    unit = centered * spread
    result[...] = unit * vec[6:7, :] + vec[7:8, :]
    grad = dy[...].astype(F32)
    e = grad * vec[6:7, :]
    back = spread * (
        e - jnp.mean(e, axis=1, keepdims=True) - unit * jnp.mean(e * unit, axis=1, keepdims=True)
    )
    dr2[...] = back
    df[...] = back.astype(BF16)

    @pl.when(pl.program_id(0) == 0)
    def _():
        sums[...] = jnp.zeros(sums.shape, F32)

    sums[3:4, :] += jnp.sum(back, axis=0, keepdims=True)
    sums[6:7, :] += jnp.sum(grad * unit, axis=0, keepdims=True)
    sums[7:8, :] += jnp.sum(grad, axis=0, keepdims=True)


def second_norm(r2, out_grad, vec):
    tokens, width = r2.shape
    tile = 256
    rows = pl.BlockSpec((tile, width), lambda i: (i, 0))
    top = pl.BlockSpec((8, width), lambda i: (0, 0))
    return pl.pallas_call(
        second_norm_kernel,
        grid=(tokens // tile,),
        out_shape=[
            jax.ShapeDtypeStruct((tokens, width), F32),
            jax.ShapeDtypeStruct((tokens, width), F32),
            jax.ShapeDtypeStruct((tokens, width), BF16),
            jax.ShapeDtypeStruct((8, width), F32),
        ],
        in_specs=[rows, rows, top],
        out_specs=[rows, rows, rows, top],
        compiler_params=pltpu.CompilerParams(vmem_limit_bytes=VMEM_BYTES),
        name="second_norm",
    )(r2, out_grad, vec)


class Reduce:
    def __init__(self, grid, sems, base, bufs, other, product, write):
        self.grid, self.sems, self.base = grid, sems, base
        self.other, self.product, self.write = other, product, write
        self.sum, self.in2a, self.in2b, self.in3a, self.in3b, self.in4 = bufs
        self.half = self.sum.shape[2] // 2
        self.rows = self.sum.shape[2] // grid.nz

    def copies(self, stage):
        g = self.grid
        lo, hi = pl.ds(0, self.half), pl.ds(self.half, self.half)
        ys, xs, zs = range(1, g.ny), range(1, g.nx), range(1, g.nz)
        if stage == 1:
            ends = [(self.other, self.sum, g.peer("c", 1))]
        elif stage == 2:
            ends = [(self.sum.at[g.off("y", k), :, lo], self.in2a.at[k - 1], g.peer("y", k)) for k in ys]
            ends += [(self.sum.at[:, g.off("x", k), hi], self.in2b.at[k - 1], g.peer("x", k)) for k in xs]
        elif stage == 3:
            ends = [(self.sum.at[g.y, g.off("x", k), lo], self.in3a.at[k - 1], g.peer("x", k)) for k in xs]
            ends += [(self.sum.at[g.off("y", k), g.x, hi], self.in3b.at[k - 1], g.peer("y", k)) for k in ys]
        else:
            mine = lambda k: self.sum.at[g.y, g.x, block_rows(g.off("z", k), self.rows)]
            ends = [(mine(k), self.in4.at[k - 1], g.peer("z", k)) for k in zs]
        plane = len(ys) + len(xs)
        base = self.base + (0, 0, 1, 1 + plane, 1 + 2 * plane)[stage]
        return [self.sems(base + i, *e) for i, e in enumerate(ends)]

    def send(self, stage):
        for copy in self.copies(stage):
            copy.start()

    def landed(self, stage):
        for copy in self.copies(stage):
            copy.wait_recv()

    def start(self):
        def store(y, x, cols, value):
            self.other[y, x, :, cols] = value.astype(BF16)

        self.product(self.grid.off("c", 1), store)
        self.send(1)

    def second(self):
        self.landed(1)

        def add(y, x, cols, value):
            self.sum[y, x, :, cols] = (self.sum[y, x, :, cols].astype(F32) + value).astype(BF16)

        self.product(self.grid.c, add)
        self.send(2)

    def third(self):
        g = self.grid
        self.landed(2)
        lo, hi = pl.ds(0, self.half), pl.ds(self.half, self.half)
        for x in range(g.nx):
            add_into(self.sum.at[g.y, x, lo], [self.in2a.at[k, x] for k in range(g.ny - 1)])
        for y in range(g.ny):
            add_into(self.sum.at[y, g.x, hi], [self.in2b.at[k, y] for k in range(g.nx - 1)])
        self.send(3)

    def fourth(self):
        g = self.grid
        self.landed(3)
        lo, hi = pl.ds(0, self.half), pl.ds(self.half, self.half)
        add_into(self.sum.at[g.y, g.x, lo], [self.in3a.at[k] for k in range(g.nx - 1)])
        add_into(self.sum.at[g.y, g.x, hi], [self.in3b.at[k] for k in range(g.ny - 1)])
        self.send(4)

    def finish(self):
        g = self.grid
        self.landed(4)
        total = self.sum[g.y, g.x, block_rows(g.z, self.rows), :].astype(F32)
        for k in range(g.nz - 1):
            total += self.in4[k].astype(F32)
        self.write(total)

    def freed(self):
        for copy in self.copies(1):
            copy.wait_send()

    def drain(self):
        for stage in (2, 3, 4):
            for copy in self.copies(stage):
                copy.wait_send()


def add_into(dst, srcs):
    total = dst[...].astype(F32)
    for src in srcs:
        total += src[...].astype(F32)
    dst[...] = total.astype(dst.dtype)


def reduce_bufs(grid, rows, width, count):
    group, half = rows * grid.nz, rows * grid.nz // 2
    ny, nx = grid.ny, grid.nx
    return [
        pltpu.VMEM((count, *shape, width), BF16)
        for shape in (
            (ny, nx, group),
            (ny - 1, nx, half),
            (nx - 1, ny, half),
            (nx - 1, half),
            (ny - 1, half),
            (grid.nz - 1, rows),
        )
    ]


class Line:
    STAGES = {2: "second", 3: "third", 4: "fourth", 5: "finish"}

    def __init__(self, plan):
        self.jobs, self.plan, self.pumps, self.stage = [], plan, 0, []

    def start(self, job, stage=3):
        self.jobs.append(job)
        self.stage.append(stage)
        job.start()

    def step(self, k):
        getattr(self.jobs[k], self.STAGES[self.stage[k]])()
        self.stage[k] += 1

    def pump(self):
        for k, stage in self.plan[self.pumps] if self.pumps < len(self.plan) else ():
            if self.stage[k] == stage:
                self.step(k)
        self.pumps += 1

    def drain(self):
        for at in range(len(self.jobs) + 4):
            for lag, stage in ((3, 5), (2, 4), (1, 3), (0, 2)):
                k = at - lag
                if 0 <= k < len(self.jobs) and self.stage[k] == stage:
                    self.step(k)
        for job in self.jobs:
            job.drain()


BWD_TILE = 512


def backward_kernel(
    grid,
    ctx_len,
    vec,
    sums_in,
    logs,
    dr2,
    df_in,
    hid_in,
    slope_in,
    ub_in,
    n1_in,
    ctx_in,
    qkv_in,
    hin_in,
    wq_in,
    wo_in,
    wi_in,
    wb_in,
    grad_input,
    grad_qkv,
    grad_out,
    grad_in,
    grad_back,
    grad_small,
    send,
    recv,
    move_sems,
    pool,
    du,
    n1,
    sums,
    bias_sum,
    other_wide,
    other_back,
    other_small,
    *bufs,
):
    tokens, width = du.shape
    hidden = bias_sum.shape[1]
    slots = tokens // SLOT
    blocks = hidden // width
    tile = BWD_TILE
    grid.here()
    moves = Locals(move_sems)
    line = Line(BWD_PLAN)

    def sems(k, src, dst, device):
        return pltpu.make_async_remote_copy(
            src_ref=src,
            dst_ref=dst,
            send_sem=send.at[k],
            recv_sem=recv.at[k],
            device_id=device,
            device_id_type=MESH,
        )

    def write_to(out, at, wide):
        def write(total):
            out[:, at : at + wide] = total

        return write


    def load(src, block):
        return moves.start(lambda: (src(), pool.at[block]))

    def columns(ref, j):
        return lambda: ref.at[:, pl.ds(j * width, width)]

    hid, df, ub = [0, 1, 2, 3], 4, 5
    ff_blocks = [(6, 7, 8), (10, 1, 2)]
    dz_blocks = [9, 3]

    def load_back(j):
        return load(lambda: wb_in.at[pl.ds(j * width, width)], ff_blocks[j % 2][0])

    def load_slope(j):
        return load(columns(slope_in, j), ff_blocks[j % 2][1])

    def load_inner(j):
        return load(columns(wi_in, j), ff_blocks[j % 2][2])

    first_loads = [load(lambda: df_in, df), load_back(0), load_slope(0)]
    hid_loads = [load(columns(hid_in, j), hid[j]) for j in range(blocks)]
    inner_load = load_inner(0)
    du_copy = moves.start(lambda: (dr2, du))
    greet(grid)
    back_loads = {1: load_back(1)}
    ub_load = load(lambda: ub_in, ub)
    norm_rows = n1.shape[1]

    def load_n1(i):
        return moves.start(lambda: (n1_in.at[pl.ds(i * norm_rows, norm_rows)], n1.at[i % 2]))

    n1_loads = [load_n1(0), load_n1(1)]
    sums[...] = sums_in[...]
    bias_sum[...] = jnp.zeros(bias_sum.shape, F32)

    places = [(y, x) for y in range(grid.ny) for x in range(grid.nx)]
    group = width // (len(places) * grid.nc)

    def token_product(lhs, rhs, wide, step):
        def product(c, take):
            for part in [places] if step <= tile else [places[: len(places) // 2], places[len(places) // 2 :]]:
                left = jnp.concatenate(
                    [pool[lhs, :, block_rows((y * grid.nx + x) * grid.nc + c, group)] for y, x in part], axis=1
                )
                for n in range(wide // step):
                    cols = pl.ds(n * step, step)
                    value = mm(left, rhs(cols), TN)
                    for i, (y, x) in enumerate(part):
                        take(y, x, cols, value[i * group : (i + 1) * group])

        return product

    def back_product(k, wide):
        def product(c, take):
            rows = width // grid.nc
            left = jnp.concatenate([pool[hid[i], :, block_rows(c, rows)] for i in range(len(places))], axis=1)
            value = mm(left, pool[df, :, k * wide : (k + 1) * wide], TN)
            for i, (y, x) in enumerate(places):
                take(y, x, slice(None), value[i * rows : (i + 1) * rows])

        return product

    bufs_back, bufs_wide, bufs_two, bufs_one, bufs_small = [bufs[6 * i : 6 * i + 6] for i in range(5)]
    back_wide = width // blocks
    back_jobs = [
        Reduce(
            grid,
            sems,
            k * grid.sums(),
            [b.at[k] for b in bufs_back],
            other_back.at[k % 2],
            back_product(k, back_wide),
            write_to(grad_back, k * back_wide, back_wide),
        )
        for k in range(blocks)
    ]
    wide_jobs = 0

    def wide_job(lhs, rhs, out, at):
        nonlocal wide_jobs
        k = wide_jobs
        wide_jobs += 1
        return Reduce(
            grid,
            sems,
            (blocks + k) * grid.sums(),
            [b.at[k] for b in bufs_wide],
            other_wide.at[k % 2],
            token_product(lhs, lambda cols: pool[rhs, :, cols], width, tile),
            write_to(out, at, width),
        )

    def slope_product(j, n):
        back, slope, _ = ff_blocks[j % 2]
        cols = pl.ds(n * tile, tile)
        at = slice(j * width + n * tile, j * width + (n + 1) * tile)

        @pl.loop(0, tokens // tile, unroll=True)
        def _(t):
            rows = block_rows(t, tile)
            grad = mm(pool[df, rows, :], pool[back, cols, :], NT) * pool[slope, rows, cols].astype(F32)
            bias_sum[:, at] += jnp.sum(grad, axis=0, keepdims=True)
            pool[dz_blocks[j % 2], rows, cols] = grad.astype(BF16)

    def inner_product(j, n):
        inner = ff_blocks[j % 2][2]
        rows = pl.ds(n * tile, tile)

        @pl.loop(0, width // tile, unroll=True)
        def _(t):
            cols = block_rows(t, tile)
            du[rows, cols] += mm(pool[dz_blocks[j % 2], rows, :], pool[inner, cols, :], NT)

    tiles = range(width // tile)
    for copy in first_loads:
        moves.wait(copy)
    for n in tiles:
        slope_product(0, n)
    for copy in hid_loads:
        moves.wait(copy)
    line.start(back_jobs[0])
    line.start(back_jobs[1])
    moves.wait(inner_load)
    moves.wait(du_copy)
    inner_product(0, 0)
    back_jobs[0].second()
    back_jobs[0].freed()
    line.start(back_jobs[2])
    back_jobs[1].second()
    back_jobs[1].freed()
    line.start(back_jobs[3])
    line.pump()
    moves.wait(ub_load)
    in_jobs = [wide_job(ub, dz_blocks[j % 2], grad_in, j * width) for j in range(blocks)]
    line.start(in_jobs[0])
    back_jobs[2].second()
    back_jobs[3].second()
    line.pump()
    ff_loads = {1: [load_slope(1), load_inner(1)]}
    for n in tiles[1:]:
        inner_product(0, n)
        line.pump()
    for j in range(1, blocks):
        if j + 1 < blocks:
            back_loads[j + 1] = load_back(j + 1)
            ff_loads[j + 1] = [load_slope(j + 1), load_inner(j + 1)]
        for copy in [back_loads.pop(j), *ff_loads.pop(j)]:
            moves.wait(copy)
        for n in tiles:
            slope_product(j, n)
            if n == 0:
                in_jobs[j - 1].second()
                line.pump()
        if j >= 2:
            in_jobs[j - 2].freed()
        line.start(in_jobs[j])
        line.pump()
        for n in tiles:
            inner_product(j, n)
            line.pump()

    da, out_weight, ctx, dctx = 4, 6, 7, 2
    q, k, v = 0, 8, 1
    dq, dk, dv = 3, 9, 5
    hin, wq = 4, (6, 7, 10)
    out_load = load(lambda: wo_in, out_weight)
    ctx_load = load(lambda: ctx_in, ctx)
    qkv_loads = [load(columns(qkv_in, i), block) for i, block in enumerate((q, k, v))]
    for n in range(tokens // norm_rows):
        moves.wait(n1_loads.pop(0))

        @pl.loop(0, 1)
        def _(_):
            rows = pl.ds(n * norm_rows, norm_rows)
            held = n1[n % 2]
            unit, grad = held[:, :width], du[rows, :]
            e = grad * vec[4:5, :]
            back = held[:, width : width + 1] * (
                e - jnp.mean(e, axis=1, keepdims=True) - unit * jnp.mean(e * unit, axis=1, keepdims=True)
            )
            sums[4:5, :] += jnp.sum(grad * unit, axis=0, keepdims=True)
            sums[5:6, :] += jnp.sum(grad, axis=0, keepdims=True)
            sums[2:3, :] += jnp.sum(back, axis=0, keepdims=True)
            du[rows, :] = back
            pool[da, rows, :] = back.astype(BF16)

        if (n + 2) * norm_rows < tokens:
            n1_loads.append(load_n1(n + 2))

    in_jobs[-1].second()
    line.pump()
    moves.wait(out_load)
    moves.wait(ctx_load)
    out_job = wide_job(ctx, da, grad_out, 0)
    in_jobs[-2].freed()
    line.start(out_job)

    @pl.loop(0, (tokens // tile) * (width // tile), unroll=2)
    def _(t):
        rows, cols = block_rows(t % (tokens // tile), tile), block_rows(t // (tokens // tile), tile)
        pool[dctx, rows, cols] = mm(pool[da, rows, :], pool[out_weight, cols, :], NT).astype(BF16)

    line.pump()
    out_job.second()
    line.pump()
    hin_load = load(lambda: hin_in, hin)
    wq_loads = [load(columns(wq_in, i), block) for i, block in enumerate(wq)]
    for copy in qkv_loads:
        moves.wait(copy)
    first = grid.z * slots
    pairs = width // (2 * HEAD_DIM)
    key_at = lax.broadcasted_iota(jnp.int32, (SLOT, 1), 0)
    lane = lax.broadcasted_iota(jnp.int32, (1, LANES), 1)
    scale = 1.0 / math.sqrt(HEAD_DIM)

    for job in (back_jobs[-2], back_jobs[-1], in_jobs[-1], out_job):
        job.freed()
    moves.wait(hin_load)

    def pair_job(g, first_pair, count, index):
        wide = count * LANES

        def rhs(_):
            return jnp.concatenate(
                [pool[block, :, pl.ds(first_pair * LANES, wide)] for block in (dq, dk, dv)], axis=1
            )

        def write(total):
            for i in range(3):
                at = i * width + first_pair * LANES
                grad_qkv[:, at : at + wide] = total[:, i * wide : (i + 1) * wide]

        return Reduce(
            grid,
            sems,
            (2 * blocks + 1 + g) * grid.sums(),
            [b.at[index] for b in (bufs_two if count == 2 else bufs_one)],
            other_wide.at[g % 2, :, :, :, pl.ds(0, 3 * wide)],
            token_product(hin, rhs, 3 * wide, 3 * wide),
            write,
        )

    def attend(first_pair, count):
        @pl.loop(0, count * slots)
        def _(i):
            s = i % slots
            p = first_pair + i // slots
            at = block_rows(p, LANES)
            rows = block_rows(s, SLOT)
            off = jnp.where(key_at < ctx_len[0, first + s] + BLOCK, 0.0, -1e30)
            extra = jnp.where(lane % LOG_LANES == 0, off, -1.0).astype(BF16)
            q2, k2, v2, c2 = pool[q, rows, at], pool[k, rows, at], pool[v, rows, at], pool[dctx, rows, at]
            keys = jnp.concatenate([k2, extra], axis=1)
            sum_q = sum_k = sum_v = None
            for h in range(2):
                mine = head_lanes(h)
                qh = only(mine, q2) * jnp.asarray(scale, BF16)
                ch = only(mine, c2)
                log = only(lane // LOG_LANES == 2 * p + h, logs[rows, :])
                prob = jnp.exp(mm(keys, jnp.concatenate([qh, log], axis=1), NT))
                dprob = mm(v2, ch, NT)
                dot = jnp.sum(prob * dprob, axis=0, keepdims=True)
                dscore = (prob * (dprob - dot)).astype(BF16)
                add_v = mm(prob.astype(BF16), ch, NN)
                add_k = mm(dscore, qh, NN)
                add_q = mm(dscore, only(mine, k2), TN)
                sum_q = add_q if sum_q is None else sum_q + add_q
                sum_k = add_k if sum_k is None else sum_k + add_k
                sum_v = add_v if sum_v is None else sum_v + add_v
            pool[dq, rows, at] = (sum_q * scale).astype(BF16)
            pool[dk, rows, at] = sum_k.astype(BF16)
            pool[dv, rows, at] = sum_v.astype(BF16)

            for n in range(count * slots):

                @pl.when(i == n)
                def _():
                    line.pump()

        cols = pl.ds(first_pair * LANES, count * LANES)
        for row, block in enumerate((dq, dv)):
            sums[row : row + 1, cols] = jnp.sum(pool[block, :, cols].astype(F32), axis=0, keepdims=True)

    pair_jobs = []
    for g, count in enumerate(PAIR_GROUPS):
        first_pair = sum(PAIR_GROUPS[:g])
        attend(first_pair, count)
        if g >= 2:
            pair_jobs[g - 2].freed()
        pair_jobs.append(pair_job(g, first_pair, count, PAIR_GROUPS[:g].count(count)))
        line.start(pair_jobs[g], 2)
        line.pump()

    def small_product(c, take):
        for y, x in places:
            at = (y * grid.nx + x) * grid.nc + c
            eight = sums[:, block_rows(at, LANES)]
            rows = []
            for z in range(grid.nz):
                rows += [eight, bias_sum[:, block_rows(at * grid.nz + z, LANES)], jnp.zeros((7, LANES), F32)]
            take(y, x, slice(None), jnp.concatenate(rows, axis=0))

    small = Reduce(
        grid,
        sems,
        (2 * blocks + 1 + len(PAIR_GROUPS)) * grid.sums(),
        [b.at[0] for b in bufs_small],
        other_small,
        small_product,
        write_to(grad_small, 0, LANES),
    )
    line.start(small, 2)
    for copy in wq_loads:
        moves.wait(copy)
    for n in range(tokens // tile):
        rows = pl.ds(n * tile, tile)
        for m in range(width // tile):
            cols = pl.ds(m * tile, tile)
            total = du[rows, cols]
            for block, weight in zip((dq, dk, dv), wq):
                total += mm(pool[block, rows, :], pool[weight, cols, :], NT)
            du[rows, cols] = total
            line.pump()

        moves.start(lambda rows=rows: (du.at[rows], grad_input.at[rows]))
    line.pump()
    for job in (*pair_jobs[-2:], small):
        job.freed()
    line.drain()
    moves.drain()


PAIR_GROUPS = (2, 2, 2, 1, 1)
BWD_PLAN = (
    (),
    (),
    ((0, 3),),
    (),
    ((1, 3),),
    (),
    ((2, 3),),
    (),
    ((3, 3), (0, 4),),
    (),
    (),
    ((4, 3),),
    ((1, 4),),
    ((2, 4),),
    (),
    ((0, 5), (3, 4), (5, 3),),
    ((6, 3),),
    ((1, 5), (4, 4),),
    (),
    ((2, 5),),
    ((7, 3),),
    ((3, 5), (5, 4),),
    ((6, 4),),
    (),
    ((4, 5), (8, 3), (9, 2),),
    ((7, 4),),
    (),
    ((8, 4),),
    ((5, 5),),
    ((9, 3), (10, 2), (6, 5),),
    (),
    ((9, 4),),
    ((7, 5),),
    ((10, 3),),
    ((8, 5), (11, 2),),
    (),
    ((10, 4),),
    ((12, 2), (9, 5),),
    (),
    ((10, 5), (11, 3), (12, 3), (13, 2), (14, 2),),
    (),
    ((11, 4), (12, 4),),
    ((13, 3), (14, 3),),
    ((13, 4), (14, 4), (11, 5), (12, 5), (13, 5), (14, 5),),
)


def backward(grid, context_len, vec, sums, logs, dr2, df, hid, slope, ub, n1, ctx, qkv, hin, weights):
    tokens, width = ub.shape
    hidden = hid.shape[1]
    blocks = hidden // width
    count = grid.count
    rows = width // count
    jobs = blocks + blocks + 1 + len(PAIR_GROUPS) + 1
    out = [
        (tokens, width),
        (rows, 3 * width),
        (rows, width),
        (rows, hidden),
        (hidden // count, width),
        (16, LANES),
    ]
    scratch = [
        pltpu.SemaphoreType.DMA((jobs * grid.sums(),)),
        pltpu.SemaphoreType.DMA((jobs * grid.sums(),)),
        pltpu.SemaphoreType.DMA((64,)),
        pltpu.VMEM((11, tokens, width), BF16),
        pltpu.VMEM((tokens, width), F32),
        pltpu.VMEM((2, 64, width + LANES), F32),
        pltpu.VMEM((8, width), F32),
        pltpu.VMEM((1, hidden), F32),
        pltpu.VMEM((2, grid.ny, grid.nx, grid.nz * rows, width), BF16),
        pltpu.VMEM((2, grid.ny, grid.nx, hidden // count * grid.nz, width // blocks), BF16),
        pltpu.VMEM((grid.ny, grid.nx, 16 * grid.nz, LANES), BF16),
        *reduce_bufs(grid, hidden // count, width // blocks, blocks),
        *reduce_bufs(grid, rows, width, blocks + 1),
        *[pair for n in (2, 1) for pair in reduce_bufs(grid, rows, 3 * n * LANES, PAIR_GROUPS.count(n))],
        *reduce_bufs(grid, 16, LANES, 1),
    ]
    return pl.pallas_call(
        functools.partial(backward_kernel, grid),
        out_shape=[jax.ShapeDtypeStruct(o, F32) for o in out],
        in_specs=[IN_SMEM, *[IN_VMEM] * 3, *[ANY] * 13],
        out_specs=[ANY, *[IN_VMEM] * 5],
        scratch_shapes=scratch,
        compiler_params=pltpu.CompilerParams(
            collective_id=2, has_side_effects=True, vmem_limit_bytes=VMEM_BYTES
        ),
        name="backward_pass",
    )(context_len, vec, sums, logs, dr2, df, hid, slope, ub, n1, ctx, qkv, hin, *weights)


def outputs_kernel(*refs):
    n = (len(refs) - 3) // 2
    arrays, small, copies, (vec, bias) = refs[:n], refs[n], refs[n + 1 : 2 * n + 1], refs[2 * n + 1 :]
    for src, dst in zip(arrays, copies):
        dst[...] = src[...]
    z = lax.axis_index("seq")
    rows = vec.shape[0]
    mine = [jnp.where(z == k, small[:8, k * rows : (k + 1) * rows], 0.0) for k in range(LANES // rows)]
    vec[...] = sum(mine).T
    bias[...] = small[8:9, :]


def outputs(arrays, small, rows):
    steps = 4
    like = [jax.ShapeDtypeStruct(a.shape, F32) for a in arrays]
    parts = [pl.BlockSpec((a.shape[0] // steps, a.shape[1]), lambda i: (i, 0)) for a in arrays]
    whole = [pl.BlockSpec(shape, lambda i: (0, 0)) for shape in (small.shape, (rows, 8), (1, LANES))]
    return pl.pallas_call(
        outputs_kernel,
        grid=(steps,),
        out_shape=[*like, jax.ShapeDtypeStruct((rows, 8), F32), jax.ShapeDtypeStruct((1, LANES), F32)],
        in_specs=[*parts, whole[0]],
        out_specs=[*parts, *whole[1:]],
        compiler_params=pltpu.CompilerParams(vmem_limit_bytes=VMEM_BYTES),
        name="outputs",
    )(*arrays, small)


def shards(
    grid, inputs, timestep, context_len, out_grad, qkv_weight, out_weight, in_weight, back_weight, vectors, bias_ff
):
    weights = (qkv_weight, out_weight, in_weight, back_weight)
    if not fits(grid, inputs, vectors, bias_ff, in_weight):
        return plain_shards(inputs, timestep, context_len, out_grad, *weights, vectors, bias_ff)
    *full, vec, hin, qkv, logs, ctx, n1, ub, hid, slope, r2 = forward(
        grid, context_len, inputs, timestep, vectors, bias_ff, *weights
    )
    full = [f.reshape(-1, f.shape[-1]) for f in full]
    result, dr2, df, sums = second_norm(r2, out_grad, vec)
    *grads, grad_small = backward(
        grid, context_len, vec, sums, logs, dr2, df, hid, slope, ub, n1, ctx, qkv, hin, full
    )
    *grads, vec_share, bias_share = outputs(grads, grad_small, vectors.shape[0])
    return (result, *grads, vec_share, bias_share.reshape(-1))


def fits(grid, inputs, vectors, bias_ff, in_weight):
    tokens, width = inputs.shape
    return (
        tokens == width
        and tokens % SLOT == 0
        and vectors.shape[0] * grid.nz == LANES
        and bias_ff.shape[0] == LANES
        and in_weight.shape[1] % width == 0
        and vectors.shape[0] % 32 == 0
        and width // HEAD_DIM * LOG_LANES <= LANES
        and width == sum(PAIR_GROUPS) * LANES
        and grid.nc == 2
        and grid.nx > 1
        and grid.ny > 1
        and grid.nz == 4
        and in_weight.shape[1] == grid.ny * grid.nx * width
    )


def specs():
    rows = P(("dp", "seq"), None)
    return dict(
        in_specs=(rows, P("dp", None), P("dp", None), *[rows] * 6, P(("dp", "seq"))),
        out_specs=(*[rows] * 7, P(("dp", "seq"))),
    )


def solution(mesh):
    return jax.shard_map(functools.partial(shards, Grid(mesh)), mesh=mesh, check_vma=False, **specs())
```
